256 devices in a mesh: dp: 8 (over z_lo, x), expert: 32 (over z_hi, y, core).
Axes of the slice: x: 4, y: 4, z: 8 (z_hi: 4, z_lo: 2; z = z_hi * 2 + z_lo), core: 2. Of those that a mesh axis runs over, the one named last changes fastest.
Arguments:
- tokens: bfloat16 [1024, 196, 768], P(('dp', 'expert')), may hold values from -40 to 40
- router: bfloat16 [768, 64], P(None, 'expert'), may hold values from -0.375 to 0.375
- w_in: bfloat16 [64, 768, 3072], P('expert', None, 'dp'), may hold values from -0.21875 to 0.21875
- w_out: bfloat16 [64, 3072, 768], P('expert', 'dp'), may hold values from -0.109375 to 0.109375
- cotangent: bfloat16 [1024, 196, 768], P(('dp', 'expert')), may hold values from -6 to 6
Outputs:
- mixed: bfloat16 [1024, 196, 768], P(('dp', 'expert'))
- tokens_grad: bfloat16 [1024, 196, 768], P(('dp', 'expert'))
- w_in_grad: float32 [64, 768, 3072], P('expert', None, 'dp')
- w_out_grad: float32 [64, 3072, 768], P('expert', 'dp')
- router_grad: float32 [768, 64], P(None, 'expert')
The draws below stay inside these ranges and needn't reach their ends.
All inputs are finite; a program needn't handle non-finite values.
Results may differ from the reference program's by a relative error of at most 0.025.
Values may be sent and summed in bfloat16 or wider, within the bound.
A program may use at most 128 MiB of HBM per device.

```python
import math
import jax
import jax.numpy as jnp
from jax import lax

D = 768
FF = 3072
M = 196
EXPERTS = 64
IMAGES = 1024


def shared_router(key):
    spread = 2.5 / math.sqrt(D)
    limit = min(4.0, 0.375 / spread)
    return jax.random.truncated_normal(key, -limit, limit, (D, EXPERTS), jnp.float32) * spread


def draw_router(key, part):
    return shared_router(key).astype(jnp.bfloat16)


def draw_tokens(key, part):
    key = jax.random.fold_in(key, 11)
    key_base = jax.random.fold_in(key, 0)
    return jax.random.truncated_normal(key_base, -4.0, 4.0, (IMAGES, M, D), jnp.float32).astype(jnp.bfloat16)


def levels(own_key, shape, cuts, smallest, top_value):
    level = 1.0
    for axis_at, blocks in cuts:
        steps = jax.random.uniform(jax.random.fold_in(jax.random.fold_in(own_key, 6), axis_at), (blocks,), jnp.float32, smallest / len(cuts), top_value / len(cuts))
        level = level * jnp.repeat(jnp.exp(steps), shape[axis_at] // blocks).reshape((-1,) + (1,) * (len(shape) - 1 - axis_at))
    return level


def normal_values(key, extent, scale, bound, shards=(), kind=jnp.bfloat16):
    values = jax.random.normal(key, extent, jnp.float32) * scale
    if len(shards) > 0:
        values = levels(key, extent, shards, -0.22, 0.18) * values
    return jnp.clip(values, min=-bound, max=bound).astype(kind)


def setup_inputs(seed: int = 0) -> dict:
    keys = jax.random.split(jax.random.key(seed), 6)
    tokens = draw_tokens(jax.random.fold_in(keys[5], 71), 0)
    router = draw_router(jax.random.fold_in(keys[5], 71), 0)
    w_in = normal_values(keys[2], (EXPERTS, D, FF), D ** -0.5, 0.21875, ((0, 32), (2, 8)))
    w_out = normal_values(keys[3], (EXPERTS, FF, D), FF ** -0.5, 0.109375, ((0, 32), (1, 8)))
    cotangent = normal_values(keys[4], (IMAGES, M, D), 1.0, 6.0, ((0, 256),))
    return {"tokens": tokens, "router": router, "w_in": w_in, "w_out": w_out, "cotangent": cotangent}


def reference(tokens, router, w_in, w_out, cotangent):
    single = jnp.float32
    tokens_wide = tokens.astype(single)
    router_wide = router.astype(single)
    logits = jnp.einsum('bmd,ds->bms', tokens_wide, router_wide)
    dispatch = jax.nn.softmax(logits, axis=1)
    combine = jax.nn.softmax(logits, axis=2)
    dispatch_low = dispatch.astype(jnp.bfloat16)
    combine_low = combine.astype(jnp.bfloat16)
    slot_in = jnp.einsum('bms,bmd->bsd', dispatch_low.astype(single), tokens_wide).astype(jnp.bfloat16)
    cot_wide = cotangent.astype(single)
    slot_grad = jnp.einsum('bms,bmd->bsd', combine_low.astype(single), cot_wide).astype(jnp.bfloat16)

    def one_expert(index):
        rows = slot_in[:, index, :]
        grads = slot_grad[:, index, :]
        first = w_in[index]
        second = w_out[index]
        pre = jnp.dot(rows, first, preferred_element_type=single)
        act = jax.nn.gelu(pre).astype(jnp.bfloat16)
        out = jnp.dot(act, second, preferred_element_type=single).astype(jnp.bfloat16)
        act_grad = jnp.dot(grads, second.T, preferred_element_type=single)
        _, back = jax.vjp(jax.nn.gelu, pre)
        pre_grad = back(act_grad)[0].astype(jnp.bfloat16)
        second_grad = jnp.dot(act.T, grads, preferred_element_type=single)
        first_grad = jnp.dot(rows.T, pre_grad, preferred_element_type=single)
        input_rows = jnp.dot(pre_grad, first.T, preferred_element_type=single).astype(jnp.bfloat16)
        return (out, input_rows, first_grad, second_grad)
    results = lax.map(one_expert, jnp.arange(EXPERTS, dtype=jnp.int32))
    slot_out = jnp.transpose(results[0], (1, 0, 2))
    input_slots = jnp.transpose(results[1], (1, 0, 2))
    w_in_grad = results[2]
    w_out_grad = results[3]
    mixed = jnp.einsum('bms,bsd->bmd', combine_low.astype(single), slot_out.astype(single)).astype(jnp.bfloat16)
    combine_grad = jnp.einsum('bmd,bsd->bms', cot_wide, slot_out.astype(single))
    input_wide = input_slots.astype(single)
    input_part = jnp.einsum('bms,bsd->bmd', dispatch_low.astype(single), input_wide)
    dispatch_grad = jnp.einsum('bmd,bsd->bms', tokens_wide, input_wide)
    logit_grad = dispatch * (dispatch_grad - lax.optimization_barrier(jnp.sum(dispatch * dispatch_grad, axis=1, keepdims=True)))
    logit_grad = logit_grad + combine * (combine_grad - lax.optimization_barrier(jnp.sum(combine * combine_grad, axis=2, keepdims=True)))
    logit_low = logit_grad.astype(jnp.bfloat16).astype(single)
    tokens_grad = (input_part + jnp.einsum('bms,ds->bmd', logit_low, router_wide)).astype(jnp.bfloat16)
    router_grad = jnp.einsum('bmd,bms->ds', tokens_wide, logit_low)
    return (mixed, tokens_grad, w_in_grad, w_out_grad, router_grad)
```

```python
import functools

import jax
import jax.numpy as jnp
from jax import lax
from jax.experimental import pallas as pl
from jax.experimental.pallas import tpu as pltpu
from jax.sharding import PartitionSpec as P

SINGLE = jnp.float32
LOW = jnp.bfloat16
MESH = pl.DeviceIdType.MESH
RING = 4


def remote(src, dst, send, recv, device):
    copy = pltpu.make_async_remote_copy(
        src_ref=src, dst_ref=dst, send_sem=send, recv_sem=recv, device_id=device, device_id_type=MESH
    )
    copy.start()
    return copy


def await_bytes(ref, sem):
    pltpu.make_async_copy(ref, ref, sem).wait()


def greet(devices):
    barrier = pltpu.get_barrier_semaphore()
    for device in devices:
        pl.semaphore_signal(barrier, inc=1, device_id=device, device_id_type=MESH)
    return barrier


def greet_experts(barrier, dp, ex, experts):
    def one(k, carry):
        pl.semaphore_signal(
            barrier, inc=1, device_id=(dp, lax.rem(ex + k, experts)), device_id_type=MESH
        )
        return carry

    lax.fori_loop(1, experts, one, 0)


def exchange(src, dst, send, recv, dp, ex, experts):
    def one(k, carry):
        to = lax.rem(ex + k, experts)
        pltpu.make_async_remote_copy(
            src_ref=src.at[to],
            dst_ref=dst.at[ex],
            send_sem=send,
            recv_sem=recv,
            device_id=(dp, to),
            device_id_type=MESH,
        ).start()
        return carry

    lax.fori_loop(1, experts, one, 0)


def gather_kernel(experts, own, whole, send, recv):
    dp, ex = lax.axis_index("dp"), lax.axis_index("expert")
    barrier = pltpu.get_barrier_semaphore()
    greet_experts(barrier, dp, ex, experts)
    pl.semaphore_wait(barrier, experts - 1)

    def one(k, carry):
        pltpu.make_async_remote_copy(
            src_ref=own,
            dst_ref=whole.at[ex],
            send_sem=send,
            recv_sem=recv,
            device_id=(dp, lax.rem(ex + k, experts)),
            device_id_type=MESH,
        ).start()
        return carry

    lax.fori_loop(1, experts, one, 0)
    whole[ex] = own[...]
    await_bytes(whole.at[pl.ds(0, experts - 1)], send)
    await_bytes(whole.at[pl.ds(0, experts - 1)], recv)


def gather_router(router, experts):
    d, owned = router.shape
    lanes = 128
    used = d * owned // lanes
    rows = -(-used // 16) * 16
    flat = jnp.pad(router.T.reshape(used, lanes), ((0, rows - used), (0, 0)))
    whole = pl.pallas_call(
        functools.partial(gather_kernel, experts),
        out_shape=jax.ShapeDtypeStruct((experts, rows, lanes), router.dtype),
        in_specs=[pl.BlockSpec(memory_space=pltpu.VMEM)],
        out_specs=pl.BlockSpec(memory_space=pltpu.VMEM),
        scratch_shapes=[pltpu.SemaphoreType.DMA, pltpu.SemaphoreType.DMA],
        compiler_params=pltpu.CompilerParams(collective_id=0, has_side_effects=True),
        name="gather_router",
    )(flat)
    return whole[:, :used].reshape(experts * owned, d)


def reduce_kernel(experts, shards, part, total, first, held, second, sems):
    dp, ex = lax.axis_index("dp"), lax.axis_index("expert")
    barrier = pltpu.get_barrier_semaphore()
    greet_experts(barrier, dp, ex, experts)

    def greet_dp(k, carry):
        pl.semaphore_signal(
            barrier, inc=1, device_id=(lax.rem(dp + k, shards), ex), device_id_type=MESH
        )
        return carry

    lax.fori_loop(1, shards, greet_dp, 0)
    pl.semaphore_wait(barrier, experts + shards - 2)
    exchange(part, first, sems.at[0], sems.at[1], dp, ex, experts)
    first[ex] = part[ex]
    await_bytes(first.at[pl.ds(0, experts - 1)], sems.at[0])
    await_bytes(first.at[pl.ds(0, experts - 1)], sems.at[1])
    held[...] = jnp.sum(first[...], axis=0)

    def one(k, carry):
        pltpu.make_async_remote_copy(
            src_ref=held,
            dst_ref=second.at[dp],
            send_sem=sems.at[2],
            recv_sem=sems.at[3],
            device_id=(lax.rem(dp + k, shards), ex),
            device_id_type=MESH,
        ).start()
        return carry

    lax.fori_loop(1, shards, one, 0)
    second[dp] = held[...]
    await_bytes(second.at[pl.ds(0, shards - 1)], sems.at[2])
    await_bytes(second.at[pl.ds(0, shards - 1)], sems.at[3])
    total[...] = jnp.sum(second[...], axis=0)


def reduce_router(part, experts, shards):
    slots, d = part.shape
    owned = slots // experts
    lanes = owned * d // 6
    blocks = jnp.pad(part.reshape(experts, 6, lanes), ((0, 0), (0, 2), (0, 0)))
    total = pl.pallas_call(
        functools.partial(reduce_kernel, experts, shards),
        out_shape=jax.ShapeDtypeStruct((8, lanes), SINGLE),
        in_specs=[pl.BlockSpec(memory_space=pltpu.VMEM)],
        out_specs=pl.BlockSpec(memory_space=pltpu.VMEM),
        scratch_shapes=[
            pltpu.VMEM((experts, 8, lanes), SINGLE),
            pltpu.VMEM((8, lanes), SINGLE),
            pltpu.VMEM((shards, 8, lanes), SINGLE),
            pltpu.SemaphoreType.DMA((4,)),
        ],
        compiler_params=pltpu.CompilerParams(collective_id=2, has_side_effects=True),
        name="reduce_router",
    )(blocks)
    return total[:6].reshape(owned, d).T


def gelu_and_slope(v):
    c = 0.7978845608028654
    square = v * v
    t = jnp.tanh(c * v * (1.0 + 0.044715 * square))
    half = 0.5 * (1.0 + t)
    slope = half + 0.5 * v * (1.0 - t * t) * (c * (1.0 + 3.0 * 0.044715 * square))
    return v * half, slope


def turn(lhs, rhs):
    return lax.dot_general(lhs, rhs, (((1,), (1,)), ((), ())), preferred_element_type=SINGLE)


def outer(lhs, rhs):
    return lax.dot_general(lhs, rhs, (((0,), (0,)), ((), ())), preferred_element_type=SINGLE)


def dot(lhs, rhs):
    return jnp.dot(lhs, rhs, preferred_element_type=SINGLE)


def expert_kernel(
    experts,
    images,
    msg_in,
    msg_grad,
    w_in,
    w_out,
    back_out,
    back_inp,
    w_in_grad,
    w_out_grad,
    got,
    rows,
    part,
    act,
    slope,
    pre_grad,
    far,
    near,
    over,
    ready,
    a2a_send,
    a2a_recv,
    ag_send,
    ag_recv,
    rs_send,
    far_recv,
    near_recv,
    over_recv,
):
    dp, ex = lax.axis_index("dp"), lax.axis_index("expert")
    x, z = lax.rem(dp, RING), dp // RING
    x_right, x_left = lax.rem(x + 1, RING), lax.rem(x + 3, RING)
    x_far = lax.rem(x + 2, RING)
    other = 1 - z
    partner = (other * RING + x, ex)
    right = (z * RING + x_right, ex)
    left = (z * RING + x_left, ex)
    own = dp
    mate = other * RING + x
    n_rows = experts * images
    half = rows.shape[-1] // 2

    barrier = greet((partner, right, left))
    greet_experts(barrier, dp, ex, experts)
    pl.semaphore_wait(barrier, experts + 2)

    for a, msg in ((0, msg_in), (1, msg_grad)):
        exchange(msg, got.at[a], a2a_send.at[a], a2a_recv.at[a], dp, ex, experts)
        got[a, ex] = msg[ex]

    def place(shape, row_axis):
        row = lax.broadcasted_iota(jnp.int32, shape, row_axis)
        col = lax.broadcasted_iota(jnp.int32, shape, 1 - row_axis)
        slot = (row >= n_rows).astype(jnp.int32)
        row = row - slot * n_rows
        image = lax.bitwise_and(row, images - 1)
        source = lax.shift_right_logical(row, images.bit_length() - 1)
        return col - (source * 4 * images + slot * images + image)

    def mark(distance, which):
        return (distance == which * 2 * images).astype(SINGLE).astype(LOW)

    def unpack(a):
        await_bytes(got.at[a, pl.ds(0, experts - 1)], a2a_recv.at[a])
        flat = got[a].reshape(experts * 4 * images, half)
        distance = place((2 * n_rows, experts * 4 * images), 0)
        for h in range(2):
            block = dot(mark(distance, h), flat).astype(LOW)
            for e in range(2):
                rows[a, e, own, :, h * half : (h + 1) * half] = block[e * n_rows : (e + 1) * n_rows]

    sent = []

    def send_block(a, e, p, to, slot):
        block = rows.at[a, e, p]
        sent.append(remote(block, block, ag_send.at[a, slot], ag_recv.at[a, e, p], to))

    def arrived(a, e, p):
        await_bytes(rows.at[a, e, p], ag_recv.at[a, e, p])

    def gather_own(a):
        for e in range(2):
            send_block(a, e, own, partner, 3 * e)
            send_block(a, e, own, right, 3 * e + 1)
            send_block(a, e, own, left, 3 * e + 2)

    def gather_mate(a):
        for e in range(2):
            arrived(a, e, mate)
            send_block(a, e, mate, right, 6 + 2 * e)
            send_block(a, e, mate, left, 7 + 2 * e)

    def gather_near(a):
        for k, ring in enumerate((z, other)):
            p = ring * RING + x_left
            arrived(a, 0, p)
            send_block(a, 0, p, right, 10 + 2 * k)
            p = ring * RING + x_right
            arrived(a, 1, p)
            send_block(a, 1, p, left, 11 + 2 * k)

    def near_rest(a):
        for ring in (z, other):
            arrived(a, 1, ring * RING + x_left)
            arrived(a, 0, ring * RING + x_right)

    def far_rest(a):
        for ring in (z, other):
            for e in range(2):
                arrived(a, e, ring * RING + x_far)

    def forward(e, p):
        pre = dot(rows[0, e, p], w_in[e])
        value, grade = gelu_and_slope(pre)
        value = value.astype(LOW)
        act[e, p] = value
        slope[e, p] = grade
        part[0, e, p] = dot(value, w_out[e]).astype(LOW)

    def backward(e, p):
        grad = turn(rows[1, e, p], w_out[e])
        grad = (grad * slope[e, p]).astype(LOW)
        pre_grad[e, p] = grad
        part[1, e, p] = turn(grad, w_in[e]).astype(LOW)

    def over_blocks(step, first, count):
        def one(k, carry):
            e, k = lax.rem(k, 2), k // 2
            ring, k = lax.rem(k, 2), k // 2
            step(e, ring * RING + lax.rem(x + first + 2 * k, RING))
            return carry

        lax.fori_loop(0, 4 * count, one, 0)

    def over_experts(step, p):
        def one(e, carry):
            step(e, p)
            return carry

        lax.fori_loop(0, 2, one, 0)

    def reduce_far(a):
        for ring in range(2):
            p = ring * RING + x_far
            for e, to in ((0, right), (1, left)):
                sent.append(
                    remote(
                        part.at[a, e, p],
                        far.at[a, e, ring],
                        rs_send.at[a, 2 * ring + e],
                        far_recv.at[a, e, ring],
                        to,
                    )
                )

    def send_near(a, e, ring, side):
        p = ring * RING + (x_right, x_left)[side]
        sent.append(
            remote(
                part.at[a, e, p],
                near.at[a, side, e, ring],
                rs_send.at[a, 4 + 4 * side + 2 * ring + e],
                near_recv.at[a, side, e, ring],
                (right, left)[side],
            )
        )

    def reduce_near(a):
        for ring in range(2):
            send_near(a, 1, ring, 0)
            send_near(a, 0, ring, 1)
        for ring in range(2):
            for e in range(2):
                p = ring * RING + (x_right, x_left)[e]
                await_bytes(far.at[a, e, ring], far_recv.at[a, e, ring])
                total = part[a, e, p].astype(SINGLE) + far[a, e, ring].astype(SINGLE)
                part[a, e, p] = total.astype(LOW)
                send_near(a, e, ring, e)

    def near_total(a, e, ring):
        for side in range(2):
            await_bytes(near.at[a, side, e, ring], near_recv.at[a, side, e, ring])
        return (
            part[a, e, ring * RING + x].astype(SINGLE)
            + near[a, 0, e, ring].astype(SINGLE)
            + near[a, 1, e, ring].astype(SINGLE)
        )

    def reduce_over(a):
        for e in range(2):
            part[a, e, mate] = near_total(a, e, other).astype(LOW)
            sent.append(
                remote(
                    part.at[a, e, mate],
                    over.at[a, e],
                    rs_send.at[a, 12 + e],
                    over_recv.at[a, e],
                    partner,
                )
            )

    def give_back(a, back):
        halves = ([], [])
        for e in range(2):
            total = near_total(a, e, z)
            await_bytes(over.at[a, e], over_recv.at[a, e])
            total = (total + over[a, e].astype(SINGLE)).astype(LOW)
            for h in range(2):
                halves[h].append(total[:, h * half : (h + 1) * half])
        distance = place((experts * 4 * images, 2 * n_rows), 1)
        block = sum(dot(mark(distance, h), jnp.concatenate(halves[h], axis=0)) for h in range(2))
        ready[a] = block.astype(LOW).reshape(experts, 4 * images, half)
        exchange(ready.at[a], back, a2a_send.at[2 + a], a2a_recv.at[2 + a], dp, ex, experts)
        back[ex] = ready[a, ex]

    unpack(0)
    gather_own(0)
    unpack(1)
    over_experts(forward, own)
    gather_mate(0)
    gather_own(1)
    over_experts(forward, mate)
    gather_near(0)
    gather_mate(1)
    near_rest(0)
    over_blocks(forward, 1, 2)
    far_rest(0)
    over_blocks(forward, 2, 1)
    reduce_far(0)
    gather_near(1)
    over_experts(backward, own)
    over_experts(backward, mate)
    reduce_near(0)
    near_rest(1)
    over_blocks(backward, 1, 2)
    far_rest(1)
    over_blocks(backward, 2, 1)
    reduce_far(1)
    reduce_over(0)
    reduce_near(1)
    give_back(0, back_out)

    def weights(e, carry):
        def flat(value):
            return value.reshape(value.shape[0] * value.shape[1], value.shape[2])

        w_out_grad[e] = outer(flat(act[e]), flat(rows[1, e]))
        w_in_grad[e] = outer(flat(rows[0, e]), flat(pre_grad[e]))
        return carry

    lax.fori_loop(0, 2, weights, 0)
    reduce_over(1)
    give_back(1, back_inp)
    for a, back in ((0, back_out), (1, back_inp)):
        await_bytes(back.at[pl.ds(0, experts - 1)], a2a_recv.at[2 + a])
    for k in range(4):
        await_bytes(got.at[0, pl.ds(0, experts - 1)], a2a_send.at[k])
    for copy in sent:
        copy.wait_send()


def run_experts(slot_in, slot_grad, w_in, w_out, experts):
    images, slots, d = slot_in.shape
    half = d // 2
    hidden = w_in.shape[2]
    n_rows = experts * images

    def messages(value):
        value = value.reshape(images, experts, 2, 2, half)
        return value.transpose(1, 3, 2, 0, 4).reshape(experts, 4 * images, half)

    def slots_of(value):
        value = value.reshape(experts, 2, 2, images, half)
        return value.transpose(3, 0, 2, 1, 4).reshape(images, slots, d)

    vmem = pl.BlockSpec(memory_space=pltpu.VMEM)
    message = jax.ShapeDtypeStruct((experts, 4 * images, half), LOW)
    dma = pltpu.SemaphoreType.DMA
    back_out, back_inp, w_in_grad, w_out_grad = pl.pallas_call(
        functools.partial(expert_kernel, experts, images),
        out_shape=[
            message,
            message,
            jax.ShapeDtypeStruct(w_in.shape, SINGLE),
            jax.ShapeDtypeStruct(w_out.shape, SINGLE),
        ],
        in_specs=[vmem] * 4,
        out_specs=[vmem] * 4,
        scratch_shapes=[
            pltpu.VMEM((2, experts, 4 * images, half), LOW),
            pltpu.VMEM((2, 2, 2 * RING, n_rows, d), LOW),
            pltpu.VMEM((2, 2, 2 * RING, n_rows, d), LOW),
            pltpu.VMEM((2, 2 * RING, n_rows, hidden), LOW),
            pltpu.VMEM((2, 2 * RING, n_rows, hidden), SINGLE),
            pltpu.VMEM((2, 2 * RING, n_rows, hidden), LOW),
            pltpu.VMEM((2, 2, 2, n_rows, d), LOW),
            pltpu.VMEM((2, 2, 2, 2, n_rows, d), LOW),
            pltpu.VMEM((2, 2, n_rows, d), LOW),
            pltpu.VMEM((2, experts, 4 * images, half), LOW),
            dma((4,)),
            dma((4,)),
            dma((2, 14)),
            dma((2, 2, 2 * RING)),
            dma((2, 14)),
            dma((2, 2, 2)),
            dma((2, 2, 2, 2)),
            dma((2, 2)),
        ],
        compiler_params=pltpu.CompilerParams(
            collective_id=1, has_side_effects=True, vmem_limit_bytes=56 * 1024 * 1024
        ),
        name="experts",
    )(messages(slot_in), messages(slot_grad), w_in, w_out)
    return slots_of(back_out), slots_of(back_inp), w_in_grad, w_out_grad


def body(experts, shards, tokens, router, w_in, w_out, cotangent):
    slots = gather_router(router, experts)
    logits = jnp.einsum("bmd,sd->bms", tokens, slots, preferred_element_type=SINGLE)
    dispatch = jax.nn.softmax(logits, axis=1)
    combine = jax.nn.softmax(logits, axis=2)
    dispatch_low = dispatch.astype(LOW)
    combine_low = combine.astype(LOW)
    slot_in = jnp.einsum(
        "bms,bmd->bsd", dispatch_low, tokens, preferred_element_type=SINGLE
    ).astype(LOW)
    slot_grad = jnp.einsum(
        "bms,bmd->bsd", combine_low, cotangent, preferred_element_type=SINGLE
    ).astype(LOW)
    slot_out, input_slots, w_in_grad, w_out_grad = run_experts(
        slot_in, slot_grad, w_in, w_out, experts
    )
    mixed = jnp.einsum("bms,bsd->bmd", combine_low, slot_out, preferred_element_type=SINGLE).astype(
        LOW
    )
    combine_grad = jnp.einsum("bmd,bsd->bms", cotangent, slot_out, preferred_element_type=SINGLE)
    input_part = jnp.einsum(
        "bms,bsd->bmd", dispatch_low, input_slots, preferred_element_type=SINGLE
    )
    dispatch_grad = jnp.einsum("bmd,bsd->bms", tokens, input_slots, preferred_element_type=SINGLE)
    logit_grad = dispatch * (
        dispatch_grad - jnp.sum(dispatch * dispatch_grad, axis=1, keepdims=True)
    )
    logit_grad = logit_grad + combine * (
        combine_grad - jnp.sum(combine * combine_grad, axis=2, keepdims=True)
    )
    logit_low = logit_grad.astype(LOW)
    router_part = jnp.einsum("bmd,bms->sd", tokens, logit_low, preferred_element_type=SINGLE)
    router_grad = reduce_router(router_part, experts, shards)
    tokens_grad = (
        input_part + jnp.einsum("bms,sd->bmd", logit_low, slots, preferred_element_type=SINGLE)
    ).astype(LOW)
    return (mixed, tokens_grad, w_in_grad, w_out_grad, router_grad)


def solution(mesh):
    placed = (
        P(("dp", "expert"), None, None),
        P(None, "expert"),
        P("expert", None, "dp"),
        P("expert", "dp", None),
        P(("dp", "expert"), None, None),
    )
    return jax.shard_map(
        functools.partial(body, mesh.shape["expert"], mesh.shape["dp"]),
        mesh=mesh,
        in_specs=placed,
        out_specs=(
            P(("dp", "expert"), None, None),
            P(("dp", "expert"), None, None),
            P("expert", None, "dp"),
            P("expert", "dp", None),
            P(None, "expert"),
        ),
        check_vma=False,
    )
```

```python
import functools

import jax
import jax.numpy as jnp
from jax import lax
from jax.experimental import pallas as pl
from jax.experimental.pallas import tpu as pltpu
from jax.sharding import PartitionSpec as P

SINGLE = jnp.float32
LOW = jnp.bfloat16
MESH = pl.DeviceIdType.MESH
RING = 4
Z_HIGH = 4
LANES = 128
CHUNK = 16


def remote(src, dst, send, recv, device):
    copy = pltpu.make_async_remote_copy(
        src_ref=src, dst_ref=dst, send_sem=send, recv_sem=recv, device_id=device, device_id_type=MESH
    )
    copy.start()
    return copy


def await_bytes(ref, sem):
    pltpu.make_async_copy(ref, ref, sem).wait()


def gelu_and_slope(v):
    c = 0.7978845608028654
    square = v * v
    t = jnp.tanh(c * v * (1.0 + 0.044715 * square))
    half = 0.5 * (1.0 + t)
    slope = half + 0.5 * v * (1.0 - t * t) * (c * (1.0 + 3.0 * 0.044715 * square))
    return v * half, slope


def turn(lhs, rhs):
    return lax.dot_general(lhs, rhs, (((1,), (1,)), ((), ())), preferred_element_type=SINGLE)


def outer(lhs, rhs):
    return lax.dot_general(lhs, rhs, (((0,), (0,)), ((), ())), preferred_element_type=SINGLE)


def dot(lhs, rhs):
    return jnp.dot(lhs, rhs, preferred_element_type=SINGLE)


def place_of(z_at, lane, x, experts):
    z_at = lax.rem(z_at + 4 * Z_HIGH, 2 * Z_HIGH)
    return (lax.rem(z_at, 2) * RING + x, (z_at // 2) * (experts // Z_HIGH) + lane)


def layer_kernel(
    experts,
    images,
    tokens_hbm,
    cotangent_hbm,
    router_own,
    w_in_hbm,
    w_out_hbm,
    mixed_hbm,
    tokens_grad_hbm,
    w_in_grad_hbm,
    w_out_grad_hbm,
    router_total,
    held,
    w_in,
    w_out,
    router_got,
    router,
    dispatch,
    combine,
    dispatch_low,
    combine_low,
    message,
    got,
    rows,
    part,
    act,
    slope,
    pre_grad,
    cross,
    far,
    near,
    over,
    ready,
    back,
    combine_term,
    w_in_grad,
    w_out_grad,
    result,
    router_message,
    router_first,
    router_mine,
    router_second,
    local,
    a2a_send,
    a2a_recv,
    ag_send,
    ag_recv,
    rs_send,
    cross_recv,
    far_recv,
    near_recv,
    over_recv,
):
    dp, ex = lax.axis_index("dp"), lax.axis_index("expert")
    shards = 2 * RING
    x, z = lax.rem(dp, RING), dp // RING
    x_right, x_left = lax.rem(x + 1, RING), lax.rem(x + 3, RING)
    x_far = lax.rem(x + 2, RING)
    other = 1 - z
    partner = (other * RING + x, ex)
    right = (z * RING + x_right, ex)
    left = (z * RING + x_left, ex)
    own = dp
    mate = other * RING + x
    n_rows = experts * images
    half = rows.shape[-1] // 2
    slots = 2 * experts
    pairs = images * slots
    n_tokens, n_padded = tokens_hbm.shape[0], held.shape[1]
    chunks = rows.shape[-1] // LANES
    inner = experts // Z_HIGH
    lane = lax.rem(ex, inner)
    z_at = (ex // inner) * 2 + z
    way = 1 - 2 * z

    loads = [
        pltpu.make_async_copy(src, dst, local.at[k])
        for k, (src, dst) in enumerate(
            (
                (tokens_hbm, held.at[0, pl.ds(0, n_tokens)]),
                (cotangent_hbm, held.at[1, pl.ds(0, n_tokens)]),
                (w_in_hbm, w_in),
                (w_out_hbm, w_out),
            )
        )
    ]
    for load in loads:
        load.start()

    barrier = pltpu.get_barrier_semaphore()

    def greet_experts(k, carry):
        step = k // inner
        step = step - (step // Z_HIGH) * (Z_HIGH + 2)
        to = place_of(z_at - step * way, lax.rem(lane + k, inner), x, experts)
        pl.semaphore_signal(barrier, inc=1, device_id=to, device_id_type=MESH)
        return carry

    def greet_shards(k, carry):
        to = (lax.rem(dp + k, shards), ex)
        pl.semaphore_signal(barrier, inc=1, device_id=to, device_id_type=MESH)
        return carry

    greeted = (Z_HIGH + 1) * inner
    lax.fori_loop(1, greeted, greet_experts, 0)
    lax.fori_loop(1, shards, greet_shards, 0)
    pl.semaphore_wait(barrier, greeted - 1 + shards - 1)

    def deliver(src, dst, k):
        def one(i, carry):
            step = i // inner
            to = place_of(
                z_at + step * way * (1 - 2 * lax.rem(step, 2)), lax.rem(lane + i, inner), x, experts
            )
            pltpu.make_async_remote_copy(
                src_ref=src.at[to[1]],
                dst_ref=dst.at[step * inner + lane],
                send_sem=a2a_send.at[k],
                recv_sem=a2a_recv.at[k],
                device_id=to,
                device_id_type=MESH,
            ).start()
            return carry

        lax.fori_loop(1, experts, one, 0)
        dst[lane] = src[ex]

    def collect(src_of, dst, k):
        def one(i, carry):
            step = i // inner
            there = lax.rem(lane + i, inner)
            pltpu.make_async_remote_copy(
                src_ref=src_of(step * inner + there),
                dst_ref=dst.at[ex],
                send_sem=a2a_send.at[k],
                recv_sem=a2a_recv.at[k],
                device_id=place_of(z_at - step * way, there, x, experts),
                device_id_type=MESH,
            ).start()
            return carry

        lax.fori_loop(1, experts, one, 0)

    def received(ref, k):
        await_bytes(ref.at[pl.ds(0, experts - 1)], a2a_recv.at[k])

    def iota(shape, axis):
        return lax.broadcasted_iota(jnp.int32, shape, axis)

    def bits(n):
        return n.bit_length() - 1

    def by_expert(row):
        slot = (row >= n_rows).astype(jnp.int32)
        row = row - slot * n_rows
        image = lax.bitwise_and(row, images - 1)
        return lax.shift_right_logical(row, bits(images)) * 4 * images + slot * images + image

    def by_image(row):
        slot = lax.bitwise_and(row, slots - 1)
        image = lax.shift_right_logical(row, bits(slots))
        odd = lax.bitwise_and(slot, 1)
        return lax.shift_right_logical(slot, 1) * 4 * images + odd * images + image

    def by_slot(row):
        odd = lax.bitwise_and(row, 1)
        return lax.shift_right_logical(row, 1) * CHUNK + odd * chunks

    def distance(shape, axis, order):
        return iota(shape, axis) - order(iota(shape, 1 - axis))

    def mark(distances, at):
        return (distances == at).astype(SINGLE).astype(LOW)

    def pack(value, order):
        n = value.shape[0]
        away = distance((experts * 4 * images, n), 0, order)
        block = sum(
            dot(mark(away, h * 2 * images), value[:, h * half : (h + 1) * half]) for h in range(2)
        )
        return block.astype(LOW).reshape(experts, 4 * images, half)

    def unpack(value, order, n):
        flat = value.reshape(experts * 4 * images, half)
        away = distance((n, experts * 4 * images), 1, order)
        return [dot(mark(away, h * 2 * images), flat).astype(LOW) for h in range(2)]

    collect(lambda block: router_own, router_got, 4)
    router_got[ex] = router_own[...]
    for load in loads[:2]:
        load.wait()
    if n_padded > n_tokens:
        for k in range(2):
            held[k, n_tokens:] = jnp.zeros((n_padded - n_tokens, held.shape[2]), LOW)
    received(router_got, 4)
    flat = router_got[...].reshape(experts * CHUNK, LANES)
    away = distance((slots, experts * CHUNK), 1, by_slot)
    for c in range(chunks):
        router[:, c * LANES : (c + 1) * LANES] = dot(mark(away, c), flat).astype(LOW)

    column = iota((slots, n_padded), 1)
    image_of = jnp.where(column < n_tokens, lax.bitwise_and(column, images - 1), -1)

    def per_image(reduce, value, fill):
        spread = jnp.zeros_like(value)
        for i in range(images):
            mine = image_of == i
            total = reduce(jnp.where(mine, value, fill), axis=1, keepdims=True)
            spread = jnp.where(mine, total, spread)
        return spread

    def apart(value, low):
        for i in range(images):
            low[i * slots : (i + 1) * slots] = jnp.where(image_of == i, value, 0.0).astype(LOW)

    def together(value):
        total = jnp.zeros((slots, n_padded), SINGLE)
        for i in range(images):
            total = jnp.where(image_of == i, value[i * slots : (i + 1) * slots], total)
        return total

    logits = turn(router[...], held[0])
    weight = jnp.exp(logits - per_image(jnp.max, logits, -jnp.inf))
    weight = jnp.where(image_of >= 0, weight, 0.0)
    weight = weight / jnp.where(image_of >= 0, per_image(jnp.sum, weight, 0.0), 1.0)
    dispatch[...] = weight
    apart(weight, dispatch_low)
    message[0] = pack(dot(dispatch_low[...], held[0]).astype(LOW), by_image)
    deliver(message.at[0], got.at[0], 0)
    weight = jnp.exp(logits - jnp.max(logits, axis=0, keepdims=True))
    weight = weight / jnp.sum(weight, axis=0, keepdims=True)
    combine[...] = weight
    apart(weight, combine_low)
    message[1] = pack(dot(combine_low[...], held[1]).astype(LOW), by_image)

    def own_rows(a):
        received(got.at[a], a)
        for h, block in enumerate(unpack(got[a], by_expert, 2 * n_rows)):
            for e in range(2):
                rows[a, e, own, :, h * half : (h + 1) * half] = block[e * n_rows : (e + 1) * n_rows]

    sent = []

    def send_block(a, e, p, to, slot):
        block = rows.at[a, e, p]
        sent.append(remote(block, block, ag_send.at[a, slot], ag_recv.at[a, e, p], to))

    def arrived(a, e, p):
        await_bytes(rows.at[a, e, p], ag_recv.at[a, e, p])

    def gather_own(a):
        for e in range(2):
            send_block(a, e, own, partner, 3 * e)
            send_block(a, e, own, right, 3 * e + 1)
            send_block(a, e, own, left, 3 * e + 2)

    def gather_mate(a):
        for e in range(2):
            arrived(a, e, mate)
            send_block(a, e, mate, right, 6 + 2 * e)
            send_block(a, e, mate, left, 7 + 2 * e)

    def gather_far(a):
        for e, p, to in ((0, z * RING + x_left, right), (1, z * RING + x_right, left)):
            arrived(a, e, p)
            send_block(a, e, p, to, 10 + e)

    def gather_cross(a):
        for e in range(2):
            arrived(a, e, z * RING + x_far)
            send_block(a, e, z * RING + x_far, partner, 12 + e)

    def near_rest(a):
        arrived(a, 1, z * RING + x_left)
        arrived(a, 0, z * RING + x_right)

    def near_other(a):
        for e in range(2):
            arrived(a, e, other * RING + x_left)
            arrived(a, e, other * RING + x_right)

    def cross_rest(a):
        for e in range(2):
            arrived(a, e, other * RING + x_far)

    def forward(e, p):
        pre = dot(rows[0, e, p], w_in[e])
        value, grade = gelu_and_slope(pre)
        value = value.astype(LOW)
        act[e, p] = value
        slope[e, p] = grade
        part[0, e, p] = dot(value, w_out[e]).astype(LOW)

    def backward(e, p):
        grad = turn(rows[1, e, p], w_out[e])
        grad = (grad * slope[e, p]).astype(LOW)
        pre_grad[e, p] = grad
        part[1, e, p] = turn(grad, w_in[e]).astype(LOW)

    def over_near(step, ring):
        def one(k, carry):
            step(lax.rem(k, 2), ring * RING + lax.rem(x + 1 + 2 * (k // 2), RING))
            return carry

        lax.fori_loop(0, 4, one, 0)

    def over_experts(step, p):
        def one(e, carry):
            step(e, p)
            return carry

        lax.fori_loop(0, 2, one, 0)

    def send_part(a, e, p, buffer, slot, recv, to):
        sent.append(remote(part.at[a, e, p], buffer, rs_send.at[a, slot], recv, to))

    def add(a, e, p, buffer, recv):
        await_bytes(buffer, recv)
        total = part[a, e, p].astype(SINGLE) + buffer[...].astype(SINGLE)
        part[a, e, p] = total.astype(LOW)

    def reduce_cross(a):
        for e in range(2):
            p = other * RING + x_far
            send_part(a, e, p, cross.at[a, e], e, cross_recv.at[a, e], partner)

    def reduce_far(a):
        for e, to in ((0, right), (1, left)):
            p = z * RING + x_far
            add(a, e, p, cross.at[a, e], cross_recv.at[a, e])
            send_part(a, e, p, far.at[a, e], 2 + e, far_recv.at[a, e], to)

    def send_near(a, e, ring, which, side):
        send_part(
            a,
            e,
            ring * RING + (x_right, x_left)[side],
            near.at[a, side, e, which],
            4 + 4 * side + 2 * which + e,
            near_recv.at[a, side, e, which],
            (right, left)[side],
        )

    def reduce_near_free(a):
        for e in range(2):
            for side in range(2):
                send_near(a, e, other, 1, side)
        for e in range(2):
            send_near(a, e, z, 0, 1 - e)

    def reduce_near(a):
        for e in range(2):
            add(a, e, z * RING + (x_right, x_left)[e], far.at[a, e], far_recv.at[a, e])
            send_near(a, e, z, 0, e)

    def near_total(a, e, ring, which):
        for side in range(2):
            await_bytes(near.at[a, side, e, which], near_recv.at[a, side, e, which])
        return (
            part[a, e, ring * RING + x].astype(SINGLE)
            + near[a, 0, e, which].astype(SINGLE)
            + near[a, 1, e, which].astype(SINGLE)
        )

    def reduce_over(a):
        for e in range(2):
            part[a, e, mate] = near_total(a, e, other, 1).astype(LOW)
            send_part(a, e, mate, over.at[a, e], 12 + e, over_recv.at[a, e], partner)

    def give_back(a):
        halves = ([], [])
        for e in range(2):
            total = near_total(a, e, z, 0)
            await_bytes(over.at[a, e], over_recv.at[a, e])
            total = (total + over[a, e].astype(SINGLE)).astype(LOW)
            halves[0].append(total)
        ready[a] = pack(jnp.concatenate(halves[0], axis=0), by_expert)
        collect(lambda block: ready.at[a, block], back.at[a], 2 + a)
        back[a, ex] = ready[a, lane]

    def given(a):
        received(back.at[a], 2 + a)
        return jnp.concatenate(unpack(back[a], by_image, pairs), axis=1)

    stores = []

    def store(src, dst, k):
        copy = pltpu.make_async_copy(src, dst, local.at[k])
        copy.start()
        stores.append(copy)

    def weights(e):
        def flat(value):
            return value.reshape(value.shape[0] * value.shape[1], value.shape[2])

        w_out_grad[e] = outer(flat(act[e]), flat(rows[1, e]))
        w_in_grad[e] = outer(flat(rows[0, e]), flat(pre_grad[e]))
        store(w_out_grad.at[e], w_out_grad_hbm.at[e], 4 + e)
        store(w_in_grad.at[e], w_in_grad_hbm.at[e], 6 + e)

    own_rows(0)
    gather_own(0)
    deliver(message.at[1], got.at[1], 1)
    for load in loads[2:]:
        load.wait()
    over_experts(forward, own)
    gather_mate(0)
    gather_far(0)
    over_experts(forward, mate)
    own_rows(1)
    gather_own(1)
    near_rest(0)
    over_near(forward, z)
    gather_cross(0)
    over_experts(forward, z * RING + x_far)
    near_other(0)
    over_near(forward, other)
    gather_mate(1)
    gather_far(1)
    reduce_near_free(0)
    cross_rest(0)
    over_experts(forward, other * RING + x_far)
    reduce_cross(0)
    over_experts(backward, own)
    over_experts(backward, mate)
    near_rest(1)
    over_near(backward, z)
    gather_cross(1)
    reduce_far(0)
    over_experts(backward, z * RING + x_far)
    near_other(1)
    over_near(backward, other)
    reduce_near(0)
    reduce_near_free(1)
    reduce_over(0)
    cross_rest(1)
    over_experts(backward, other * RING + x_far)
    reduce_cross(1)
    give_back(0)
    weights(0)
    reduce_far(1)
    reduce_over(1)
    weights(1)
    reduce_near(1)

    slot_out = given(0)
    result[0] = outer(combine_low[...], slot_out)[:n_tokens].astype(LOW)
    store(result.at[0], mixed_hbm, 8)
    grad = together(turn(slot_out, held[1]))
    weight = combine[...]
    combine_term[...] = weight * (grad - jnp.sum(weight * grad, axis=0, keepdims=True))

    give_back(1)
    input_slots = given(1)
    grad = together(turn(input_slots, held[0]))
    weight = dispatch[...]
    grad = weight * (grad - per_image(jnp.sum, weight * grad, 0.0)) + combine_term[...]
    grad = jnp.where(image_of >= 0, grad, 0.0).astype(LOW)
    total = dot(grad, held[0]).astype(LOW)
    away = distance((experts * CHUNK, slots), 0, by_slot)
    block = sum(
        dot(mark(away, c), total[:, c * LANES : (c + 1) * LANES]) for c in range(chunks)
    )
    router_message[...] = block.astype(LOW).reshape(experts, CHUNK, LANES)
    deliver(router_message, router_first, 5)
    value = outer(dispatch_low[...], input_slots) + outer(grad, router[...])
    result[1] = value[:n_tokens].astype(LOW)
    store(result.at[1], tokens_grad_hbm, 9)

    received(router_first, 5)
    router_mine[...] = jnp.sum(router_first[...].astype(SINGLE), axis=0)

    def share(k, carry):
        pltpu.make_async_remote_copy(
            src_ref=router_mine,
            dst_ref=router_second.at[dp],
            send_sem=a2a_send.at[6],
            recv_sem=a2a_recv.at[6],
            device_id=(lax.rem(dp + k, shards), ex),
            device_id_type=MESH,
        ).start()
        return carry

    lax.fori_loop(1, shards, share, 0)
    router_second[dp] = router_mine[...]
    await_bytes(router_second.at[pl.ds(0, shards - 1)], a2a_recv.at[6])
    router_total[...] = jnp.sum(router_second[...], axis=0)

    for k in range(4):
        await_bytes(got.at[0, pl.ds(0, experts - 1)], a2a_send.at[k])
    for k in range(4, 6):
        await_bytes(router_got.at[pl.ds(0, experts - 1)], a2a_send.at[k])
    await_bytes(router_second.at[pl.ds(0, shards - 1)], a2a_send.at[6])
    for copy in sent:
        copy.wait_send()
    for copy in stores:
        copy.wait()


def body(experts, tokens, router, w_in, w_out, cotangent):
    images, n, d = tokens.shape
    hidden = w_in.shape[2]
    owned = router.shape[1]
    slots = experts * owned
    n_tokens = images * n
    n_padded = -(-n_tokens // LANES) * LANES
    n_rows = experts * images
    used = d * owned // LANES
    half = d // 2

    def flat(value):
        return value.transpose(1, 0, 2).reshape(n_tokens, d)

    def unflat(value):
        return value.reshape(n, images, d).transpose(1, 0, 2)

    def low(*shape):
        return pltpu.VMEM(shape, LOW)

    def single(*shape):
        return pltpu.VMEM(shape, SINGLE)

    router_own = jnp.pad(router.T.reshape(used, LANES), ((0, CHUNK - used), (0, 0)))
    anywhere = pl.BlockSpec(memory_space=pl.ANY)
    vmem = pl.BlockSpec(memory_space=pltpu.VMEM)
    dma = pltpu.SemaphoreType.DMA
    mixed, tokens_grad, w_in_grad, w_out_grad, router_total = pl.pallas_call(
        functools.partial(layer_kernel, experts, images),
        out_shape=[
            jax.ShapeDtypeStruct((n_tokens, d), LOW),
            jax.ShapeDtypeStruct((n_tokens, d), LOW),
            jax.ShapeDtypeStruct(w_in.shape, SINGLE),
            jax.ShapeDtypeStruct(w_out.shape, SINGLE),
            jax.ShapeDtypeStruct((CHUNK, LANES), SINGLE),
        ],
        in_specs=[anywhere, anywhere, vmem, anywhere, anywhere],
        out_specs=[anywhere] * 4 + [vmem],
        scratch_shapes=[
            low(2, n_padded, d),
            low(*w_in.shape),
            low(*w_out.shape),
            low(experts, CHUNK, LANES),
            low(slots, d),
            single(slots, n_padded),
            single(slots, n_padded),
            low(images * slots, n_padded),
            low(images * slots, n_padded),
            low(2, experts, 4 * images, half),
            low(2, experts, 4 * images, half),
            low(2, 2, 2 * RING, n_rows, d),
            low(2, 2, 2 * RING, n_rows, d),
            low(2, 2 * RING, n_rows, hidden),
            single(2, 2 * RING, n_rows, hidden),
            low(2, 2 * RING, n_rows, hidden),
            low(2, 2, n_rows, d),
            low(2, 2, n_rows, d),
            low(2, 2, 2, 2, n_rows, d),
            low(2, 2, n_rows, d),
            low(2, experts, 4 * images, half),
            low(2, experts, 4 * images, half),
            single(slots, n_padded),
            single(*w_in.shape),
            single(*w_out.shape),
            low(2, n_tokens, d),
            low(experts, CHUNK, LANES),
            low(experts, CHUNK, LANES),
            single(CHUNK, LANES),
            single(2 * RING, CHUNK, LANES),
            dma((10,)),
            dma((7,)),
            dma((7,)),
            dma((2, 14)),
            dma((2, 2, 2 * RING)),
            dma((2, 14)),
            dma((2, 2)),
            dma((2, 2)),
            dma((2, 2, 2, 2)),
            dma((2, 2)),
        ],
        compiler_params=pltpu.CompilerParams(
            collective_id=0, has_side_effects=True, vmem_limit_bytes=58 * 1024 * 1024
        ),
        name="layer",
    )(flat(tokens), flat(cotangent), router_own, w_in, w_out)
    router_grad = router_total[:used].reshape(owned, d).T
    return (unflat(mixed), unflat(tokens_grad), w_in_grad, w_out_grad, router_grad)


def solution(mesh):
    placed = (
        P(("dp", "expert"), None, None),
        P(None, "expert"),
        P("expert", None, "dp"),
        P("expert", "dp", None),
        P(("dp", "expert"), None, None),
    )
    return jax.shard_map(
        functools.partial(body, mesh.shape["expert"]),
        mesh=mesh,
        in_specs=placed,
        out_specs=(
            P(("dp", "expert"), None, None),
            P(("dp", "expert"), None, None),
            P("expert", None, "dp"),
            P("expert", "dp", None),
            P(None, "expert"),
        ),
        check_vma=False,
    )
```

```python
import functools

import jax
import jax.numpy as jnp
from jax import lax
from jax.experimental import pallas as pl
from jax.experimental.pallas import tpu as pltpu
from jax.sharding import PartitionSpec as P

SINGLE = jnp.float32
LOW = jnp.bfloat16
MESH = pl.DeviceIdType.MESH
RING = 4
Z_HIGH = 4
LANES = 128
CHUNK = 16


def remote(src, dst, send, recv, device):
    copy = pltpu.make_async_remote_copy(
        src_ref=src, dst_ref=dst, send_sem=send, recv_sem=recv, device_id=device, device_id_type=MESH
    )
    copy.start()
    return copy


def await_bytes(ref, sem):
    pltpu.make_async_copy(ref, ref, sem).wait()


def gelu_and_slope(v):
    c = 0.7978845608028654
    square = v * v
    t = jnp.tanh(c * v * (1.0 + 0.044715 * square))
    half = 0.5 * (1.0 + t)
    slope = half + 0.5 * v * (1.0 - t * t) * (c * (1.0 + 3.0 * 0.044715 * square))
    return v * half, slope


def turn(lhs, rhs):
    return lax.dot_general(lhs, rhs, (((1,), (1,)), ((), ())), preferred_element_type=SINGLE)


def outer(lhs, rhs):
    return lax.dot_general(lhs, rhs, (((0,), (0,)), ((), ())), preferred_element_type=SINGLE)


def dot(lhs, rhs):
    return jnp.dot(lhs, rhs, preferred_element_type=SINGLE)


def place_of(z_at, lane, x, experts):
    z_at = lax.rem(z_at + 4 * Z_HIGH, 2 * Z_HIGH)
    return (lax.rem(z_at, 2) * RING + x, (z_at // 2) * (experts // Z_HIGH) + lane)


def layer_kernel(
    experts,
    images,
    tokens_hbm,
    cotangent_hbm,
    router_own,
    w_in_hbm,
    w_out_hbm,
    mixed_hbm,
    tokens_grad_hbm,
    w_in_grad_hbm,
    w_out_grad_hbm,
    router_total,
    raw,
    held,
    w_in,
    w_out,
    mate_in,
    mate_out,
    give_in,
    give_out,
    took_in,
    took_out,
    router_got,
    router,
    dispatch,
    combine,
    dispatch_low,
    combine_low,
    message,
    got,
    rows,
    part,
    act,
    slope,
    pre_grad,
    cross,
    far,
    near,
    over,
    ready,
    back,
    combine_term,
    w_in_grad,
    w_out_grad,
    router_message,
    router_first,
    router_mine,
    router_second,
    local,
    a2a_send,
    a2a_recv,
    swap_send,
    swap_recv,
    ag_send,
    ag_recv,
    ag_far,
    rs_send,
    cross_recv,
    far_recv,
    near_recv,
    over_recv,
):
    dp, ex = lax.axis_index("dp"), lax.axis_index("expert")
    shards = 2 * RING
    x, z = lax.rem(dp, RING), dp // RING
    x_right, x_left = lax.rem(x + 1, RING), lax.rem(x + 3, RING)
    x_far = lax.rem(x + 2, RING)
    other = 1 - z
    partner = (other * RING + x, ex)
    right = (z * RING + x_right, ex)
    left = (z * RING + x_left, ex)
    own = dp
    mate = other * RING + x
    n_rows = experts * images
    half = rows.shape[-1] // 2
    slots = 2 * experts
    pairs = images * slots
    n_tokens, n_padded = tokens_hbm.shape[0] * images, held.shape[1]
    chunks = rows.shape[-1] // LANES
    inner = experts // Z_HIGH
    lane = lax.rem(ex, inner)
    z_at = (ex // inner) * 2 + z
    way = 1 - 2 * z

    loads = [
        pltpu.make_async_copy(src, dst, local.at[k])
        for k, (src, dst) in enumerate(
            (
                (tokens_hbm, raw.at[0]),
                (cotangent_hbm, raw.at[1]),
                (w_in_hbm, w_in),
                (w_out_hbm, w_out),
            )
        )
    ]
    for load in loads:
        load.start()

    barrier = pltpu.get_barrier_semaphore()

    def greet_experts(k, carry):
        step = k // inner
        step = step - (step // Z_HIGH) * (Z_HIGH + 2)
        to = place_of(z_at - step * way, lax.rem(lane + k, inner), x, experts)
        pl.semaphore_signal(barrier, inc=1, device_id=to, device_id_type=MESH)
        return carry

    def greet_shards(k, carry):
        to = (lax.rem(dp + k, shards), ex)
        pl.semaphore_signal(barrier, inc=1, device_id=to, device_id_type=MESH)
        return carry

    greeted = (Z_HIGH + 1) * inner
    lax.fori_loop(1, greeted, greet_experts, 0)
    lax.fori_loop(1, shards, greet_shards, 0)
    for k in range(2):
        loads[k].wait()
        held[k, :n_tokens] = raw[k].reshape(n_tokens, held.shape[2])
        if n_padded > n_tokens:
            held[k, n_tokens:] = jnp.zeros((n_padded - n_tokens, held.shape[2]), LOW)
    pl.semaphore_wait(barrier, greeted - 1 + shards - 1)

    for load in loads[2:]:
        load.wait()
    swaps = [
        remote(w_in.at[0], mate_in, swap_send.at[0], swap_recv.at[0], partner),
        remote(w_out.at[0], mate_out, swap_send.at[1], swap_recv.at[1], partner),
    ]

    def deliver(src, dst, k):
        def one(i, carry):
            step = i // inner
            to = place_of(
                z_at + step * way * (1 - 2 * lax.rem(step, 2)), lax.rem(lane + i, inner), x, experts
            )
            pltpu.make_async_remote_copy(
                src_ref=src.at[to[1]],
                dst_ref=dst.at[step * inner + lane],
                send_sem=a2a_send.at[k],
                recv_sem=a2a_recv.at[k],
                device_id=to,
                device_id_type=MESH,
            ).start()
            return carry

        lax.fori_loop(1, experts, one, 0)
        dst[lane] = src[ex]

    def collect(src_of, dst, k):
        def one(i, carry):
            step = i // inner
            there = lax.rem(lane + i, inner)
            pltpu.make_async_remote_copy(
                src_ref=src_of(step * inner + there),
                dst_ref=dst.at[ex],
                send_sem=a2a_send.at[k],
                recv_sem=a2a_recv.at[k],
                device_id=place_of(z_at - step * way, there, x, experts),
                device_id_type=MESH,
            ).start()
            return carry

        lax.fori_loop(1, experts, one, 0)

    def received(ref, k):
        await_bytes(ref.at[pl.ds(0, experts - 1)], a2a_recv.at[k])

    def iota(shape, axis):
        return lax.broadcasted_iota(jnp.int32, shape, axis)

    def bits(n):
        return n.bit_length() - 1

    def by_expert(row):
        slot = (row >= n_rows).astype(jnp.int32)
        row = row - slot * n_rows
        image = lax.bitwise_and(row, images - 1)
        return lax.shift_right_logical(row, bits(images)) * 4 * images + slot * images + image

    def by_image(row):
        slot = lax.bitwise_and(row, slots - 1)
        image = lax.shift_right_logical(row, bits(slots))
        odd = lax.bitwise_and(slot, 1)
        return lax.shift_right_logical(slot, 1) * 4 * images + odd * images + image

    def by_slot(row):
        odd = lax.bitwise_and(row, 1)
        return lax.shift_right_logical(row, 1) * CHUNK + odd * chunks

    def distance(shape, axis, order):
        return iota(shape, axis) - order(iota(shape, 1 - axis))

    def mark(distances, at):
        return (distances == at).astype(SINGLE).astype(LOW)

    def pack(value, order):
        n = value.shape[0]
        away = distance((experts * 4 * images, n), 0, order)
        block = sum(
            dot(mark(away, h * 2 * images), value[:, h * half : (h + 1) * half]) for h in range(2)
        )
        return block.astype(LOW).reshape(experts, 4 * images, half)

    def unpack(value, order, n):
        flat = value.reshape(experts * 4 * images, half)
        away = distance((n, experts * 4 * images), 1, order)
        return [dot(mark(away, h * 2 * images), flat).astype(LOW) for h in range(2)]

    collect(lambda block: router_own, router_got, 4)
    router_got[ex] = router_own[...]
    received(router_got, 4)
    flat = router_got[...].reshape(experts * CHUNK, LANES)
    away = distance((slots, experts * CHUNK), 1, by_slot)
    for c in range(chunks):
        router[:, c * LANES : (c + 1) * LANES] = dot(mark(away, c), flat).astype(LOW)

    column = iota((slots, n_padded), 1)
    image_of = jnp.where(column < n_tokens, lax.bitwise_and(column, images - 1), -1)

    def per_image(reduce, value, fill):
        spread = jnp.zeros_like(value)
        for i in range(images):
            mine = image_of == i
            total = reduce(jnp.where(mine, value, fill), axis=1, keepdims=True)
            spread = jnp.where(mine, total, spread)
        return spread

    def apart(value, low):
        for i in range(images):
            low[i * slots : (i + 1) * slots] = jnp.where(image_of == i, value, 0.0).astype(LOW)

    def together(value):
        total = jnp.zeros((slots, n_padded), SINGLE)
        for i in range(images):
            total = jnp.where(image_of == i, value[i * slots : (i + 1) * slots], total)
        return total

    logits = turn(router[...], held[0])
    weight = jnp.exp(logits - per_image(jnp.max, logits, -jnp.inf))
    weight = jnp.where(image_of >= 0, weight, 0.0)
    weight = weight / jnp.where(image_of >= 0, per_image(jnp.sum, weight, 0.0), 1.0)
    dispatch[...] = weight
    apart(weight, dispatch_low)
    message[0] = pack(dot(dispatch_low[...], held[0]).astype(LOW), by_image)
    deliver(message.at[0], got.at[0], 0)
    weight = jnp.exp(logits - jnp.max(logits, axis=0, keepdims=True))
    weight = weight / jnp.sum(weight, axis=0, keepdims=True)
    combine[...] = weight
    apart(weight, combine_low)
    message[1] = pack(dot(combine_low[...], held[1]).astype(LOW), by_image)

    def own_rows(a):
        received(got.at[a], a)
        for h, block in enumerate(unpack(got[a], by_expert, 2 * n_rows)):
            for e in range(2):
                rows[a, e, own, :, h * half : (h + 1) * half] = block[e * n_rows : (e + 1) * n_rows]

    sent = []
    bands = (pl.ds(0, n_rows // 2), pl.ds(n_rows // 2, n_rows // 2))
    x_near = (x_left, x_right)
    onward = (right, left)

    def send_block(a, e, p, to, slot):
        block = rows.at[a, e, p]
        sent.append(remote(block, block, ag_send.at[a, slot], ag_recv.at[a, e, p], to))

    def arrived(a, e, p):
        await_bytes(rows.at[a, e, p], ag_recv.at[a, e, p])

    def gather_own(a):
        send_block(a, 0, own, right, 0)
        send_block(a, 0, own, left, 1)
        send_block(a, 1, own, partner, 2)
        send_block(a, 1, own, right, 3)
        send_block(a, 1, own, left, 4)

    def gather_mate(a):
        arrived(a, 1, mate)
        send_block(a, 1, mate, right, 5)
        send_block(a, 1, mate, left, 6)

    def gather_far(a, path):
        e, ring = min(path, 1), (z, z, other)[path]
        for side in range(2):
            p = ring * RING + x_near[side]
            arrived(a, e, p)
            block = rows.at[a, e, p, bands[side]]
            sent.append(
                remote(
                    block,
                    block,
                    ag_send.at[a, 7 + 2 * path + side],
                    ag_far.at[a, path, side],
                    onward[side],
                )
            )

    def far_rest(a, path):
        e, ring = min(path, 1), (z, z, other)[path]
        for side in range(2):
            await_bytes(rows.at[a, e, ring * RING + x_far, bands[side]], ag_far.at[a, path, side])

    def gather_cross(a):
        send_block(a, 1, z * RING + x_far, partner, 11)

    def near_other(a):
        for side in range(2):
            arrived(a, 1, other * RING + x_near[side])

    def forward(p):
        value, grade = gelu_and_slope(dot(rows[0, 1, p], w_in[1]))
        value = value.astype(LOW)
        act[1, p] = value
        slope[1, p] = grade
        part[0, 1, p] = dot(value, w_out[1]).astype(LOW)

    def backward(p):
        grad = turn(rows[1, 1, p], w_out[1])
        grad = (grad * slope[1, p]).astype(LOW)
        pre_grad[1, p] = grad
        part[1, 1, p] = turn(grad, w_in[1]).astype(LOW)

    def near_ring(step, ring):
        def one(k, carry):
            step(ring * RING + lax.rem(x + 1 + 2 * k, RING))
            return carry

        lax.fori_loop(0, 2, one, 0)

    def whole_ring(step):
        def one(k, carry):
            step(k)
            return carry

        lax.fori_loop(0, RING, one, 0)

    hidden = ((w_in.at[0], w_out.at[0]), (mate_in, mate_out))

    def forward_both(k):
        p = z * RING + k
        total = 0.0
        for h, (first, second) in enumerate(hidden):
            value, grade = gelu_and_slope(dot(rows[0, 0, p], first[...]))
            value = value.astype(LOW)
            act[0, h * RING + k] = value
            slope[0, h * RING + k] = grade
            total = total + dot(value, second[...])
        part[0, 0, p] = total.astype(LOW)

    def backward_both(k):
        p = z * RING + k
        total = 0.0
        for h, (first, second) in enumerate(hidden):
            grad = turn(rows[1, 0, p], second[...])
            grad = (grad * slope[0, h * RING + k]).astype(LOW)
            pre_grad[0, h * RING + k] = grad
            total = total + turn(grad, first[...])
        part[1, 0, p] = total.astype(LOW)

    def send_part(src, dst, send, recv, to):
        sent.append(remote(src, dst, send, recv, to))

    def reduce_cross(a):
        send_part(
            part.at[a, 1, other * RING + x_far], cross, rs_send.at[a, 0], cross_recv.at[0], partner
        )

    def add_cross(a):
        p = z * RING + x_far
        await_bytes(cross, cross_recv.at[0])
        total = part[a, 1, p].astype(SINGLE) + cross[...].astype(SINGLE)
        part[a, 1, p] = total.astype(LOW)

    def reduce_far(a, path):
        e, ring = min(path, 1), (z, z, other)[path]
        for side in range(2):
            send_part(
                part.at[a, e, ring * RING + x_far, bands[side]],
                far.at[a, path, side],
                rs_send.at[a, 1 + 2 * path + side],
                far_recv.at[a, path, side],
                onward[side],
            )

    def send_near(a, path, side, band):
        e, ring = min(path, 1), (z, z, other)[path]
        send_part(
            part.at[a, e, ring * RING + x_near[1 - side], bands[band]],
            near.at[a, path, side, bands[band]],
            rs_send.at[a, 7 + 4 * path + 2 * side + band],
            near_recv.at[a, path, side, band],
            onward[side],
        )

    def near_free(a, path):
        for side in range(2):
            send_near(a, path, side, 1 - side)

    def near_same(a, path):
        for side in range(2):
            send_near(a, path, side, side)

    def near_summed(a, path):
        e, ring = min(path, 1), (z, z, other)[path]
        for side in range(2):
            p = ring * RING + x_near[1 - side]
            await_bytes(far.at[a, path, side], far_recv.at[a, path, side])
            total = part[a, e, p, bands[side]].astype(SINGLE) + far[a, path, side].astype(SINGLE)
            part[a, e, p, bands[side]] = total.astype(LOW)
            send_near(a, path, side, side)

    def near_total(a, path):
        e, ring = min(path, 1), (z, z, other)[path]
        for side in range(2):
            for band in range(2):
                await_bytes(near.at[a, path, side, bands[band]], near_recv.at[a, path, side, band])
        return (
            part[a, e, ring * RING + x].astype(SINGLE)
            + near[a, path, 0].astype(SINGLE)
            + near[a, path, 1].astype(SINGLE)
        )

    def reduce_over(a):
        part[a, 1, mate] = near_total(a, 2).astype(LOW)
        send_part(part.at[a, 1, mate], over.at[a], rs_send.at[a, 19], over_recv.at[a], partner)

    def give_back(a):
        first = near_total(a, 0)
        second = near_total(a, 1)
        await_bytes(over.at[a], over_recv.at[a])
        second = second + over[a].astype(SINGLE)
        total = jnp.concatenate([first.astype(LOW), second.astype(LOW)], axis=0)
        ready[a] = pack(total, by_expert)
        collect(lambda block: ready.at[a, block], back.at[a], 2 + a)
        back[a, ex] = ready[a, lane]

    def given(a):
        received(back.at[a], 2 + a)
        return jnp.concatenate(unpack(back[a], by_image, pairs), axis=1)

    stores = []

    def store(src, dst, k):
        copy = pltpu.make_async_copy(src, dst, local.at[k])
        copy.start()
        stores.append(copy)

    def flat(value):
        return value.reshape(value.shape[0] * value.shape[1], value.shape[2])

    def weights():
        w_out_grad[1] = outer(flat(act[1]), flat(rows[1, 1]))
        w_in_grad[1] = outer(flat(rows[0, 1]), flat(pre_grad[1]))
        store(w_out_grad.at[1], w_out_grad_hbm.at[1], 5)
        store(w_in_grad.at[1], w_in_grad_hbm.at[1], 7)

    def weights_both():
        mine = pl.ds(z * RING, RING)
        halves = (pl.ds(0, RING), pl.ds(RING, RING))
        give_out[...] = outer(flat(act[0, halves[1]]), flat(rows[1, 0, mine])).astype(LOW)
        sent.append(remote(give_out, took_out, swap_send.at[2], swap_recv.at[2], partner))
        give_in[...] = outer(flat(rows[0, 0, mine]), flat(pre_grad[0, halves[1]])).astype(LOW)
        sent.append(remote(give_in, took_in, swap_send.at[3], swap_recv.at[3], partner))
        w_out_grad[0] = outer(flat(act[0, halves[0]]), flat(rows[1, 0, mine]))
        w_in_grad[0] = outer(flat(rows[0, 0, mine]), flat(pre_grad[0, halves[0]]))

    def weights_taken():
        await_bytes(took_out, swap_recv.at[2])
        w_out_grad[0] = w_out_grad[0] + took_out[...].astype(SINGLE)
        store(w_out_grad.at[0], w_out_grad_hbm.at[0], 4)
        await_bytes(took_in, swap_recv.at[3])
        w_in_grad[0] = w_in_grad[0] + took_in[...].astype(SINGLE)
        store(w_in_grad.at[0], w_in_grad_hbm.at[0], 6)

    far_ring = z * RING + x_far
    far_other = other * RING + x_far
    own_rows(0)
    gather_own(0)
    deliver(message.at[1], got.at[1], 1)
    forward(own)
    gather_mate(0)
    gather_far(0, 1)
    gather_far(0, 0)
    forward(mate)
    own_rows(1)
    gather_own(1)
    near_ring(forward, z)
    far_rest(0, 1)
    gather_cross(0)
    forward(far_ring)
    near_other(0)
    near_ring(forward, other)
    gather_mate(1)
    gather_far(1, 0)
    gather_far(1, 1)
    far_rest(0, 0)
    await_bytes(mate_in, swap_recv.at[0])
    await_bytes(mate_out, swap_recv.at[1])
    whole_ring(forward_both)
    reduce_far(0, 0)
    near_free(0, 0)
    near_free(0, 2)
    near_same(0, 2)
    near_free(0, 1)
    gather_far(1, 2)
    arrived(0, 1, far_other)
    forward(far_other)
    reduce_cross(0)
    backward(own)
    backward(mate)
    near_ring(backward, z)
    far_rest(1, 0)
    whole_ring(backward_both)
    reduce_far(1, 0)
    near_free(1, 0)
    add_cross(0)
    reduce_far(0, 1)
    weights_both()
    near_summed(0, 0)
    far_rest(1, 1)
    backward(far_ring)
    reduce_far(1, 1)
    near_free(1, 1)
    near_ring(backward, other)
    far_rest(1, 2)
    backward(far_other)
    reduce_far(1, 2)
    near_free(1, 2)
    near_summed(0, 1)
    near_summed(1, 0)
    reduce_over(0)
    near_summed(1, 2)
    near_summed(1, 1)
    give_back(0)
    reduce_over(1)
    weights()
    weights_taken()

    slot_out = given(0)
    value = outer(combine_low[...], slot_out)[:n_tokens].astype(LOW)
    raw[0] = value.reshape(raw.shape[1:])
    store(raw.at[0], mixed_hbm, 8)
    grad = together(turn(slot_out, held[1]))
    weight = combine[...]
    combine_term[...] = weight * (grad - jnp.sum(weight * grad, axis=0, keepdims=True))

    give_back(1)
    input_slots = given(1)
    grad = together(turn(input_slots, held[0]))
    weight = dispatch[...]
    grad = weight * (grad - per_image(jnp.sum, weight * grad, 0.0)) + combine_term[...]
    grad = jnp.where(image_of >= 0, grad, 0.0).astype(LOW)
    total = dot(grad, held[0]).astype(LOW)
    away = distance((experts * CHUNK, slots), 0, by_slot)
    block = sum(
        dot(mark(away, c), total[:, c * LANES : (c + 1) * LANES]) for c in range(chunks)
    )
    router_message[...] = block.astype(LOW).reshape(experts, CHUNK, LANES)
    deliver(router_message, router_first, 5)
    value = outer(dispatch_low[...], input_slots) + outer(grad, router[...])
    raw[1] = value[:n_tokens].astype(LOW).reshape(raw.shape[1:])
    store(raw.at[1], tokens_grad_hbm, 9)

    received(router_first, 5)
    router_mine[...] = jnp.sum(router_first[...].astype(SINGLE), axis=0)

    def share(k, carry):
        pltpu.make_async_remote_copy(
            src_ref=router_mine,
            dst_ref=router_second.at[dp],
            send_sem=a2a_send.at[6],
            recv_sem=a2a_recv.at[6],
            device_id=(lax.rem(dp + k, shards), ex),
            device_id_type=MESH,
        ).start()
        return carry

    lax.fori_loop(1, shards, share, 0)
    router_second[dp] = router_mine[...]
    await_bytes(router_second.at[pl.ds(0, shards - 1)], a2a_recv.at[6])
    router_total[...] = jnp.sum(router_second[...], axis=0)

    for k in range(4):
        await_bytes(got.at[0, pl.ds(0, experts - 1)], a2a_send.at[k])
    for k in range(4, 6):
        await_bytes(router_got.at[pl.ds(0, experts - 1)], a2a_send.at[k])
    await_bytes(router_second.at[pl.ds(0, shards - 1)], a2a_send.at[6])
    for copy in swaps + sent:
        copy.wait_send()
    for copy in stores:
        copy.wait()


def body(experts, tokens, router, w_in, w_out, cotangent):
    images, n, d = tokens.shape
    hidden = w_in.shape[2]
    owned = router.shape[1]
    slots = experts * owned
    n_tokens = images * n
    n_padded = -(-n_tokens // LANES) * LANES
    n_rows = experts * images
    used = d * owned // LANES
    half = d // 2

    def swap(value):
        return value.transpose(1, 0, 2)

    def low(*shape):
        return pltpu.VMEM(shape, LOW)

    def single(*shape):
        return pltpu.VMEM(shape, SINGLE)

    router_own = jnp.pad(router.T.reshape(used, LANES), ((0, CHUNK - used), (0, 0)))
    anywhere = pl.BlockSpec(memory_space=pl.ANY)
    vmem = pl.BlockSpec(memory_space=pltpu.VMEM)
    dma = pltpu.SemaphoreType.DMA
    mixed, tokens_grad, w_in_grad, w_out_grad, router_total = pl.pallas_call(
        functools.partial(layer_kernel, experts, images),
        out_shape=[
            jax.ShapeDtypeStruct((n, images, d), LOW),
            jax.ShapeDtypeStruct((n, images, d), LOW),
            jax.ShapeDtypeStruct(w_in.shape, SINGLE),
            jax.ShapeDtypeStruct(w_out.shape, SINGLE),
            jax.ShapeDtypeStruct((CHUNK, LANES), SINGLE),
        ],
        in_specs=[anywhere, anywhere, vmem, anywhere, anywhere],
        out_specs=[anywhere] * 4 + [vmem],
        scratch_shapes=[
            low(2, n, images, d),
            low(2, n_padded, d),
            low(*w_in.shape),
            low(*w_out.shape),
            low(*w_in.shape[1:]),
            low(*w_out.shape[1:]),
            low(*w_in.shape[1:]),
            low(*w_out.shape[1:]),
            low(*w_in.shape[1:]),
            low(*w_out.shape[1:]),
            low(experts, CHUNK, LANES),
            low(slots, d),
            single(slots, n_padded),
            single(slots, n_padded),
            low(images * slots, n_padded),
            low(images * slots, n_padded),
            low(2, experts, 4 * images, half),
            low(2, experts, 4 * images, half),
            low(2, 2, 2 * RING, n_rows, d),
            low(2, 2, 2 * RING, n_rows, d),
            low(2, 2 * RING, n_rows, hidden),
            single(2, 2 * RING, n_rows, hidden),
            low(2, 2 * RING, n_rows, hidden),
            low(n_rows, d),
            low(2, 3, 2, n_rows // 2, d),
            low(2, 3, 2, n_rows, d),
            low(2, n_rows, d),
            low(2, experts, 4 * images, half),
            low(2, experts, 4 * images, half),
            single(slots, n_padded),
            single(*w_in.shape),
            single(*w_out.shape),
            low(experts, CHUNK, LANES),
            low(experts, CHUNK, LANES),
            single(CHUNK, LANES),
            single(2 * RING, CHUNK, LANES),
            dma((10,)),
            dma((7,)),
            dma((7,)),
            dma((4,)),
            dma((4,)),
            dma((2, 13)),
            dma((2, 2, 2 * RING)),
            dma((2, 3, 2)),
            dma((2, 20)),
            dma((1,)),
            dma((2, 3, 2)),
            dma((2, 3, 2, 2)),
            dma((2,)),
        ],
        compiler_params=pltpu.CompilerParams(
            collective_id=0, has_side_effects=True, vmem_limit_bytes=58 * 1024 * 1024
        ),
        name="layer",
    )(swap(tokens), swap(cotangent), router_own, w_in, w_out)
    router_grad = router_total[:used].reshape(owned, d).T
    return (swap(mixed), swap(tokens_grad), w_in_grad, w_out_grad, router_grad)


def solution(mesh):
    placed = (
        P(("dp", "expert"), None, None),
        P(None, "expert"),
        P("expert", None, "dp"),
        P("expert", "dp", None),
        P(("dp", "expert"), None, None),
    )
    return jax.shard_map(
        functools.partial(body, mesh.shape["expert"]),
        mesh=mesh,
        in_specs=placed,
        out_specs=(
            P(("dp", "expert"), None, None),
            P(("dp", "expert"), None, None),
            P("expert", None, "dp"),
            P("expert", "dp", None),
            P(None, "expert"),
        ),
        check_vma=False,
    )
```

```python
import functools

import jax
import jax.numpy as jnp
from jax import lax
from jax.experimental import pallas as pl
from jax.experimental.pallas import tpu as pltpu
from jax.sharding import PartitionSpec as P

SINGLE = jnp.float32
LOW = jnp.bfloat16
MESH = pl.DeviceIdType.MESH
RING = 4
Z_HIGH = 4
LANES = 128
CHUNK = 16


def remote(src, dst, send, recv, device):
    copy = pltpu.make_async_remote_copy(
        src_ref=src, dst_ref=dst, send_sem=send, recv_sem=recv, device_id=device, device_id_type=MESH
    )
    copy.start()
    return copy


def await_bytes(ref, sem):
    pltpu.make_async_copy(ref, ref, sem).wait()


def gelu_and_slope(v):
    c = 0.7978845608028654
    square = v * v
    t = jnp.tanh(c * v * (1.0 + 0.044715 * square))
    half = 0.5 * (1.0 + t)
    slope = half + 0.5 * v * (1.0 - t * t) * (c * (1.0 + 3.0 * 0.044715 * square))
    return v * half, slope


def turn(lhs, rhs):
    return lax.dot_general(lhs, rhs, (((1,), (1,)), ((), ())), preferred_element_type=SINGLE)


def outer(lhs, rhs):
    return lax.dot_general(lhs, rhs, (((0,), (0,)), ((), ())), preferred_element_type=SINGLE)


def dot(lhs, rhs):
    return jnp.dot(lhs, rhs, preferred_element_type=SINGLE)


def place_of(z_at, lane, x, experts):
    z_at = lax.rem(z_at + 4 * Z_HIGH, 2 * Z_HIGH)
    return (lax.rem(z_at, 2) * RING + x, (z_at // 2) * (experts // Z_HIGH) + lane)


def layer_kernel(
    experts,
    images,
    tokens_hbm,
    cotangent_hbm,
    router_own,
    w_in_hbm,
    w_out_hbm,
    mixed_hbm,
    tokens_grad_hbm,
    w_in_grad_hbm,
    w_out_grad_hbm,
    router_total,
    raw,
    held,
    w_in,
    w_out,
    mate_in,
    mate_out,
    give_in,
    give_out,
    took_in,
    took_out,
    router_got,
    router,
    dispatch,
    combine,
    dispatch_low,
    combine_low,
    message,
    got,
    rows,
    part,
    act,
    slope,
    pre_grad,
    far,
    near,
    aside,
    over,
    ready,
    back,
    combine_term,
    w_in_grad,
    w_out_grad,
    router_message,
    router_first,
    router_mine,
    router_second,
    local,
    a2a_send,
    a2a_recv,
    swap_send,
    swap_recv,
    ag_send,
    ag_recv,
    ag_far,
    rs_send,
    far_recv,
    near_recv,
    aside_recv,
    over_recv,
):
    dp, ex = lax.axis_index("dp"), lax.axis_index("expert")
    shards = 2 * RING
    x, z = lax.rem(dp, RING), dp // RING
    odd = lax.rem(x, 2)
    partner = ((1 - z) * RING + x, ex)
    right = (z * RING + lax.rem(x + 1, RING), ex)
    left = (z * RING + lax.rem(x + 3, RING), ex)
    across = (z * RING + lax.rem(x + 1 + 2 * odd, RING), ex)
    beside = (z * RING + lax.rem(x + 3 + 2 * odd, RING), ex)
    n_rows = experts * images
    half = rows.shape[-1] // 2
    slots = 2 * experts
    pairs = images * slots
    n_tokens, n_padded = tokens_hbm.shape[0] * images, held.shape[1]
    chunks = rows.shape[-1] // LANES
    inner = experts // Z_HIGH
    lane = lax.rem(ex, inner)
    z_at = (ex // inner) * 2 + z
    way = 1 - 2 * z

    loads = [
        pltpu.make_async_copy(src, dst, local.at[k])
        for k, (src, dst) in enumerate(
            (
                (tokens_hbm, raw.at[0]),
                (cotangent_hbm, raw.at[1]),
                (w_in_hbm, w_in),
                (w_out_hbm, w_out),
            )
        )
    ]
    for load in loads:
        load.start()

    barrier = pltpu.get_barrier_semaphore()

    def greet_experts(k, carry):
        step = k // inner
        step = step - (step // Z_HIGH) * (Z_HIGH + 2)
        to = place_of(z_at - step * way, lax.rem(lane + k, inner), x, experts)
        pl.semaphore_signal(barrier, inc=1, device_id=to, device_id_type=MESH)
        return carry

    def greet_shards(k, carry):
        to = (lax.rem(dp + k, shards), ex)
        pl.semaphore_signal(barrier, inc=1, device_id=to, device_id_type=MESH)
        return carry

    greeted = (Z_HIGH + 1) * inner
    lax.fori_loop(1, greeted, greet_experts, 0)
    lax.fori_loop(1, shards, greet_shards, 0)
    for k in range(2):
        loads[k].wait()
        held[k, :n_tokens] = raw[k].reshape(n_tokens, held.shape[2])
        if n_padded > n_tokens:
            held[k, n_tokens:] = jnp.zeros((n_padded - n_tokens, held.shape[2]), LOW)
    pl.semaphore_wait(barrier, greeted - 1 + shards - 1)

    for load in loads[2:]:
        load.wait()
    swap_with = (partner, across)

    def swap(e, k, src, dst):
        sent.append(remote(src, dst, swap_send.at[e, k], swap_recv.at[e, k], swap_with[e]))

    sent = []
    swap(1, 0, w_in.at[1], mate_in.at[1])
    swap(0, 0, w_in.at[0], mate_in.at[0])
    swap(1, 1, w_out.at[1], mate_out.at[1])

    def deliver(src, dst, k):
        def one(i, carry):
            step = i // inner
            to = place_of(
                z_at + step * way * (1 - 2 * lax.rem(step, 2)), lax.rem(lane + i, inner), x, experts
            )
            pltpu.make_async_remote_copy(
                src_ref=src.at[to[1]],
                dst_ref=dst.at[step * inner + lane],
                send_sem=a2a_send.at[k],
                recv_sem=a2a_recv.at[k],
                device_id=to,
                device_id_type=MESH,
            ).start()
            return carry

        lax.fori_loop(1, experts, one, 0)
        dst[lane] = src[ex]

    def collect(src_of, dst, k):
        def one(i, carry):
            step = i // inner
            there = lax.rem(lane + i, inner)
            pltpu.make_async_remote_copy(
                src_ref=src_of(step * inner + there),
                dst_ref=dst.at[ex],
                send_sem=a2a_send.at[k],
                recv_sem=a2a_recv.at[k],
                device_id=place_of(z_at - step * way, there, x, experts),
                device_id_type=MESH,
            ).start()
            return carry

        lax.fori_loop(1, experts, one, 0)

    def received(ref, k):
        await_bytes(ref.at[pl.ds(0, experts - 1)], a2a_recv.at[k])

    def iota(shape, axis):
        return lax.broadcasted_iota(jnp.int32, shape, axis)

    def bits(n):
        return n.bit_length() - 1

    def by_expert(row):
        slot = (row >= n_rows).astype(jnp.int32)
        row = row - slot * n_rows
        image = lax.bitwise_and(row, images - 1)
        return lax.shift_right_logical(row, bits(images)) * 4 * images + slot * images + image

    def by_image(row):
        slot = lax.bitwise_and(row, slots - 1)
        image = lax.shift_right_logical(row, bits(slots))
        odd = lax.bitwise_and(slot, 1)
        return lax.shift_right_logical(slot, 1) * 4 * images + odd * images + image

    def by_slot(row):
        odd = lax.bitwise_and(row, 1)
        return lax.shift_right_logical(row, 1) * CHUNK + odd * chunks

    def distance(shape, axis, order):
        return iota(shape, axis) - order(iota(shape, 1 - axis))

    def mark(distances, at):
        return (distances == at).astype(SINGLE).astype(LOW)

    def pack(value, order):
        n = value.shape[0]
        away = distance((experts * 4 * images, n), 0, order)
        block = sum(
            dot(mark(away, h * 2 * images), value[:, h * half : (h + 1) * half]) for h in range(2)
        )
        return block.astype(LOW).reshape(experts, 4 * images, half)

    def unpack(value, order, n):
        flat = value.reshape(experts * 4 * images, half)
        away = distance((n, experts * 4 * images), 1, order)
        return [dot(mark(away, h * 2 * images), flat).astype(LOW) for h in range(2)]

    collect(lambda block: router_own, router_got, 4)
    router_got[ex] = router_own[...]
    received(router_got, 4)
    flat = router_got[...].reshape(experts * CHUNK, LANES)
    away = distance((slots, experts * CHUNK), 1, by_slot)
    for c in range(chunks):
        router[:, c * LANES : (c + 1) * LANES] = dot(mark(away, c), flat).astype(LOW)

    column = iota((slots, n_padded), 1)
    image_of = jnp.where(column < n_tokens, lax.bitwise_and(column, images - 1), -1)

    def per_image(reduce, value, fill):
        spread = jnp.zeros_like(value)
        for i in range(images):
            mine = image_of == i
            total = reduce(jnp.where(mine, value, fill), axis=1, keepdims=True)
            spread = jnp.where(mine, total, spread)
        return spread

    def apart(value, low):
        for i in range(images):
            low[i * slots : (i + 1) * slots] = jnp.where(image_of == i, value, 0.0).astype(LOW)

    def together(value):
        total = jnp.zeros((slots, n_padded), SINGLE)
        for i in range(images):
            total = jnp.where(image_of == i, value[i * slots : (i + 1) * slots], total)
        return total

    logits = turn(router[...], held[0])
    weight = jnp.exp(logits - per_image(jnp.max, logits, -jnp.inf))
    weight = jnp.where(image_of >= 0, weight, 0.0)
    weight = weight / jnp.where(image_of >= 0, per_image(jnp.sum, weight, 0.0), 1.0)
    dispatch[...] = weight
    apart(weight, dispatch_low)
    message[0] = pack(dot(dispatch_low[...], held[0]).astype(LOW), by_image)
    deliver(message.at[0], got.at[0], 0)
    weight = jnp.exp(logits - jnp.max(logits, axis=0, keepdims=True))
    weight = weight / jnp.sum(weight, axis=0, keepdims=True)
    combine[...] = weight
    apart(weight, combine_low)
    message[1] = pack(dot(combine_low[...], held[1]).astype(LOW), by_image)

    def own_rows(a):
        received(got.at[a], a)
        for h, block in enumerate(unpack(got[a], by_expert, 2 * n_rows)):
            for e in range(2):
                rows[a, e, 0, :, h * half : (h + 1) * half] = block[e * n_rows : (e + 1) * n_rows]

    bands = (pl.ds(0, n_rows // 2), pl.ds(n_rows // 2, n_rows // 2))
    onward = (right, left)

    def send_block(a, e, src, dst, to, slot):
        sent.append(
            remote(rows.at[a, e, src], rows.at[a, e, dst], ag_send.at[a, slot], ag_recv.at[a, e, dst], to)
        )

    def arrived(a, e, j):
        await_bytes(rows.at[a, e, j], ag_recv.at[a, e, j])

    def gather_own(a):
        send_block(a, 1, 0, 1, partner, 0)
        send_block(a, 0, 0, 3, right, 1)
        send_block(a, 0, 0, 1, left, 2)
        send_block(a, 1, 0, 2, beside, 3)

    def gather_mate(a):
        arrived(a, 1, 1)
        send_block(a, 1, 1, 3, beside, 4)

    def gather_far(a):
        for side, j in enumerate((3, 1)):
            arrived(a, 0, j)
            sent.append(
                remote(
                    rows.at[a, 0, j, bands[side]],
                    rows.at[a, 0, 2, bands[side]],
                    ag_send.at[a, 5 + side],
                    ag_far.at[a, side],
                    onward[side],
                )
            )

    def far_rest(a):
        for side in range(2):
            await_bytes(rows.at[a, 0, 2, bands[side]], ag_far.at[a, side])

    def hidden(e):
        return ((w_in.at[e], w_out.at[e]), (mate_in.at[e], mate_out.at[e]))

    def forward(e, j):
        total = 0.0
        for h, (first, second) in enumerate(hidden(e)):
            value, grade = gelu_and_slope(dot(rows[0, e, j], first[...]))
            value = value.astype(LOW)
            act[e, h, j] = value
            slope[e, h, j] = grade
            total = total + dot(value, second[...])
        part[0, e, j] = total.astype(LOW)

    def backward(e, j):
        total = 0.0
        for h, (first, second) in enumerate(hidden(e)):
            grad = turn(rows[1, e, j], second[...])
            grad = (grad * slope[e, h, j]).astype(LOW)
            pre_grad[e, h, j] = grad
            total = total + turn(grad, first[...])
        part[1, e, j] = total.astype(LOW)

    def several(step, e, start, stop):
        def one(j, carry):
            step(e, j)
            return carry

        lax.fori_loop(start, stop, one, 0)

    def send_part(src, dst, send, recv, to):
        sent.append(remote(src, dst, send, recv, to))

    def reduce_far(a):
        for side in range(2):
            send_part(
                part.at[a, 0, 2, bands[side]],
                far.at[a, side],
                rs_send.at[a, side],
                far_recv.at[a, side],
                onward[side],
            )

    def send_near(a, side, band):
        send_part(
            part.at[a, 0, (1, 3)[side], bands[band]],
            near.at[a, side, bands[band]],
            rs_send.at[a, 2 + 2 * side + band],
            near_recv.at[a, side, band],
            onward[side],
        )

    def near_free(a):
        for side in range(2):
            send_near(a, side, 1 - side)

    def near_summed(a):
        for side in range(2):
            j = (1, 3)[side]
            await_bytes(far.at[a, side], far_recv.at[a, side])
            total = part[a, 0, j, bands[side]].astype(SINGLE) + far[a, side].astype(SINGLE)
            part[a, 0, j, bands[side]] = total.astype(LOW)
            send_near(a, side, side)

    def reduce_beside(a):
        for k in (1, 0):
            send_part(
                part.at[a, 1, 2 + k], aside.at[a, k], rs_send.at[a, 6 + k], aside_recv.at[a, k], beside
            )

    def aside_total(a, k):
        await_bytes(aside.at[a, k], aside_recv.at[a, k])
        return part[a, 1, k].astype(SINGLE) + aside[a, k].astype(SINGLE)

    def reduce_over(a):
        part[a, 1, 1] = aside_total(a, 1).astype(LOW)
        send_part(part.at[a, 1, 1], over.at[a], rs_send.at[a, 8], over_recv.at[a], partner)

    def give_back(a):
        first = part[a, 0, 0].astype(SINGLE)
        for side in range(2):
            for band in range(2):
                await_bytes(near.at[a, side, bands[band]], near_recv.at[a, side, band])
            first = first + near[a, side].astype(SINGLE)
        second = aside_total(a, 0)
        await_bytes(over.at[a], over_recv.at[a])
        second = second + over[a].astype(SINGLE)
        total = jnp.concatenate([first.astype(LOW), second.astype(LOW)], axis=0)
        ready[a] = pack(total, by_expert)
        collect(lambda block: ready.at[a, block], back.at[a], 2 + a)
        back[a, ex] = ready[a, lane]

    def given(a):
        received(back.at[a], 2 + a)
        return jnp.concatenate(unpack(back[a], by_image, pairs), axis=1)

    stores = []

    def store(src, dst, k):
        copy = pltpu.make_async_copy(src, dst, local.at[k])
        copy.start()
        stores.append(copy)

    def flat(value):
        return value.reshape(value.shape[0] * value.shape[1], value.shape[2])

    def weights(e):
        give_out[e] = outer(flat(act[e, 1]), flat(rows[1, e])).astype(LOW)
        give_in[e] = outer(flat(rows[0, e]), flat(pre_grad[e, 1])).astype(LOW)
        w_out_grad[e] = outer(flat(act[e, 0]), flat(rows[1, e]))
        w_in_grad[e] = outer(flat(rows[0, e]), flat(pre_grad[e, 0]))

    def weights_given(e):
        swap(e, 2, give_out.at[e], took_out.at[e])
        swap(e, 3, give_in.at[e], took_in.at[e])

    def weights_taken(e):
        await_bytes(took_out.at[e], swap_recv.at[e, 2])
        w_out_grad[e] = w_out_grad[e] + took_out[e].astype(SINGLE)
        store(w_out_grad.at[e], w_out_grad_hbm.at[e], 4 + e)
        await_bytes(took_in.at[e], swap_recv.at[e, 3])
        w_in_grad[e] = w_in_grad[e] + took_in[e].astype(SINGLE)
        store(w_in_grad.at[e], w_in_grad_hbm.at[e], 6 + e)

    def weights_here(e):
        await_bytes(mate_in.at[e], swap_recv.at[e, 0])
        await_bytes(mate_out.at[e], swap_recv.at[e, 1])

    own_rows(0)
    gather_own(0)
    deliver(message.at[1], got.at[1], 1)
    swap(0, 1, w_out.at[0], mate_out.at[0])
    gather_mate(0)
    weights_here(1)
    forward(1, 0)
    gather_far(0)
    forward(1, 1)
    own_rows(1)
    gather_own(1)
    for j in (2, 3):
        arrived(0, 1, j)
    several(forward, 1, 2, 4)
    gather_mate(1)
    gather_far(1)
    reduce_beside(0)
    weights_here(0)
    far_rest(0)
    several(forward, 0, 0, 4)
    reduce_far(0)
    near_free(0)
    reduce_over(0)
    several(backward, 1, 0, 2)
    for j in (2, 3):
        arrived(1, 1, j)
    several(backward, 1, 2, 4)
    reduce_beside(1)
    near_summed(0)
    far_rest(1)
    several(backward, 0, 0, 4)
    reduce_far(1)
    near_free(1)
    reduce_over(1)
    give_back(0)
    near_summed(1)
    weights(1)
    weights_given(1)
    give_back(1)
    weights(0)
    weights_given(0)

    slot_out = given(0)
    value = outer(combine_low[...], slot_out)[:n_tokens].astype(LOW)
    raw[0] = value.reshape(raw.shape[1:])
    store(raw.at[0], mixed_hbm, 8)
    grad = together(turn(slot_out, held[1]))
    weight = combine[...]
    combine_term[...] = weight * (grad - jnp.sum(weight * grad, axis=0, keepdims=True))

    input_slots = given(1)
    grad = together(turn(input_slots, held[0]))
    weight = dispatch[...]
    grad = weight * (grad - per_image(jnp.sum, weight * grad, 0.0)) + combine_term[...]
    grad = jnp.where(image_of >= 0, grad, 0.0).astype(LOW)
    total = dot(grad, held[0]).astype(LOW)
    away = distance((experts * CHUNK, slots), 0, by_slot)
    block = sum(
        dot(mark(away, c), total[:, c * LANES : (c + 1) * LANES]) for c in range(chunks)
    )
    router_message[...] = block.astype(LOW).reshape(experts, CHUNK, LANES)
    deliver(router_message, router_first, 5)
    value = outer(dispatch_low[...], input_slots) + outer(grad, router[...])
    raw[1] = value[:n_tokens].astype(LOW).reshape(raw.shape[1:])
    store(raw.at[1], tokens_grad_hbm, 9)

    received(router_first, 5)
    router_mine[...] = jnp.sum(router_first[...].astype(SINGLE), axis=0)

    def share(k, carry):
        pltpu.make_async_remote_copy(
            src_ref=router_mine,
            dst_ref=router_second.at[dp],
            send_sem=a2a_send.at[6],
            recv_sem=a2a_recv.at[6],
            device_id=(lax.rem(dp + k, shards), ex),
            device_id_type=MESH,
        ).start()
        return carry

    lax.fori_loop(1, shards, share, 0)
    router_second[dp] = router_mine[...]
    await_bytes(router_second.at[pl.ds(0, shards - 1)], a2a_recv.at[6])
    router_total[...] = jnp.sum(router_second[...], axis=0)

    for e in (1, 0):
        weights_taken(e)
    for k in range(4):
        await_bytes(got.at[0, pl.ds(0, experts - 1)], a2a_send.at[k])
    for k in range(4, 6):
        await_bytes(router_got.at[pl.ds(0, experts - 1)], a2a_send.at[k])
    await_bytes(router_second.at[pl.ds(0, shards - 1)], a2a_send.at[6])
    for copy in sent:
        copy.wait_send()
    for copy in stores:
        copy.wait()


def body(experts, tokens, router, w_in, w_out, cotangent):
    images, n, d = tokens.shape
    hidden = w_in.shape[2]
    owned = router.shape[1]
    slots = experts * owned
    n_tokens = images * n
    n_padded = -(-n_tokens // LANES) * LANES
    n_rows = experts * images
    used = d * owned // LANES
    half = d // 2

    def swap(value):
        return value.transpose(1, 0, 2)

    def low(*shape):
        return pltpu.VMEM(shape, LOW)

    def single(*shape):
        return pltpu.VMEM(shape, SINGLE)

    router_own = jnp.pad(router.T.reshape(used, LANES), ((0, CHUNK - used), (0, 0)))
    anywhere = pl.BlockSpec(memory_space=pl.ANY)
    vmem = pl.BlockSpec(memory_space=pltpu.VMEM)
    dma = pltpu.SemaphoreType.DMA
    mixed, tokens_grad, w_in_grad, w_out_grad, router_total = pl.pallas_call(
        functools.partial(layer_kernel, experts, images),
        out_shape=[
            jax.ShapeDtypeStruct((n, images, d), LOW),
            jax.ShapeDtypeStruct((n, images, d), LOW),
            jax.ShapeDtypeStruct(w_in.shape, SINGLE),
            jax.ShapeDtypeStruct(w_out.shape, SINGLE),
            jax.ShapeDtypeStruct((CHUNK, LANES), SINGLE),
        ],
        in_specs=[anywhere, anywhere, vmem, anywhere, anywhere],
        out_specs=[anywhere] * 4 + [vmem],
        scratch_shapes=[
            low(2, n, images, d),
            low(2, n_padded, d),
            low(*w_in.shape),
            low(*w_out.shape),
            low(*w_in.shape),
            low(*w_out.shape),
            low(*w_in.shape),
            low(*w_out.shape),
            low(*w_in.shape),
            low(*w_out.shape),
            low(experts, CHUNK, LANES),
            low(slots, d),
            single(slots, n_padded),
            single(slots, n_padded),
            low(images * slots, n_padded),
            low(images * slots, n_padded),
            low(2, experts, 4 * images, half),
            low(2, experts, 4 * images, half),
            low(2, 2, RING, n_rows, d),
            low(2, 2, RING, n_rows, d),
            low(2, 2, RING, n_rows, hidden),
            single(2, 2, RING, n_rows, hidden),
            low(2, 2, RING, n_rows, hidden),
            low(2, 2, n_rows // 2, d),
            low(2, 2, n_rows, d),
            low(2, 2, n_rows, d),
            low(2, n_rows, d),
            low(2, experts, 4 * images, half),
            low(2, experts, 4 * images, half),
            single(slots, n_padded),
            single(*w_in.shape),
            single(*w_out.shape),
            low(experts, CHUNK, LANES),
            low(experts, CHUNK, LANES),
            single(CHUNK, LANES),
            single(2 * RING, CHUNK, LANES),
            dma((10,)),
            dma((7,)),
            dma((7,)),
            dma((2, 4)),
            dma((2, 4)),
            dma((2, 7)),
            dma((2, 2, RING)),
            dma((2, 2)),
            dma((2, 9)),
            dma((2, 2)),
            dma((2, 2, 2)),
            dma((2, 2)),
            dma((2,)),
        ],
        compiler_params=pltpu.CompilerParams(
            collective_id=0, has_side_effects=True, vmem_limit_bytes=58 * 1024 * 1024
        ),
        name="layer",
    )(swap(tokens), swap(cotangent), router_own, w_in, w_out)
    router_grad = router_total[:used].reshape(owned, d).T
    return (swap(mixed), swap(tokens_grad), w_in_grad, w_out_grad, router_grad)


def solution(mesh):
    placed = (
        P(("dp", "expert"), None, None),
        P(None, "expert"),
        P("expert", None, "dp"),
        P("expert", "dp", None),
        P(("dp", "expert"), None, None),
    )
    return jax.shard_map(
        functools.partial(body, mesh.shape["expert"]),
        mesh=mesh,
        in_specs=placed,
        out_specs=(
            P(("dp", "expert"), None, None),
            P(("dp", "expert"), None, None),
            P("expert", None, "dp"),
            P("expert", "dp", None),
            P(None, "expert"),
        ),
        check_vma=False,
    )
```

```python
import functools

import jax
import jax.numpy as jnp
from jax import lax
from jax.experimental import pallas as pl
from jax.experimental.pallas import tpu as pltpu
from jax.sharding import PartitionSpec as P

SINGLE = jnp.float32
LOW = jnp.bfloat16
MESH = pl.DeviceIdType.MESH
RING = 4
Z_HIGH = 4
LANES = 128
VMEM_BYTES = 58 * 1024 * 1024
PARTS = 4
CHUNK = 16


def remote(src, dst, send, recv, device):
    copy = pltpu.make_async_remote_copy(
        src_ref=src, dst_ref=dst, send_sem=send, recv_sem=recv, device_id=device, device_id_type=MESH
    )
    copy.start()
    return copy


def await_bytes(ref, sem):
    pltpu.make_async_copy(ref, ref, sem).wait()


def gelu_and_slope(v):
    c = 0.7978845608028654
    square = v * v
    t = jnp.tanh(c * v * (1.0 + 0.044715 * square))
    half = 0.5 * (1.0 + t)
    slope = half + 0.5 * v * (1.0 - t * t) * (c * (1.0 + 3.0 * 0.044715 * square))
    return v * half, slope


def turn(lhs, rhs):
    return lax.dot_general(lhs, rhs, (((1,), (1,)), ((), ())), preferred_element_type=SINGLE)


def outer(lhs, rhs):
    return lax.dot_general(lhs, rhs, (((0,), (0,)), ((), ())), preferred_element_type=SINGLE)


def dot(lhs, rhs):
    return jnp.dot(lhs, rhs, preferred_element_type=SINGLE)


def place_of(z_at, lane, x, experts):
    z_at = lax.rem(z_at + 4 * Z_HIGH, 2 * Z_HIGH)
    return (lax.rem(z_at, 2) * RING + x, (z_at // 2) * (experts // Z_HIGH) + lane)


def layer_kernel(
    experts,
    images,
    tokens_hbm,
    cotangent_hbm,
    router_columns,
    w_in_hbm,
    w_out_hbm,
    mixed_hbm,
    tokens_grad_hbm,
    w_in_grad_hbm,
    w_out_grad_hbm,
    router_grad,
    raw,
    held,
    w_in,
    w_out,
    mate_in,
    mate_out,
    give_in,
    give_out,
    took_in,
    took_out,
    router_own,
    router_got,
    router,
    dispatch,
    combine,
    dispatch_low,
    combine_low,
    message,
    got,
    rows,
    part,
    act,
    slope,
    pre_grad,
    far,
    near,
    cross,
    aside,
    over,
    ready,
    back,
    combine_term,
    w_in_grad,
    w_out_grad,
    router_message,
    router_first,
    router_mine,
    router_second,
    local,
    a2a_send,
    a2a_recv,
    swap_send,
    swap_recv,
    ag_send,
    ag_recv,
    ag_far,
    rs_send,
    far_recv,
    near_recv,
    cross_recv,
    aside_recv,
    over_recv,
):
    dp, ex = lax.axis_index("dp"), lax.axis_index("expert")
    shards = 2 * RING
    x, z = lax.rem(dp, RING), dp // RING
    odd = lax.rem(x, 2)
    partner = ((1 - z) * RING + x, ex)
    right = (z * RING + lax.rem(x + 1, RING), ex)
    left = (z * RING + lax.rem(x + 3, RING), ex)
    across = (z * RING + lax.rem(x + 1 + 2 * odd, RING), ex)
    beside = (z * RING + lax.rem(x + 3 + 2 * odd, RING), ex)
    n_rows = experts * images
    half = rows.shape[-1] // 2
    slots = 2 * experts
    pairs = images * slots
    n_tokens, n_padded = tokens_hbm.shape[0] * images, held.shape[1]
    chunks = rows.shape[-1] // LANES
    inner = experts // Z_HIGH
    lane = lax.rem(ex, inner)
    z_at = (ex // inner) * 2 + z
    way = 1 - 2 * z

    loads = [
        pltpu.make_async_copy(src, dst, local.at[k])
        for k, (src, dst) in enumerate(
            (
                (tokens_hbm, raw.at[0]),
                (cotangent_hbm, raw.at[1]),
                (w_in_hbm, w_in),
                (w_out_hbm, w_out),
            )
        )
    ]
    for load in loads:
        load.start()
    owned = router_columns.shape[0]
    value = router_columns[...].astype(SINGLE)
    lines = [value[s : s + 1, c * LANES : (c + 1) * LANES] for s in range(owned) for c in range(chunks)]
    lines.append(jnp.zeros((CHUNK - owned * chunks, LANES), SINGLE))
    router_own[...] = jnp.concatenate(lines, axis=0).astype(LOW)

    barrier = pltpu.get_barrier_semaphore()

    def greet_experts(k, carry):
        step = k // inner
        step = step - (step // Z_HIGH) * (Z_HIGH + 2)
        to = place_of(z_at - step * way, lax.rem(lane + k, inner), x, experts)
        pl.semaphore_signal(barrier, inc=1, device_id=to, device_id_type=MESH)
        return carry

    def greet_shards(k, carry):
        to = (lax.rem(dp + k, shards), ex)
        pl.semaphore_signal(barrier, inc=1, device_id=to, device_id_type=MESH)
        return carry

    greeted = (Z_HIGH + 1) * inner
    lax.fori_loop(1, greeted, greet_experts, 0)
    lax.fori_loop(1, shards, greet_shards, 0)

    def hold(k):
        loads[k].wait()
        held[k, :n_tokens] = raw[k].reshape(n_tokens, held.shape[2])
        if n_padded > n_tokens:
            held[k, n_tokens:] = jnp.zeros((n_padded - n_tokens, held.shape[2]), LOW)

    hold(0)
    pl.semaphore_wait(barrier, greeted - 1 + shards - 1)

    for load in loads[2:]:
        load.wait()
    swap_with = (partner, across)

    def swap(e, k, src, dst):
        sent.append(remote(src, dst, swap_send.at[e, k], swap_recv.at[e, k], swap_with[e]))

    sent = []
    swap(1, 0, w_in.at[1], mate_in.at[1])
    swap(0, 0, w_in.at[0], mate_in.at[0])
    swap(1, 1, w_out.at[1], mate_out.at[1])

    def deliver(src, dst, k):
        def one(i, carry):
            step = i // inner
            to = place_of(
                z_at + step * way * (1 - 2 * lax.rem(step, 2)), lax.rem(lane + i, inner), x, experts
            )
            pltpu.make_async_remote_copy(
                src_ref=src.at[to[1]],
                dst_ref=dst.at[step * inner + lane],
                send_sem=a2a_send.at[k],
                recv_sem=a2a_recv.at[k],
                device_id=to,
                device_id_type=MESH,
            ).start()
            return carry

        lax.fori_loop(1, experts, one, 0)
        dst[lane] = src[ex]

    def collect(src_of, dst, k):
        def one(i, carry):
            step = i // inner
            there = lax.rem(lane + i, inner)
            pltpu.make_async_remote_copy(
                src_ref=src_of(step * inner + there),
                dst_ref=dst.at[ex],
                send_sem=a2a_send.at[k],
                recv_sem=a2a_recv.at[k],
                device_id=place_of(z_at - step * way, there, x, experts),
                device_id_type=MESH,
            ).start()
            return carry

        lax.fori_loop(1, experts, one, 0)

    def received(ref, k):
        await_bytes(ref.at[pl.ds(0, experts - 1)], a2a_recv.at[k])

    def iota(shape, axis):
        return lax.broadcasted_iota(jnp.int32, shape, axis)

    def bits(n):
        return n.bit_length() - 1

    def by_expert(row):
        slot = (row >= n_rows).astype(jnp.int32)
        row = row - slot * n_rows
        image = lax.bitwise_and(row, images - 1)
        return lax.shift_right_logical(row, bits(images)) * 4 * images + slot * images + image

    def by_image(row):
        slot = lax.bitwise_and(row, slots - 1)
        image = lax.shift_right_logical(row, bits(slots))
        odd = lax.bitwise_and(slot, 1)
        return lax.shift_right_logical(slot, 1) * 4 * images + odd * images + image

    def by_slot(row):
        odd = lax.bitwise_and(row, 1)
        return lax.shift_right_logical(row, 1) * CHUNK + odd * chunks

    def distance(shape, axis, order):
        return iota(shape, axis) - order(iota(shape, 1 - axis))

    def mark(distances, at):
        return (distances == at).astype(SINGLE).astype(LOW)

    def pack(value, order):
        n = value.shape[0]
        away = distance((experts * 4 * images, n), 0, order)
        block = sum(
            dot(mark(away, h * 2 * images), value[:, h * half : (h + 1) * half]) for h in range(2)
        )
        return block.astype(LOW).reshape(experts, 4 * images, half)

    def unpack(value, order, n):
        flat = value.reshape(experts * 4 * images, half)
        away = distance((n, experts * 4 * images), 1, order)
        return [dot(mark(away, h * 2 * images), flat).astype(LOW) for h in range(2)]

    collect(lambda block: router_own, router_got, 4)
    router_got[ex] = router_own[...]
    received(router_got, 4)
    flat = router_got[...].reshape(experts * CHUNK, LANES)
    away = distance((slots, experts * CHUNK), 1, by_slot)
    for c in range(chunks):
        router[:, c * LANES : (c + 1) * LANES] = dot(mark(away, c), flat).astype(LOW)

    column = iota((slots, n_padded), 1)
    image_of = jnp.where(column < n_tokens, lax.bitwise_and(column, images - 1), -1)

    def per_image(reduce, value, fill):
        spread = jnp.zeros_like(value)
        for i in range(images):
            mine = image_of == i
            total = reduce(jnp.where(mine, value, fill), axis=1, keepdims=True)
            spread = jnp.where(mine, total, spread)
        return spread

    def apart(value, low):
        for i in range(images):
            low[i * slots : (i + 1) * slots] = jnp.where(image_of == i, value, 0.0).astype(LOW)

    def together(value):
        total = jnp.zeros((slots, n_padded), SINGLE)
        for i in range(images):
            total = jnp.where(image_of == i, value[i * slots : (i + 1) * slots], total)
        return total

    logits = turn(router[...], held[0])
    weight = jnp.exp(logits - per_image(jnp.max, logits, -jnp.inf))
    weight = jnp.where(image_of >= 0, weight, 0.0)
    weight = weight / jnp.where(image_of >= 0, per_image(jnp.sum, weight, 0.0), 1.0)
    dispatch[...] = weight
    apart(weight, dispatch_low)
    message[0] = pack(dot(dispatch_low[...], held[0]).astype(LOW), by_image)
    deliver(message.at[0], got.at[0], 0)
    hold(1)
    weight = jnp.exp(logits - jnp.max(logits, axis=0, keepdims=True))
    weight = weight / jnp.sum(weight, axis=0, keepdims=True)
    combine[...] = weight
    apart(weight, combine_low)
    message[1] = pack(dot(combine_low[...], held[1]).astype(LOW), by_image)

    def own_rows(a):
        received(got.at[a], a)
        for h, block in enumerate(unpack(got[a], by_expert, 2 * n_rows)):
            for e in range(2):
                rows[a, e, 0, :, h * half : (h + 1) * half] = block[e * n_rows : (e + 1) * n_rows]

    bands = (pl.ds(0, n_rows // 2), pl.ds(n_rows // 2, n_rows // 2))
    onward = (right, left)

    def send_block(a, e, src, dst, to, slot):
        sent.append(
            remote(rows.at[a, e, src], rows.at[a, e, dst], ag_send.at[a, slot], ag_recv.at[a, e, dst], to)
        )

    def arrived(a, e, j):
        await_bytes(rows.at[a, e, j], ag_recv.at[a, e, j])

    def gather_own(a):
        send_block(a, 1, 0, 1, partner, 0)
        send_block(a, 0, 0, 3, right, 1)
        send_block(a, 0, 0, 1, left, 2)
        send_block(a, 1, 0, 2, beside, 3)

    def gather_mate(a):
        arrived(a, 1, 1)
        send_block(a, 1, 1, 3, beside, 4)

    def gather_far(a):
        for side, j in enumerate((3, 1)):
            arrived(a, 0, j)
            sent.append(
                remote(
                    rows.at[a, 0, j, bands[side]],
                    rows.at[a, 0, 2, bands[side]],
                    ag_send.at[a, 5 + side],
                    ag_far.at[a, side],
                    onward[side],
                )
            )

    def far_rest(a):
        for side in range(2):
            await_bytes(rows.at[a, 0, 2, bands[side]], ag_far.at[a, side])

    def hidden(e):
        return ((w_in.at[e], w_out.at[e]), (mate_in.at[e], mate_out.at[e]))

    def forward(e, j):
        total = 0.0
        for h, (first, second) in enumerate(hidden(e)):
            value, grade = gelu_and_slope(dot(rows[0, e, j], first[...]))
            value = value.astype(LOW)
            act[e, h, j] = value
            slope[e, h, j] = grade
            total = total + dot(value, second[...])
        part[0, e, j] = total.astype(LOW)

    def backward(e, j):
        total = 0.0
        for h, (first, second) in enumerate(hidden(e)):
            grad = turn(rows[1, e, j], second[...])
            grad = (grad * slope[e, h, j]).astype(LOW)
            pre_grad[e, h, j] = grad
            total = total + turn(grad, first[...])
        part[1, e, j] = total.astype(LOW)

    def several(step, e, start, stop):
        def one(j, carry):
            step(e, j)
            return carry

        lax.fori_loop(start, stop, one, 0)

    def send_part(src, dst, send, recv, to):
        sent.append(remote(src, dst, send, recv, to))

    def reduce_far(a):
        for side in range(2):
            send_part(
                part.at[a, 0, 2, bands[side]],
                far.at[a, side],
                rs_send.at[a, side],
                far_recv.at[a, side],
                onward[side],
            )

    def send_near(a, side, band):
        send_part(
            part.at[a, 0, (1, 3)[side], bands[band]],
            near.at[a, side, bands[band]],
            rs_send.at[a, 2 + 2 * side + band],
            near_recv.at[a, side, band],
            onward[side],
        )

    def near_free(a):
        for side in range(2):
            send_near(a, side, 1 - side)

    def near_summed(a):
        for side in range(2):
            j = (1, 3)[side]
            await_bytes(far.at[a, side], far_recv.at[a, side])
            total = part[a, 0, j, bands[side]].astype(SINGLE) + far[a, side].astype(SINGLE)
            part[a, 0, j, bands[side]] = total.astype(LOW)
            send_near(a, side, side)

    def reduce_cross(a):
        send_part(part.at[a, 1, 3], cross.at[a], rs_send.at[a, 6], cross_recv.at[a], partner)
        send_part(part.at[a, 1, 1], over.at[a], rs_send.at[a, 7], over_recv.at[a], partner)

    def reduce_beside(a):
        await_bytes(cross.at[a], cross_recv.at[a])
        total = part[a, 1, 2].astype(SINGLE) + cross[a].astype(SINGLE)
        part[a, 1, 2] = total.astype(LOW)
        send_part(part.at[a, 1, 2], aside.at[a], rs_send.at[a, 8], aside_recv.at[a], beside)

    def give_back(a):
        first = part[a, 0, 0].astype(SINGLE)
        for side in range(2):
            for band in range(2):
                await_bytes(near.at[a, side, bands[band]], near_recv.at[a, side, band])
            first = first + near[a, side].astype(SINGLE)
        await_bytes(aside.at[a], aside_recv.at[a])
        await_bytes(over.at[a], over_recv.at[a])
        second = part[a, 1, 0].astype(SINGLE) + aside[a].astype(SINGLE) + over[a].astype(SINGLE)
        total = jnp.concatenate([first.astype(LOW), second.astype(LOW)], axis=0)
        ready[a] = pack(total, by_expert)
        collect(lambda block: ready.at[a, block], back.at[a], 2 + a)
        back[a, ex] = ready[a, lane]

    def given(a):
        received(back.at[a], 2 + a)
        return jnp.concatenate(unpack(back[a], by_image, pairs), axis=1)

    stores = []

    def store(src, dst, k):
        copy = pltpu.make_async_copy(src, dst, local.at[k])
        copy.start()
        stores.append(copy)

    def flat(value):
        return value.reshape(value.shape[0] * value.shape[1], value.shape[2])

    def weights_out(e):
        give_out[e] = outer(flat(act[e, 1]), flat(rows[1, e])).astype(LOW)
        swap(e, 2, give_out.at[e], took_out.at[e])

    def weights_in(e):
        give_in[e] = outer(flat(rows[0, e]), flat(pre_grad[e, 1])).astype(LOW)
        swap(e, 3, give_in.at[e], took_in.at[e])

    def weights_own(e):
        w_out_grad[e] = outer(flat(act[e, 0]), flat(rows[1, e]))
        w_in_grad[e] = outer(flat(rows[0, e]), flat(pre_grad[e, 0]))

    def weights_taken(e):
        await_bytes(took_out.at[e], swap_recv.at[e, 2])
        w_out_grad[e] = w_out_grad[e] + took_out[e].astype(SINGLE)
        store(w_out_grad.at[e], w_out_grad_hbm.at[e], 4 + e)
        await_bytes(took_in.at[e], swap_recv.at[e, 3])
        w_in_grad[e] = w_in_grad[e] + took_in[e].astype(SINGLE)
        store(w_in_grad.at[e], w_in_grad_hbm.at[e], 6 + e)

    def weights_here(e):
        await_bytes(mate_in.at[e], swap_recv.at[e, 0])
        await_bytes(mate_out.at[e], swap_recv.at[e, 1])

    own_rows(0)
    gather_own(0)
    deliver(message.at[1], got.at[1], 1)
    swap(0, 1, w_out.at[0], mate_out.at[0])
    gather_mate(0)
    weights_here(1)
    forward(1, 0)
    gather_far(0)
    forward(1, 1)
    own_rows(1)
    gather_own(1)
    for j in (2, 3):
        arrived(0, 1, j)
    several(forward, 1, 2, 4)
    gather_mate(1)
    gather_far(1)
    reduce_cross(0)
    weights_here(0)
    far_rest(0)
    several(forward, 0, 0, 4)
    reduce_far(0)
    near_free(0)
    reduce_beside(0)
    several(backward, 1, 0, 2)
    for j in (2, 3):
        arrived(1, 1, j)
    several(backward, 1, 2, 4)
    reduce_cross(1)
    near_summed(0)
    far_rest(1)
    several(backward, 0, 0, 4)
    reduce_far(1)
    near_free(1)
    reduce_beside(1)
    near_summed(1)
    give_back(0)
    weights_out(0)
    give_back(1)
    weights_in(0)
    weights_out(1)
    weights_in(1)
    weights_own(0)
    weights_own(1)

    slot_out = given(0)
    value = outer(combine_low[...], slot_out)[:n_tokens].astype(LOW)
    raw[0] = value.reshape(raw.shape[1:])
    store(raw.at[0], mixed_hbm, 8)
    grad = together(turn(slot_out, held[1]))
    weight = combine[...]
    combine_term[...] = weight * (grad - jnp.sum(weight * grad, axis=0, keepdims=True))

    input_slots = given(1)
    grad = together(turn(input_slots, held[0]))
    weight = dispatch[...]
    grad = weight * (grad - per_image(jnp.sum, weight * grad, 0.0)) + combine_term[...]
    grad = jnp.where(image_of >= 0, grad, 0.0).astype(LOW)
    total = dot(grad, held[0]).astype(LOW)
    away = distance((experts * CHUNK, slots), 0, by_slot)
    block = sum(
        dot(mark(away, c), total[:, c * LANES : (c + 1) * LANES]) for c in range(chunks)
    )
    router_message[...] = block.astype(LOW).reshape(experts, CHUNK, LANES)
    deliver(router_message, router_first, 5)
    value = outer(dispatch_low[...], input_slots) + outer(grad, router[...])
    raw[1] = value[:n_tokens].astype(LOW).reshape(raw.shape[1:])
    store(raw.at[1], tokens_grad_hbm, 9)

    received(router_first, 5)
    router_mine[...] = jnp.sum(router_first[...].astype(SINGLE), axis=0)

    def share(k, carry):
        pltpu.make_async_remote_copy(
            src_ref=router_mine,
            dst_ref=router_second.at[dp],
            send_sem=a2a_send.at[6],
            recv_sem=a2a_recv.at[6],
            device_id=(lax.rem(dp + k, shards), ex),
            device_id_type=MESH,
        ).start()
        return carry

    lax.fori_loop(1, shards, share, 0)
    router_second[dp] = router_mine[...]
    await_bytes(router_second.at[pl.ds(0, shards - 1)], a2a_recv.at[6])
    value = jnp.sum(router_second[...], axis=0)
    for s in range(owned):
        for c in range(chunks):
            at = s * chunks + c
            router_grad[s : s + 1, c * LANES : (c + 1) * LANES] = value[at : at + 1]

    for e in (1, 0):
        weights_taken(e)
    for k in range(4):
        await_bytes(got.at[0, pl.ds(0, experts - 1)], a2a_send.at[k])
    for k in range(4, 6):
        await_bytes(router_got.at[pl.ds(0, experts - 1)], a2a_send.at[k])
    await_bytes(router_second.at[pl.ds(0, shards - 1)], a2a_send.at[6])
    for copy in sent:
        copy.wait_send()
    for copy in stores:
        copy.wait()


def finish_kernel(*refs):
    count = (len(refs) - 2) // 3
    sources, results, staged = (refs[k * count : (k + 1) * count] for k in range(3))
    into, out = refs[-2:]
    pieces = []
    for src, dst, held in zip(sources, results, staged):
        parts = 1 if len(src.shape) < 3 else PARTS if src.shape[0] % PARTS == 0 else src.shape[0]
        size = src.shape[0] // parts
        for at in range(parts):
            rows, k = pl.ds(at * size, size), len(pieces)
            pieces.append(
                (
                    pltpu.make_async_copy(src.at[rows], held.at[rows], into.at[k]),
                    pltpu.make_async_copy(held.at[rows], dst.at[rows], out.at[k]),
                )
            )
    for read, _ in pieces:
        read.start()
    for read, write in pieces:
        read.wait()
        write.start()
    for _, write in pieces:
        write.wait()


def finish(*values):
    anywhere = pl.BlockSpec(memory_space=pl.ANY)
    return pl.pallas_call(
        finish_kernel,
        out_shape=[jax.ShapeDtypeStruct(value.shape, value.dtype) for value in values],
        in_specs=[anywhere] * len(values),
        out_specs=[anywhere] * len(values),
        scratch_shapes=[pltpu.VMEM(value.shape, value.dtype) for value in values]
        + [pltpu.SemaphoreType.DMA((PARTS * len(values),))] * 2,
        compiler_params=pltpu.CompilerParams(vmem_limit_bytes=VMEM_BYTES),
        name="finish",
    )(*values)


def body(experts, tokens, router, w_in, w_out, cotangent):
    images, n, d = tokens.shape
    hidden = w_in.shape[2]
    owned = router.shape[1]
    slots = experts * owned
    n_tokens = images * n
    n_padded = -(-n_tokens // LANES) * LANES
    n_rows = experts * images
    half = d // 2

    def swap(value):
        return value.transpose(1, 0, 2)

    def low(*shape):
        return pltpu.VMEM(shape, LOW)

    def single(*shape):
        return pltpu.VMEM(shape, SINGLE)

    anywhere = pl.BlockSpec(memory_space=pl.ANY)
    in_hbm = pl.BlockSpec(memory_space=pltpu.HBM)
    vmem = pl.BlockSpec(memory_space=pltpu.VMEM)
    dma = pltpu.SemaphoreType.DMA
    mixed, tokens_grad, w_in_grad, w_out_grad, router_grad = pl.pallas_call(
        functools.partial(layer_kernel, experts, images),
        out_shape=[
            jax.ShapeDtypeStruct((n, images, d), LOW),
            jax.ShapeDtypeStruct((n, images, d), LOW),
            jax.ShapeDtypeStruct(w_in.shape, SINGLE),
            jax.ShapeDtypeStruct(w_out.shape, SINGLE),
            jax.ShapeDtypeStruct((owned, d), SINGLE),
        ],
        in_specs=[in_hbm, in_hbm, vmem, in_hbm, in_hbm],
        out_specs=[anywhere] * 4 + [vmem],
        scratch_shapes=[
            low(2, n, images, d),
            low(2, n_padded, d),
            low(*w_in.shape),
            low(*w_out.shape),
            low(*w_in.shape),
            low(*w_out.shape),
            low(*w_in.shape),
            low(*w_out.shape),
            low(*w_in.shape),
            low(*w_out.shape),
            low(CHUNK, LANES),
            low(experts, CHUNK, LANES),
            low(slots, d),
            single(slots, n_padded),
            single(slots, n_padded),
            low(images * slots, n_padded),
            low(images * slots, n_padded),
            low(2, experts, 4 * images, half),
            low(2, experts, 4 * images, half),
            low(2, 2, RING, n_rows, d),
            low(2, 2, RING, n_rows, d),
            low(2, 2, RING, n_rows, hidden),
            single(2, 2, RING, n_rows, hidden),
            low(2, 2, RING, n_rows, hidden),
            low(2, 2, n_rows // 2, d),
            low(2, 2, n_rows, d),
            low(2, n_rows, d),
            low(2, n_rows, d),
            low(2, n_rows, d),
            low(2, experts, 4 * images, half),
            low(2, experts, 4 * images, half),
            single(slots, n_padded),
            single(*w_in.shape),
            single(*w_out.shape),
            low(experts, CHUNK, LANES),
            low(experts, CHUNK, LANES),
            single(CHUNK, LANES),
            single(2 * RING, CHUNK, LANES),
            dma((10,)),
            dma((7,)),
            dma((7,)),
            dma((2, 4)),
            dma((2, 4)),
            dma((2, 7)),
            dma((2, 2, RING)),
            dma((2, 2)),
            dma((2, 9)),
            dma((2, 2)),
            dma((2, 2, 2)),
            dma((2,)),
            dma((2,)),
            dma((2,)),
        ],
        compiler_params=pltpu.CompilerParams(
            collective_id=0, has_side_effects=True, vmem_limit_bytes=VMEM_BYTES
        ),
        name="layer",
    )(swap(tokens), swap(cotangent), router.T, w_in, w_out)
    mixed, tokens_grad, w_in_grad, w_out_grad, router_grad = finish(
        mixed, tokens_grad, w_in_grad, w_out_grad, router_grad
    )
    return (swap(mixed), swap(tokens_grad), w_in_grad, w_out_grad, router_grad.T)


def solution(mesh):
    placed = (
        P(("dp", "expert"), None, None),
        P(None, "expert"),
        P("expert", None, "dp"),
        P("expert", "dp", None),
        P(("dp", "expert"), None, None),
    )
    return jax.shard_map(
        functools.partial(body, mesh.shape["expert"]),
        mesh=mesh,
        in_specs=placed,
        out_specs=(
            P(("dp", "expert"), None, None),
            P(("dp", "expert"), None, None),
            P("expert", None, "dp"),
            P("expert", "dp", None),
            P(None, "expert"),
        ),
        check_vma=False,
    )
```

```python
import functools

import jax
import jax.numpy as jnp
from jax import lax
from jax.experimental import pallas as pl
from jax.experimental.pallas import tpu as pltpu
from jax.sharding import PartitionSpec as P

SINGLE = jnp.float32
LOW = jnp.bfloat16
MESH = pl.DeviceIdType.MESH
RING = 4
Z_HIGH = 4
LANES = 128
VMEM_BYTES = 58 * 1024 * 1024
PARTS = 4
CHUNK = 16


def remote(src, dst, send, recv, device):
    copy = pltpu.make_async_remote_copy(
        src_ref=src, dst_ref=dst, send_sem=send, recv_sem=recv, device_id=device, device_id_type=MESH
    )
    copy.start()
    return copy


def await_bytes(ref, sem):
    pltpu.make_async_copy(ref, ref, sem).wait()


def gelu_and_slope(v):
    c = 0.7978845608028654
    square = v * v
    t = jnp.tanh(c * v * (1.0 + 0.044715 * square))
    half = 0.5 * (1.0 + t)
    slope = half + 0.5 * v * (1.0 - t * t) * (c * (1.0 + 3.0 * 0.044715 * square))
    return v * half, slope


def turn(lhs, rhs):
    return lax.dot_general(lhs, rhs, (((1,), (1,)), ((), ())), preferred_element_type=SINGLE)


def outer(lhs, rhs):
    return lax.dot_general(lhs, rhs, (((0,), (0,)), ((), ())), preferred_element_type=SINGLE)


def dot(lhs, rhs):
    return jnp.dot(lhs, rhs, preferred_element_type=SINGLE)


def layer_kernel(
    experts,
    images,
    tokens_hbm,
    cotangent_hbm,
    router_columns,
    w_in_hbm,
    w_out_hbm,
    mixed_hbm,
    tokens_grad_hbm,
    w_in_grad_hbm,
    w_out_grad_hbm,
    router_grad,
    raw,
    held,
    w_in,
    w_out,
    mate_in,
    mate_out,
    give_in,
    give_out,
    took_in,
    took_out,
    router_own,
    router_got,
    router,
    dispatch,
    combine,
    dispatch_low,
    combine_low,
    message,
    got,
    rows,
    part,
    act,
    slope,
    pre_grad,
    far,
    near,
    cross,
    aside,
    over,
    ready,
    back,
    combine_term,
    w_in_grad,
    w_out_grad,
    router_message,
    router_first,
    router_mine,
    router_second,
    local,
    a2a_send,
    a2a_recv,
    swap_send,
    swap_recv,
    ag_send,
    ag_recv,
    ag_far,
    rs_send,
    far_recv,
    near_recv,
    cross_recv,
    aside_recv,
    over_recv,
):
    dp, ex = lax.axis_index("dp"), lax.axis_index("expert")
    shards = 2 * RING
    x, z = lax.rem(dp, RING), dp // RING
    odd = lax.rem(x, 2)
    partner = ((1 - z) * RING + x, ex)
    right = (z * RING + lax.rem(x + 1, RING), ex)
    left = (z * RING + lax.rem(x + 3, RING), ex)
    across = (z * RING + lax.rem(x + 1 + 2 * odd, RING), ex)
    beside = (z * RING + lax.rem(x + 3 + 2 * odd, RING), ex)
    n_rows = experts * images
    half = rows.shape[-1] // 2
    slots = 2 * experts
    pairs = images * slots
    n_tokens, n_padded = tokens_hbm.shape[0] * images, held.shape[1]
    chunks = rows.shape[-1] // LANES
    inner = experts // Z_HIGH
    lane = lax.rem(ex, inner)
    z_at = (ex // inner) * 2 + z
    way = 1 - 2 * z

    loads = [
        pltpu.make_async_copy(src, dst, local.at[k])
        for k, (src, dst) in enumerate(
            (
                (tokens_hbm, raw.at[0]),
                (cotangent_hbm, raw.at[1]),
                (w_in_hbm, w_in),
                (w_out_hbm, w_out),
            )
        )
    ]
    for load in loads:
        load.start()
    owned = router_columns.shape[0]
    value = router_columns[...].astype(SINGLE)
    lines = [value[s : s + 1, c * LANES : (c + 1) * LANES] for s in range(owned) for c in range(chunks)]
    lines.append(jnp.zeros((CHUNK - owned * chunks, LANES), SINGLE))
    router_own[...] = jnp.concatenate(lines, axis=0).astype(LOW)

    barrier = pltpu.get_barrier_semaphore()

    def each_lane(step, what):
        def one(i, carry):
            what(lax.rem(lane + i, inner))
            return carry

        lax.fori_loop(0 if step else 1, inner, one, 0, unroll=True)

    def at_z(offset):
        z_to = lax.rem(z_at + offset + 4 * Z_HIGH, 2 * Z_HIGH)
        return lax.rem(z_to, 2) * RING + x, (z_to // 2) * inner

    def greet_experts(step, offset):
        dp_to, first = at_z(offset)

        def one(there):
            to = (dp_to, first + there)
            pl.semaphore_signal(barrier, inc=1, device_id=to, device_id_type=MESH)

        each_lane(step, one)

    def greet_shards(k, carry):
        to = (lax.rem(dp + k, shards), ex)
        pl.semaphore_signal(barrier, inc=1, device_id=to, device_id_type=MESH)
        return carry

    greeted = (Z_HIGH + 1) * inner
    for step, offset in enumerate((0, -way, -2 * way, -3 * way, 2 * way)):
        greet_experts(step, offset)
    lax.fori_loop(1, shards, greet_shards, 0, unroll=True)

    def hold(k):
        loads[k].wait()
        held[k, :n_tokens] = raw[k].reshape(n_tokens, held.shape[2])
        if n_padded > n_tokens:
            held[k, n_tokens:] = jnp.zeros((n_padded - n_tokens, held.shape[2]), LOW)

    hold(0)
    pl.semaphore_wait(barrier, greeted - 1 + shards - 1)

    for load in loads[2:]:
        load.wait()
    swap_with = (partner, across)
    some = w_out.shape[1] // 2
    early, late = pl.ds(0, some), pl.ds(some, some)

    def swap(e, k, src, dst):
        sent.append(remote(src, dst, swap_send.at[e, k], swap_recv.at[e, k], swap_with[e]))

    sent = []
    swap(1, 0, w_in.at[1], mate_in.at[1])
    swap(0, 0, w_in.at[0], mate_in.at[0])
    swap(1, 1, w_out.at[1], mate_out.at[1])

    def deliver(src, dst, k):
        for step in range(Z_HIGH):
            dp_to, first = at_z(step * way * (1 - 2 * (step % 2)))

            def one(there, step=step, dp_to=dp_to, first=first):
                pltpu.make_async_remote_copy(
                    src_ref=src.at[first + there],
                    dst_ref=dst.at[step * inner + lane],
                    send_sem=a2a_send.at[k],
                    recv_sem=a2a_recv.at[k],
                    device_id=(dp_to, first + there),
                    device_id_type=MESH,
                ).start()

            each_lane(step, one)
        dst[lane] = src[ex]

    def collect(src_of, dst, k):
        for step in range(Z_HIGH):
            dp_to, first = at_z(-step * way)

            def one(there, step=step, dp_to=dp_to, first=first):
                pltpu.make_async_remote_copy(
                    src_ref=src_of(step * inner + there),
                    dst_ref=dst.at[ex],
                    send_sem=a2a_send.at[k],
                    recv_sem=a2a_recv.at[k],
                    device_id=(dp_to, first + there),
                    device_id_type=MESH,
                ).start()

            each_lane(step, one)

    def received(ref, k):
        await_bytes(ref.at[pl.ds(0, experts - 1)], a2a_recv.at[k])

    def iota(shape, axis):
        return lax.broadcasted_iota(jnp.int32, shape, axis)

    def bits(n):
        return n.bit_length() - 1

    def by_expert(row):
        slot = (row >= n_rows).astype(jnp.int32)
        row = row - slot * n_rows
        image = lax.bitwise_and(row, images - 1)
        return lax.shift_right_logical(row, bits(images)) * 4 * images + slot * images + image

    def by_image(row):
        slot = lax.bitwise_and(row, slots - 1)
        image = lax.shift_right_logical(row, bits(slots))
        odd = lax.bitwise_and(slot, 1)
        return lax.shift_right_logical(slot, 1) * 4 * images + odd * images + image

    def by_slot(row):
        odd = lax.bitwise_and(row, 1)
        return lax.shift_right_logical(row, 1) * CHUNK + odd * chunks

    def distance(shape, axis, order):
        return iota(shape, axis) - order(iota(shape, 1 - axis))

    def mark(distances, at):
        return (distances == at).astype(SINGLE).astype(LOW)

    def pack(value, order):
        n = value.shape[0]
        away = distance((experts * 4 * images, n), 0, order)
        block = sum(
            dot(mark(away, h * 2 * images), value[:, h * half : (h + 1) * half]) for h in range(2)
        )
        return block.astype(LOW).reshape(experts, 4 * images, half)

    def unpack(value, order, n):
        flat = value.reshape(experts * 4 * images, half)
        away = distance((n, experts * 4 * images), 1, order)
        return [dot(mark(away, h * 2 * images), flat).astype(LOW) for h in range(2)]

    collect(lambda block: router_own, router_got, 4)
    router_got[ex] = router_own[...]
    received(router_got, 4)
    flat = router_got[...].reshape(experts * CHUNK, LANES)
    away = distance((slots, experts * CHUNK), 1, by_slot)
    for c in range(chunks):
        router[:, c * LANES : (c + 1) * LANES] = dot(mark(away, c), flat).astype(LOW)

    column = iota((slots, n_padded), 1)
    image_of = jnp.where(column < n_tokens, lax.bitwise_and(column, images - 1), -1)

    def per_image(reduce, value, fill):
        spread = jnp.zeros_like(value)
        for i in range(images):
            mine = image_of == i
            total = reduce(jnp.where(mine, value, fill), axis=1, keepdims=True)
            spread = jnp.where(mine, total, spread)
        return spread

    def apart(value, low):
        for i in range(images):
            low[i * slots : (i + 1) * slots] = jnp.where(image_of == i, value, 0.0).astype(LOW)

    def together(value):
        total = jnp.zeros((slots, n_padded), SINGLE)
        for i in range(images):
            total = jnp.where(image_of == i, value[i * slots : (i + 1) * slots], total)
        return total

    logits = turn(router[...], held[0])
    weight = jnp.exp(logits - per_image(jnp.max, logits, -jnp.inf))
    weight = jnp.where(image_of >= 0, weight, 0.0)
    weight = weight / jnp.where(image_of >= 0, per_image(jnp.sum, weight, 0.0), 1.0)
    dispatch[...] = weight
    apart(weight, dispatch_low)
    message[0] = pack(dot(dispatch_low[...], held[0]).astype(LOW), by_image)
    deliver(message.at[0], got.at[0], 0)
    swap(0, 1, w_out.at[0, early], mate_out.at[0, early])
    hold(1)
    weight = jnp.exp(logits - jnp.max(logits, axis=0, keepdims=True))
    weight = weight / jnp.sum(weight, axis=0, keepdims=True)
    combine[...] = weight
    apart(weight, combine_low)
    message[1] = pack(dot(combine_low[...], held[1]).astype(LOW), by_image)

    def own_rows(a):
        received(got.at[a], a)
        for h, block in enumerate(unpack(got[a], by_expert, 2 * n_rows)):
            for e in range(2):
                rows[a, e, 0, :, h * half : (h + 1) * half] = block[e * n_rows : (e + 1) * n_rows]

    bands = (pl.ds(0, n_rows // 2), pl.ds(n_rows // 2, n_rows // 2))
    onward = (right, left)

    def send_block(a, e, src, dst, to, slot):
        sent.append(
            remote(rows.at[a, e, src], rows.at[a, e, dst], ag_send.at[a, slot], ag_recv.at[a, e, dst], to)
        )

    def arrived(a, e, j):
        await_bytes(rows.at[a, e, j], ag_recv.at[a, e, j])

    def gather_own(a):
        send_block(a, 1, 0, 1, partner, 0)
        send_block(a, 0, 0, 3, right, 1)
        send_block(a, 0, 0, 1, left, 2)
        send_block(a, 1, 0, 2, beside, 3)

    def gather_mate(a):
        arrived(a, 1, 1)
        send_block(a, 1, 1, 3, beside, 4)

    def gather_far(a):
        for side, j in enumerate((3, 1)):
            arrived(a, 0, j)
            sent.append(
                remote(
                    rows.at[a, 0, j, bands[side]],
                    rows.at[a, 0, 2, bands[side]],
                    ag_send.at[a, 5 + side],
                    ag_far.at[a, side],
                    onward[side],
                )
            )

    def far_rest(a):
        for side in range(2):
            await_bytes(rows.at[a, 0, 2, bands[side]], ag_far.at[a, side])

    def hidden(e):
        return ((w_in.at[e], w_out.at[e]), (mate_in.at[e], mate_out.at[e]))

    def forward(e, j):
        total = 0.0
        for h, (first, second) in enumerate(hidden(e)):
            value, grade = gelu_and_slope(dot(rows[0, e, j], first[...]))
            value = value.astype(LOW)
            act[e, h, j] = value
            slope[e, h, j] = grade
            total = total + dot(value, second[...])
        part[0, e, j] = total.astype(LOW)

    def backward(e, j):
        total = 0.0
        for h, (first, second) in enumerate(hidden(e)):
            grad = turn(rows[1, e, j], second[...])
            grad = (grad * slope[e, h, j]).astype(LOW)
            pre_grad[e, h, j] = grad
            total = total + turn(grad, first[...])
        part[1, e, j] = total.astype(LOW)

    def several(step, e, start, stop):
        def one(j, carry):
            step(e, j)
            return carry

        lax.fori_loop(start, stop, one, 0)

    def send_part(src, dst, send, recv, to):
        sent.append(remote(src, dst, send, recv, to))

    def reduce_far(a):
        for side in range(2):
            send_part(
                part.at[a, 0, 2, bands[side]],
                far.at[a, side],
                rs_send.at[a, side],
                far_recv.at[a, side],
                onward[side],
            )

    def send_near(a, side, band):
        send_part(
            part.at[a, 0, (1, 3)[side], bands[band]],
            near.at[a, side, bands[band]],
            rs_send.at[a, 2 + 2 * side + band],
            near_recv.at[a, side, band],
            onward[side],
        )

    def near_free(a):
        for side in range(2):
            send_near(a, side, 1 - side)

    def near_summed(a):
        for side in range(2):
            j = (1, 3)[side]
            await_bytes(far.at[a, side], far_recv.at[a, side])
            total = part[a, 0, j, bands[side]].astype(SINGLE) + far[a, side].astype(SINGLE)
            part[a, 0, j, bands[side]] = total.astype(LOW)
            send_near(a, side, side)

    def reduce_cross(a):
        send_part(part.at[a, 1, 3], cross.at[a], rs_send.at[a, 6], cross_recv.at[a], partner)
        send_part(part.at[a, 1, 1], over.at[a], rs_send.at[a, 7], over_recv.at[a], partner)

    def reduce_beside(a):
        await_bytes(cross.at[a], cross_recv.at[a])
        total = part[a, 1, 2].astype(SINGLE) + cross[a].astype(SINGLE)
        part[a, 1, 2] = total.astype(LOW)
        send_part(part.at[a, 1, 2], aside.at[a], rs_send.at[a, 8], aside_recv.at[a], beside)

    def give_back(a):
        first = part[a, 0, 0].astype(SINGLE)
        for side in range(2):
            for band in range(2):
                await_bytes(near.at[a, side, bands[band]], near_recv.at[a, side, band])
            first = first + near[a, side].astype(SINGLE)
        await_bytes(aside.at[a], aside_recv.at[a])
        await_bytes(over.at[a], over_recv.at[a])
        second = part[a, 1, 0].astype(SINGLE) + aside[a].astype(SINGLE) + over[a].astype(SINGLE)
        total = jnp.concatenate([first.astype(LOW), second.astype(LOW)], axis=0)
        ready[a] = pack(total, by_expert)
        collect(lambda block: ready.at[a, block], back.at[a], 2 + a)
        back[a, ex] = ready[a, lane]

    def given(a):
        received(back.at[a], 2 + a)
        return jnp.concatenate(unpack(back[a], by_image, pairs), axis=1)

    stores = []

    def store(src, dst, k):
        copy = pltpu.make_async_copy(src, dst, local.at[k])
        copy.start()
        stores.append(copy)

    def flat(value):
        return value.reshape(value.shape[0] * value.shape[1], value.shape[2])

    def weights_out(e):
        give_out[e] = outer(flat(act[e, 1]), flat(rows[1, e])).astype(LOW)
        swap(e, 2, give_out.at[e], took_out.at[e])

    def weights_in(e):
        give_in[e] = outer(flat(rows[0, e]), flat(pre_grad[e, 1])).astype(LOW)
        swap(e, 3, give_in.at[e], took_in.at[e])

    def weights_own(e):
        w_out_grad[e] = outer(flat(act[e, 0]), flat(rows[1, e]))
        w_in_grad[e] = outer(flat(rows[0, e]), flat(pre_grad[e, 0]))

    def weights_taken(e):
        await_bytes(took_out.at[e], swap_recv.at[e, 2])
        w_out_grad[e] = w_out_grad[e] + took_out[e].astype(SINGLE)
        store(w_out_grad.at[e], w_out_grad_hbm.at[e], 4 + e)
        await_bytes(took_in.at[e], swap_recv.at[e, 3])
        w_in_grad[e] = w_in_grad[e] + took_in[e].astype(SINGLE)
        store(w_in_grad.at[e], w_in_grad_hbm.at[e], 6 + e)

    def weights_here(e):
        await_bytes(mate_in.at[e], swap_recv.at[e, 0])
        if e == 0:
            await_bytes(mate_out.at[e, early], swap_recv.at[e, 1])
            await_bytes(mate_out.at[e, late], swap_recv.at[e, 4])
        else:
            await_bytes(mate_out.at[e], swap_recv.at[e, 1])

    own_rows(0)
    gather_own(0)
    deliver(message.at[1], got.at[1], 1)
    swap(0, 4, w_out.at[0, late], mate_out.at[0, late])
    gather_mate(0)
    weights_here(1)
    forward(1, 0)
    gather_far(0)
    forward(1, 1)
    own_rows(1)
    gather_own(1)
    for j in (2, 3):
        arrived(0, 1, j)
    several(forward, 1, 2, 4)
    gather_mate(1)
    gather_far(1)
    reduce_cross(0)
    weights_here(0)
    far_rest(0)
    several(forward, 0, 0, 4)
    reduce_far(0)
    near_free(0)
    reduce_beside(0)
    several(backward, 1, 0, 2)
    for j in (2, 3):
        arrived(1, 1, j)
    several(backward, 1, 2, 4)
    reduce_cross(1)
    near_summed(0)
    far_rest(1)
    several(backward, 0, 0, 4)
    reduce_far(1)
    near_free(1)
    weights_out(0)
    near_summed(1)
    give_back(0)
    reduce_beside(1)
    weights_out(1)
    give_back(1)
    weights_in(0)
    weights_in(1)
    weights_own(0)
    weights_own(1)

    slot_out = given(0)
    value = outer(combine_low[...], slot_out)[:n_tokens].astype(LOW)
    raw[0] = value.reshape(raw.shape[1:])
    store(raw.at[0], mixed_hbm, 8)
    grad = together(turn(slot_out, held[1]))
    weight = combine[...]
    combine_term[...] = weight * (grad - jnp.sum(weight * grad, axis=0, keepdims=True))

    input_slots = given(1)
    grad = together(turn(input_slots, held[0]))
    weight = dispatch[...]
    grad = weight * (grad - per_image(jnp.sum, weight * grad, 0.0)) + combine_term[...]
    grad = jnp.where(image_of >= 0, grad, 0.0).astype(LOW)
    total = dot(grad, held[0]).astype(LOW)
    away = distance((experts * CHUNK, slots), 0, by_slot)
    block = sum(
        dot(mark(away, c), total[:, c * LANES : (c + 1) * LANES]) for c in range(chunks)
    )
    router_message[...] = block.astype(LOW).reshape(experts, CHUNK, LANES)
    deliver(router_message, router_first, 5)
    value = outer(dispatch_low[...], input_slots) + outer(grad, router[...])
    raw[1] = value[:n_tokens].astype(LOW).reshape(raw.shape[1:])
    store(raw.at[1], tokens_grad_hbm, 9)

    received(router_first, 5)
    router_mine[...] = jnp.sum(router_first[...].astype(SINGLE), axis=0)

    def share(k, carry):
        pltpu.make_async_remote_copy(
            src_ref=router_mine,
            dst_ref=router_second.at[dp],
            send_sem=a2a_send.at[6],
            recv_sem=a2a_recv.at[6],
            device_id=(lax.rem(dp + k, shards), ex),
            device_id_type=MESH,
        ).start()
        return carry

    lax.fori_loop(1, shards, share, 0, unroll=True)
    router_second[dp] = router_mine[...]
    await_bytes(router_second.at[pl.ds(0, shards - 1)], a2a_recv.at[6])
    value = jnp.sum(router_second[...], axis=0)
    for s in range(owned):
        for c in range(chunks):
            at = s * chunks + c
            router_grad[s : s + 1, c * LANES : (c + 1) * LANES] = value[at : at + 1]

    for e in (1, 0):
        weights_taken(e)
    for k in range(4):
        await_bytes(got.at[0, pl.ds(0, experts - 1)], a2a_send.at[k])
    for k in range(4, 6):
        await_bytes(router_got.at[pl.ds(0, experts - 1)], a2a_send.at[k])
    await_bytes(router_second.at[pl.ds(0, shards - 1)], a2a_send.at[6])
    for copy in sent:
        copy.wait_send()
    for copy in stores:
        copy.wait()


def finish_kernel(*refs):
    count = (len(refs) - 2) // 3
    sources, results, staged = (refs[k * count : (k + 1) * count] for k in range(3))
    into, out = refs[-2:]
    pieces = []
    for src, dst, held in zip(sources, results, staged):
        parts = 1 if len(src.shape) < 3 else PARTS if src.shape[0] % PARTS == 0 else src.shape[0]
        size = src.shape[0] // parts
        for at in range(parts):
            rows, k = pl.ds(at * size, size), len(pieces)
            pieces.append(
                (
                    pltpu.make_async_copy(src.at[rows], held.at[rows], into.at[k]),
                    pltpu.make_async_copy(held.at[rows], dst.at[rows], out.at[k]),
                )
            )
    for read, _ in pieces:
        read.start()
    for read, write in pieces:
        read.wait()
        write.start()
    for _, write in pieces:
        write.wait()


def finish(*values):
    anywhere = pl.BlockSpec(memory_space=pl.ANY)
    return pl.pallas_call(
        finish_kernel,
        out_shape=[jax.ShapeDtypeStruct(value.shape, value.dtype) for value in values],
        in_specs=[anywhere] * len(values),
        out_specs=[anywhere] * len(values),
        scratch_shapes=[pltpu.VMEM(value.shape, value.dtype) for value in values]
        + [pltpu.SemaphoreType.DMA((PARTS * len(values),))] * 2,
        compiler_params=pltpu.CompilerParams(vmem_limit_bytes=VMEM_BYTES),
        name="finish",
    )(*values)


def body(experts, tokens, router, w_in, w_out, cotangent):
    images, n, d = tokens.shape
    hidden = w_in.shape[2]
    owned = router.shape[1]
    slots = experts * owned
    n_tokens = images * n
    n_padded = -(-n_tokens // LANES) * LANES
    n_rows = experts * images
    half = d // 2

    def swap(value):
        return value.transpose(1, 0, 2)

    def low(*shape):
        return pltpu.VMEM(shape, LOW)

    def single(*shape):
        return pltpu.VMEM(shape, SINGLE)

    anywhere = pl.BlockSpec(memory_space=pl.ANY)
    in_hbm = pl.BlockSpec(memory_space=pltpu.HBM)
    vmem = pl.BlockSpec(memory_space=pltpu.VMEM)
    dma = pltpu.SemaphoreType.DMA
    mixed, tokens_grad, w_in_grad, w_out_grad, router_grad = pl.pallas_call(
        functools.partial(layer_kernel, experts, images),
        out_shape=[
            jax.ShapeDtypeStruct((n, images, d), LOW),
            jax.ShapeDtypeStruct((n, images, d), LOW),
            jax.ShapeDtypeStruct(w_in.shape, SINGLE),
            jax.ShapeDtypeStruct(w_out.shape, SINGLE),
            jax.ShapeDtypeStruct((owned, d), SINGLE),
        ],
        in_specs=[in_hbm, in_hbm, vmem, in_hbm, in_hbm],
        out_specs=[anywhere] * 4 + [vmem],
        scratch_shapes=[
            low(2, n, images, d),
            low(2, n_padded, d),
            low(*w_in.shape),
            low(*w_out.shape),
            low(*w_in.shape),
            low(*w_out.shape),
            low(*w_in.shape),
            low(*w_out.shape),
            low(*w_in.shape),
            low(*w_out.shape),
            low(CHUNK, LANES),
            low(experts, CHUNK, LANES),
            low(slots, d),
            single(slots, n_padded),
            single(slots, n_padded),
            low(images * slots, n_padded),
            low(images * slots, n_padded),
            low(2, experts, 4 * images, half),
            low(2, experts, 4 * images, half),
            low(2, 2, RING, n_rows, d),
            low(2, 2, RING, n_rows, d),
            low(2, 2, RING, n_rows, hidden),
            single(2, 2, RING, n_rows, hidden),
            low(2, 2, RING, n_rows, hidden),
            low(2, 2, n_rows // 2, d),
            low(2, 2, n_rows, d),
            low(2, n_rows, d),
            low(2, n_rows, d),
            low(2, n_rows, d),
            low(2, experts, 4 * images, half),
            low(2, experts, 4 * images, half),
            single(slots, n_padded),
            single(*w_in.shape),
            single(*w_out.shape),
            low(experts, CHUNK, LANES),
            low(experts, CHUNK, LANES),
            single(CHUNK, LANES),
            single(2 * RING, CHUNK, LANES),
            dma((10,)),
            dma((7,)),
            dma((7,)),
            dma((2, 5)),
            dma((2, 5)),
            dma((2, 7)),
            dma((2, 2, RING)),
            dma((2, 2)),
            dma((2, 9)),
            dma((2, 2)),
            dma((2, 2, 2)),
            dma((2,)),
            dma((2,)),
            dma((2,)),
        ],
        compiler_params=pltpu.CompilerParams(
            collective_id=0, has_side_effects=True, vmem_limit_bytes=VMEM_BYTES
        ),
        name="layer",
    )(swap(tokens), swap(cotangent), router.T, w_in, w_out)
    mixed, tokens_grad, w_in_grad, w_out_grad, router_grad = finish(
        mixed, tokens_grad, w_in_grad, w_out_grad, router_grad
    )
    return (swap(mixed), swap(tokens_grad), w_in_grad, w_out_grad, router_grad.T)


def solution(mesh):
    placed = (
        P(("dp", "expert"), None, None),
        P(None, "expert"),
        P("expert", None, "dp"),
        P("expert", "dp", None),
        P(("dp", "expert"), None, None),
    )
    return jax.shard_map(
        functools.partial(body, mesh.shape["expert"]),
        mesh=mesh,
        in_specs=placed,
        out_specs=(
            P(("dp", "expert"), None, None),
            P(("dp", "expert"), None, None),
            P("expert", None, "dp"),
            P("expert", "dp", None),
            P(None, "expert"),
        ),
        check_vma=False,
    )
```

```python
import functools

import jax
import jax.numpy as jnp
from jax import lax
from jax.experimental import pallas as pl
from jax.experimental.pallas import tpu as pltpu
from jax.sharding import PartitionSpec as P

SINGLE = jnp.float32
LOW = jnp.bfloat16
MESH = pl.DeviceIdType.MESH
RING = 4
Z_HIGH = 4
LANES = 128
VMEM_BYTES = 58 * 1024 * 1024
PARTS = 4
CHUNK = 16


def remote(src, dst, send, recv, device):
    copy = pltpu.make_async_remote_copy(
        src_ref=src, dst_ref=dst, send_sem=send, recv_sem=recv, device_id=device, device_id_type=MESH
    )
    copy.start()
    return copy


def await_bytes(ref, sem):
    pltpu.make_async_copy(ref, ref, sem).wait()


def gelu_and_slope(v):
    c = 0.7978845608028654
    square = v * v
    t = jnp.tanh(c * v * (1.0 + 0.044715 * square))
    half = 0.5 * (1.0 + t)
    slope = half + 0.5 * v * (1.0 - t * t) * (c * (1.0 + 3.0 * 0.044715 * square))
    return v * half, slope


def turn(lhs, rhs):
    return lax.dot_general(lhs, rhs, (((1,), (1,)), ((), ())), preferred_element_type=SINGLE)


def outer(lhs, rhs):
    return lax.dot_general(lhs, rhs, (((0,), (0,)), ((), ())), preferred_element_type=SINGLE)


def dot(lhs, rhs):
    return jnp.dot(lhs, rhs, preferred_element_type=SINGLE)


def layer_kernel(
    experts,
    images,
    tokens_hbm,
    cotangent_hbm,
    router_columns,
    w_in_hbm,
    w_out_hbm,
    mixed_hbm,
    tokens_grad_hbm,
    w_in_grad_hbm,
    w_out_grad_hbm,
    router_grad,
    raw,
    held,
    w_in,
    w_out,
    mate_in,
    mate_out,
    give_in,
    give_out,
    took_in,
    took_out,
    router_own,
    router_got,
    router,
    dispatch,
    combine,
    dispatch_low,
    combine_low,
    message,
    got,
    rows,
    part,
    act,
    slope,
    pre_grad,
    far,
    near,
    cross,
    aside,
    over,
    ready,
    back,
    combine_term,
    w_in_grad,
    w_out_grad,
    router_message,
    router_first,
    router_mine,
    router_second,
    local,
    a2a_send,
    a2a_recv,
    swap_send,
    swap_recv,
    ag_send,
    ag_recv,
    ag_far,
    rs_send,
    far_recv,
    near_recv,
    cross_recv,
    aside_recv,
    over_recv,
):
    dp, ex = lax.axis_index("dp"), lax.axis_index("expert")
    shards = 2 * RING
    x, z = lax.rem(dp, RING), dp // RING
    odd = lax.rem(x, 2)
    partner = ((1 - z) * RING + x, ex)
    right = (z * RING + lax.rem(x + 1, RING), ex)
    left = (z * RING + lax.rem(x + 3, RING), ex)
    across = (z * RING + lax.rem(x + 1 + 2 * odd, RING), ex)
    beside = (z * RING + lax.rem(x + 3 + 2 * odd, RING), ex)
    n_rows = experts * images
    half = rows.shape[-1] // 2
    slots = 2 * experts
    pairs = images * slots
    n_tokens, n_padded = tokens_hbm.shape[0] * images, held.shape[1]
    chunks = rows.shape[-1] // LANES
    inner = experts // Z_HIGH
    lane = lax.rem(ex, inner)
    z_at = (ex // inner) * 2 + z
    way = 1 - 2 * z

    loads = [
        pltpu.make_async_copy(src, dst, local.at[k])
        for k, (src, dst) in enumerate(
            (
                (tokens_hbm, raw.at[0]),
                (cotangent_hbm, raw.at[1]),
                (w_in_hbm, w_in),
                (w_out_hbm, w_out),
            )
        )
    ]
    for load in loads:
        load.start()
    owned = router_columns.shape[0]
    value = router_columns[...].astype(SINGLE)
    lines = [value[s : s + 1, c * LANES : (c + 1) * LANES] for s in range(owned) for c in range(chunks)]
    lines.append(jnp.zeros((CHUNK - owned * chunks, LANES), SINGLE))
    router_own[...] = jnp.concatenate(lines, axis=0).astype(LOW)

    barrier = pltpu.get_barrier_semaphore()

    def each_lane(step, what):
        def one(i, carry):
            what(lax.rem(lane + i, inner))
            return carry

        lax.fori_loop(0 if step else 1, inner, one, 0, unroll=True)

    def at_z(offset):
        z_to = lax.rem(z_at + offset + 4 * Z_HIGH, 2 * Z_HIGH)
        return lax.rem(z_to, 2) * RING + x, (z_to // 2) * inner

    def greet_experts(step, offset):
        dp_to, first = at_z(offset)

        def one(there):
            to = (dp_to, first + there)
            pl.semaphore_signal(barrier, inc=1, device_id=to, device_id_type=MESH)

        each_lane(step, one)

    def greet_shards(k, carry):
        to = (lax.rem(dp + k, shards), ex)
        pl.semaphore_signal(barrier, inc=1, device_id=to, device_id_type=MESH)
        return carry

    greeted = (Z_HIGH + 1) * inner
    for step, offset in enumerate((0, -way, -2 * way, -3 * way, 2 * way)):
        greet_experts(step, offset)
    lax.fori_loop(1, shards, greet_shards, 0, unroll=True)

    def hold(k):
        loads[k].wait()
        held[k, :n_tokens] = raw[k].reshape(n_tokens, held.shape[2])
        if n_padded > n_tokens:
            held[k, n_tokens:] = jnp.zeros((n_padded - n_tokens, held.shape[2]), LOW)

    hold(0)
    pl.semaphore_wait(barrier, greeted - 1 + shards - 1)

    swap_with = (partner, across)
    some = w_out.shape[1] // 2
    early, late = pl.ds(0, some), pl.ds(some, some)

    def swap(e, k, src, dst):
        sent.append(remote(src, dst, swap_send.at[e, k], swap_recv.at[e, k], swap_with[e]))

    sent = []

    def deliver(src, dst, k):
        for step in range(Z_HIGH):
            dp_to, first = at_z(step * way * (1 - 2 * (step % 2)))

            def one(there, step=step, dp_to=dp_to, first=first):
                pltpu.make_async_remote_copy(
                    src_ref=src.at[first + there],
                    dst_ref=dst.at[step * inner + lane],
                    send_sem=a2a_send.at[k],
                    recv_sem=a2a_recv.at[k],
                    device_id=(dp_to, first + there),
                    device_id_type=MESH,
                ).start()

            each_lane(step, one)
        dst[lane] = src[ex]

    def collect(src_of, dst, k):
        for step in range(Z_HIGH):
            dp_to, first = at_z(-step * way)

            def one(there, step=step, dp_to=dp_to, first=first):
                pltpu.make_async_remote_copy(
                    src_ref=src_of(step * inner + there),
                    dst_ref=dst.at[ex],
                    send_sem=a2a_send.at[k],
                    recv_sem=a2a_recv.at[k],
                    device_id=(dp_to, first + there),
                    device_id_type=MESH,
                ).start()

            each_lane(step, one)

    def received(ref, k):
        await_bytes(ref.at[pl.ds(0, experts - 1)], a2a_recv.at[k])

    def iota(shape, axis):
        return lax.broadcasted_iota(jnp.int32, shape, axis)

    def bits(n):
        return n.bit_length() - 1

    def by_expert(row):
        slot = (row >= n_rows).astype(jnp.int32)
        row = row - slot * n_rows
        image = lax.bitwise_and(row, images - 1)
        return lax.shift_right_logical(row, bits(images)) * 4 * images + slot * images + image

    def by_image(row):
        slot = lax.bitwise_and(row, slots - 1)
        image = lax.shift_right_logical(row, bits(slots))
        odd = lax.bitwise_and(slot, 1)
        return lax.shift_right_logical(slot, 1) * 4 * images + odd * images + image

    def by_slot(row):
        odd = lax.bitwise_and(row, 1)
        return lax.shift_right_logical(row, 1) * CHUNK + odd * chunks

    def distance(shape, axis, order):
        return iota(shape, axis) - order(iota(shape, 1 - axis))

    def mark(distances, at):
        return (distances == at).astype(SINGLE).astype(LOW)

    def pack(value, order):
        n = value.shape[0]
        away = distance((experts * 4 * images, n), 0, order)
        block = sum(
            dot(mark(away, h * 2 * images), value[:, h * half : (h + 1) * half]) for h in range(2)
        )
        return block.astype(LOW).reshape(experts, 4 * images, half)

    def unpack(value, order, n):
        flat = value.reshape(experts * 4 * images, half)
        away = distance((n, experts * 4 * images), 1, order)
        return [dot(mark(away, h * 2 * images), flat).astype(LOW) for h in range(2)]

    collect(lambda block: router_own, router_got, 4)
    for load in loads[2:]:
        load.wait()
    swap(1, 0, w_in.at[1], mate_in.at[1])
    swap(0, 0, w_in.at[0], mate_in.at[0])
    swap(1, 1, w_out.at[1], mate_out.at[1])
    router_got[ex] = router_own[...]
    received(router_got, 4)
    flat = router_got[...].reshape(experts * CHUNK, LANES)
    away = distance((slots, experts * CHUNK), 1, by_slot)
    for c in range(chunks):
        router[:, c * LANES : (c + 1) * LANES] = dot(mark(away, c), flat).astype(LOW)

    column = iota((slots, n_padded), 1)
    image_of = jnp.where(column < n_tokens, lax.bitwise_and(column, images - 1), -1)

    def per_image(reduce, value, fill):
        spread = jnp.zeros_like(value)
        for i in range(images):
            mine = image_of == i
            total = reduce(jnp.where(mine, value, fill), axis=1, keepdims=True)
            spread = jnp.where(mine, total, spread)
        return spread

    def apart(value, low):
        for i in range(images):
            low[i * slots : (i + 1) * slots] = jnp.where(image_of == i, value, 0.0).astype(LOW)

    def together(value):
        total = jnp.zeros((slots, n_padded), SINGLE)
        for i in range(images):
            total = jnp.where(image_of == i, value[i * slots : (i + 1) * slots], total)
        return total

    logits = turn(router[...], held[0])
    weight = jnp.exp(logits - per_image(jnp.max, logits, -jnp.inf))
    weight = jnp.where(image_of >= 0, weight, 0.0)
    weight = weight / jnp.where(image_of >= 0, per_image(jnp.sum, weight, 0.0), 1.0)
    dispatch[...] = weight
    apart(weight, dispatch_low)
    message[0] = pack(dot(dispatch_low[...], held[0]).astype(LOW), by_image)
    deliver(message.at[0], got.at[0], 0)
    swap(0, 1, w_out.at[0, early], mate_out.at[0, early])
    hold(1)
    weight = jnp.exp(logits - jnp.max(logits, axis=0, keepdims=True))
    weight = weight / jnp.sum(weight, axis=0, keepdims=True)
    combine[...] = weight
    apart(weight, combine_low)
    message[1] = pack(dot(combine_low[...], held[1]).astype(LOW), by_image)

    def own_rows(a):
        received(got.at[a], a)
        for h, block in enumerate(unpack(got[a], by_expert, 2 * n_rows)):
            for e in range(2):
                rows[a, e, 0, :, h * half : (h + 1) * half] = block[e * n_rows : (e + 1) * n_rows]

    bands = (pl.ds(0, n_rows // 2), pl.ds(n_rows // 2, n_rows // 2))
    onward = (right, left)

    def send_block(a, e, src, dst, to, slot):
        sent.append(
            remote(rows.at[a, e, src], rows.at[a, e, dst], ag_send.at[a, slot], ag_recv.at[a, e, dst], to)
        )

    def arrived(a, e, j):
        await_bytes(rows.at[a, e, j], ag_recv.at[a, e, j])

    def gather_own(a):
        send_block(a, 1, 0, 1, partner, 0)
        send_block(a, 0, 0, 3, right, 1)
        send_block(a, 0, 0, 1, left, 2)
        send_block(a, 1, 0, 2, beside, 3)

    def gather_mate(a):
        arrived(a, 1, 1)
        send_block(a, 1, 1, 3, beside, 4)

    def gather_far(a):
        for side, j in enumerate((3, 1)):
            arrived(a, 0, j)
            sent.append(
                remote(
                    rows.at[a, 0, j, bands[side]],
                    rows.at[a, 0, 2, bands[side]],
                    ag_send.at[a, 5 + side],
                    ag_far.at[a, side],
                    onward[side],
                )
            )

    def far_rest(a):
        for side in range(2):
            await_bytes(rows.at[a, 0, 2, bands[side]], ag_far.at[a, side])

    def hidden(e):
        return ((w_in.at[e], w_out.at[e]), (mate_in.at[e], mate_out.at[e]))

    def forward(e, j):
        total = 0.0
        for h, (first, second) in enumerate(hidden(e)):
            value, grade = gelu_and_slope(dot(rows[0, e, j], first[...]))
            value = value.astype(LOW)
            act[e, h, j] = value
            slope[e, h, j] = grade
            total = total + dot(value, second[...])
        part[0, e, j] = total.astype(LOW)

    def backward(e, j):
        total = 0.0
        for h, (first, second) in enumerate(hidden(e)):
            grad = turn(rows[1, e, j], second[...])
            grad = (grad * slope[e, h, j]).astype(LOW)
            pre_grad[e, h, j] = grad
            total = total + turn(grad, first[...])
        part[1, e, j] = total.astype(LOW)

    def several(step, e, start, stop):
        def one(j, carry):
            step(e, j)
            return carry

        lax.fori_loop(start, stop, one, 0)

    def send_part(src, dst, send, recv, to):
        sent.append(remote(src, dst, send, recv, to))

    def reduce_far(a):
        for side in range(2):
            send_part(
                part.at[a, 0, 2, bands[side]],
                far.at[a, side],
                rs_send.at[a, side],
                far_recv.at[a, side],
                onward[side],
            )

    def send_near(a, side, band):
        send_part(
            part.at[a, 0, (1, 3)[side], bands[band]],
            near.at[a, side, bands[band]],
            rs_send.at[a, 2 + 2 * side + band],
            near_recv.at[a, side, band],
            onward[side],
        )

    def near_free(a):
        for side in range(2):
            send_near(a, side, 1 - side)

    def near_summed(a):
        for side in range(2):
            j = (1, 3)[side]
            await_bytes(far.at[a, side], far_recv.at[a, side])
            total = part[a, 0, j, bands[side]].astype(SINGLE) + far[a, side].astype(SINGLE)
            part[a, 0, j, bands[side]] = total.astype(LOW)
            send_near(a, side, side)

    def reduce_cross(a):
        send_part(part.at[a, 1, 3], cross.at[a], rs_send.at[a, 6], cross_recv.at[a], partner)
        send_part(part.at[a, 1, 1], over.at[a], rs_send.at[a, 7], over_recv.at[a], partner)

    def reduce_beside(a):
        await_bytes(cross.at[a], cross_recv.at[a])
        total = part[a, 1, 2].astype(SINGLE) + cross[a].astype(SINGLE)
        part[a, 1, 2] = total.astype(LOW)
        send_part(part.at[a, 1, 2], aside.at[a], rs_send.at[a, 8], aside_recv.at[a], beside)

    def give_back(a):
        first = part[a, 0, 0].astype(SINGLE)
        for side in range(2):
            for band in range(2):
                await_bytes(near.at[a, side, bands[band]], near_recv.at[a, side, band])
            first = first + near[a, side].astype(SINGLE)
        await_bytes(aside.at[a], aside_recv.at[a])
        await_bytes(over.at[a], over_recv.at[a])
        second = part[a, 1, 0].astype(SINGLE) + aside[a].astype(SINGLE) + over[a].astype(SINGLE)
        total = jnp.concatenate([first.astype(LOW), second.astype(LOW)], axis=0)
        ready[a] = pack(total, by_expert)
        collect(lambda block: ready.at[a, block], back.at[a], 2 + a)
        back[a, ex] = ready[a, lane]

    def given(a):
        received(back.at[a], 2 + a)
        return jnp.concatenate(unpack(back[a], by_image, pairs), axis=1)

    stores = []

    def store(src, dst, k):
        copy = pltpu.make_async_copy(src, dst, local.at[k])
        copy.start()
        stores.append(copy)

    def flat(value):
        return value.reshape(value.shape[0] * value.shape[1], value.shape[2])

    def weights_out(e):
        give_out[e] = outer(flat(act[e, 1]), flat(rows[1, e])).astype(LOW)
        swap(e, 2, give_out.at[e], took_out.at[e])

    third = w_in.shape[1] // 3
    thirds = [pl.ds(k * third, third) for k in range(3)]

    def weights_in(e):
        give_in[e] = outer(flat(rows[0, e]), flat(pre_grad[e, 1])).astype(LOW)

    def weights_in_given(e, k):
        swap(e, 4 + k, give_in.at[e, thirds[k]], took_in.at[e, thirds[k]])

    def weights_own(e):
        w_out_grad[e] = outer(flat(act[e, 0]), flat(rows[1, e]))
        w_in_grad[e] = outer(flat(rows[0, e]), flat(pre_grad[e, 0]))

    def weights_taken(e):
        await_bytes(took_out.at[e], swap_recv.at[e, 2])
        w_out_grad[e] = w_out_grad[e] + took_out[e].astype(SINGLE)
        store(w_out_grad.at[e], w_out_grad_hbm.at[e], 4 + e)
        for k in range(3):
            await_bytes(took_in.at[e, thirds[k]], swap_recv.at[e, 4 + k])
        w_in_grad[e] = w_in_grad[e] + took_in[e].astype(SINGLE)
        store(w_in_grad.at[e], w_in_grad_hbm.at[e], 6 + e)

    def weights_here(e):
        await_bytes(mate_in.at[e], swap_recv.at[e, 0])
        if e == 0:
            await_bytes(mate_out.at[e, early], swap_recv.at[e, 1])
            await_bytes(mate_out.at[e, late], swap_recv.at[e, 3])
        else:
            await_bytes(mate_out.at[e], swap_recv.at[e, 1])

    own_rows(0)
    gather_own(0)
    deliver(message.at[1], got.at[1], 1)
    swap(0, 3, w_out.at[0, late], mate_out.at[0, late])
    gather_mate(0)
    weights_here(1)
    forward(1, 0)
    gather_far(0)
    forward(1, 1)
    own_rows(1)
    gather_own(1)
    for j in (2, 3):
        arrived(0, 1, j)
    several(forward, 1, 2, 4)
    gather_mate(1)
    gather_far(1)
    reduce_cross(0)
    weights_here(0)
    far_rest(0)
    several(forward, 0, 0, 4)
    reduce_far(0)
    near_free(0)
    reduce_beside(0)
    several(backward, 1, 0, 2)
    for j in (2, 3):
        arrived(1, 1, j)
    several(backward, 1, 2, 4)
    reduce_cross(1)
    near_summed(0)
    far_rest(1)
    several(backward, 0, 0, 4)
    reduce_far(1)
    near_free(1)
    weights_out(0)
    near_summed(1)
    give_back(0)
    reduce_beside(1)
    weights_out(1)
    give_back(1)
    weights_in(0)
    weights_in_given(0, 0)
    weights_in(1)
    for k in range(3):
        weights_in_given(1, k)
    weights_own(0)
    weights_own(1)

    slot_out = given(0)
    value = outer(combine_low[...], slot_out)[:n_tokens].astype(LOW)
    raw[0] = value.reshape(raw.shape[1:])
    store(raw.at[0], mixed_hbm, 8)
    grad = together(turn(slot_out, held[1]))
    weight = combine[...]
    combine_term[...] = weight * (grad - jnp.sum(weight * grad, axis=0, keepdims=True))

    input_slots = given(1)
    grad = together(turn(input_slots, held[0]))
    weight = dispatch[...]
    grad = weight * (grad - per_image(jnp.sum, weight * grad, 0.0)) + combine_term[...]
    grad = jnp.where(image_of >= 0, grad, 0.0).astype(LOW)
    total = dot(grad, held[0]).astype(LOW)
    away = distance((experts * CHUNK, slots), 0, by_slot)
    block = sum(
        dot(mark(away, c), total[:, c * LANES : (c + 1) * LANES]) for c in range(chunks)
    )
    router_message[...] = block.astype(LOW).reshape(experts, CHUNK, LANES)
    deliver(router_message, router_first, 5)
    for k in (1, 2):
        weights_in_given(0, k)
    value = outer(dispatch_low[...], input_slots) + outer(grad, router[...])
    raw[1] = value[:n_tokens].astype(LOW).reshape(raw.shape[1:])
    store(raw.at[1], tokens_grad_hbm, 9)

    received(router_first, 5)
    router_mine[...] = jnp.sum(router_first[...].astype(SINGLE), axis=0)

    def share(k, carry):
        pltpu.make_async_remote_copy(
            src_ref=router_mine,
            dst_ref=router_second.at[dp],
            send_sem=a2a_send.at[6],
            recv_sem=a2a_recv.at[6],
            device_id=(lax.rem(dp + k, shards), ex),
            device_id_type=MESH,
        ).start()
        return carry

    lax.fori_loop(1, shards, share, 0, unroll=True)
    router_second[dp] = router_mine[...]
    await_bytes(router_second.at[pl.ds(0, shards - 1)], a2a_recv.at[6])
    value = jnp.sum(router_second[...], axis=0)
    for s in range(owned):
        for c in range(chunks):
            at = s * chunks + c
            router_grad[s : s + 1, c * LANES : (c + 1) * LANES] = value[at : at + 1]

    for e in (1, 0):
        weights_taken(e)
    for k in range(4):
        await_bytes(got.at[0, pl.ds(0, experts - 1)], a2a_send.at[k])
    for k in range(4, 6):
        await_bytes(router_got.at[pl.ds(0, experts - 1)], a2a_send.at[k])
    await_bytes(router_second.at[pl.ds(0, shards - 1)], a2a_send.at[6])
    for copy in sent:
        copy.wait_send()
    for copy in stores:
        copy.wait()


def finish_kernel(*refs):
    count = (len(refs) - 2) // 3
    sources, results, staged = (refs[k * count : (k + 1) * count] for k in range(3))
    into, out = refs[-2:]
    pieces = []
    for src, dst, held in zip(sources, results, staged):
        parts = 1 if len(src.shape) < 3 else PARTS if src.shape[0] % PARTS == 0 else src.shape[0]
        size = src.shape[0] // parts
        for at in range(parts):
            rows, k = pl.ds(at * size, size), len(pieces)
            pieces.append(
                (
                    pltpu.make_async_copy(src.at[rows], held.at[rows], into.at[k]),
                    pltpu.make_async_copy(held.at[rows], dst.at[rows], out.at[k]),
                )
            )
    for read, _ in pieces:
        read.start()
    for read, write in pieces:
        read.wait()
        write.start()
    for _, write in pieces:
        write.wait()


def finish(*values):
    anywhere = pl.BlockSpec(memory_space=pl.ANY)
    return pl.pallas_call(
        finish_kernel,
        out_shape=[jax.ShapeDtypeStruct(value.shape, value.dtype) for value in values],
        in_specs=[anywhere] * len(values),
        out_specs=[anywhere] * len(values),
        scratch_shapes=[pltpu.VMEM(value.shape, value.dtype) for value in values]
        + [pltpu.SemaphoreType.DMA((PARTS * len(values),))] * 2,
        compiler_params=pltpu.CompilerParams(vmem_limit_bytes=VMEM_BYTES),
        name="finish",
    )(*values)


def body(experts, tokens, router, w_in, w_out, cotangent):
    images, n, d = tokens.shape
    hidden = w_in.shape[2]
    owned = router.shape[1]
    slots = experts * owned
    n_tokens = images * n
    n_padded = -(-n_tokens // LANES) * LANES
    n_rows = experts * images
    half = d // 2

    def swap(value):
        return value.transpose(1, 0, 2)

    def low(*shape):
        return pltpu.VMEM(shape, LOW)

    def single(*shape):
        return pltpu.VMEM(shape, SINGLE)

    anywhere = pl.BlockSpec(memory_space=pl.ANY)
    in_hbm = pl.BlockSpec(memory_space=pltpu.HBM)
    vmem = pl.BlockSpec(memory_space=pltpu.VMEM)
    dma = pltpu.SemaphoreType.DMA
    mixed, tokens_grad, w_in_grad, w_out_grad, router_grad = pl.pallas_call(
        functools.partial(layer_kernel, experts, images),
        out_shape=[
            jax.ShapeDtypeStruct((n, images, d), LOW),
            jax.ShapeDtypeStruct((n, images, d), LOW),
            jax.ShapeDtypeStruct(w_in.shape, SINGLE),
            jax.ShapeDtypeStruct(w_out.shape, SINGLE),
            jax.ShapeDtypeStruct((owned, d), SINGLE),
        ],
        in_specs=[in_hbm, in_hbm, vmem, in_hbm, in_hbm],
        out_specs=[anywhere] * 4 + [vmem],
        scratch_shapes=[
            low(2, n, images, d),
            low(2, n_padded, d),
            low(*w_in.shape),
            low(*w_out.shape),
            low(*w_in.shape),
            low(*w_out.shape),
            low(*w_in.shape),
            low(*w_out.shape),
            low(*w_in.shape),
            low(*w_out.shape),
            low(CHUNK, LANES),
            low(experts, CHUNK, LANES),
            low(slots, d),
            single(slots, n_padded),
            single(slots, n_padded),
            low(images * slots, n_padded),
            low(images * slots, n_padded),
            low(2, experts, 4 * images, half),
            low(2, experts, 4 * images, half),
            low(2, 2, RING, n_rows, d),
            low(2, 2, RING, n_rows, d),
            low(2, 2, RING, n_rows, hidden),
            single(2, 2, RING, n_rows, hidden),
            low(2, 2, RING, n_rows, hidden),
            low(2, 2, n_rows // 2, d),
            low(2, 2, n_rows, d),
            low(2, n_rows, d),
            low(2, n_rows, d),
            low(2, n_rows, d),
            low(2, experts, 4 * images, half),
            low(2, experts, 4 * images, half),
            single(slots, n_padded),
            single(*w_in.shape),
            single(*w_out.shape),
            low(experts, CHUNK, LANES),
            low(experts, CHUNK, LANES),
            single(CHUNK, LANES),
            single(2 * RING, CHUNK, LANES),
            dma((10,)),
            dma((7,)),
            dma((7,)),
            dma((2, 7)),
            dma((2, 7)),
            dma((2, 7)),
            dma((2, 2, RING)),
            dma((2, 2)),
            dma((2, 9)),
            dma((2, 2)),
            dma((2, 2, 2)),
            dma((2,)),
            dma((2,)),
            dma((2,)),
        ],
        compiler_params=pltpu.CompilerParams(
            collective_id=0, has_side_effects=True, vmem_limit_bytes=VMEM_BYTES
        ),
        name="layer",
    )(swap(tokens), swap(cotangent), router.T, w_in, w_out)
    mixed, tokens_grad, w_in_grad, w_out_grad, router_grad = finish(
        mixed, tokens_grad, w_in_grad, w_out_grad, router_grad
    )
    return (swap(mixed), swap(tokens_grad), w_in_grad, w_out_grad, router_grad.T)


def solution(mesh):
    placed = (
        P(("dp", "expert"), None, None),
        P(None, "expert"),
        P("expert", None, "dp"),
        P("expert", "dp", None),
        P(("dp", "expert"), None, None),
    )
    return jax.shard_map(
        functools.partial(body, mesh.shape["expert"]),
        mesh=mesh,
        in_specs=placed,
        out_specs=(
            P(("dp", "expert"), None, None),
            P(("dp", "expert"), None, None),
            P("expert", None, "dp"),
            P("expert", "dp", None),
            P(None, "expert"),
        ),
        check_vma=False,
    )
```

```python
import functools

import jax
import jax.numpy as jnp
from jax import lax
from jax.experimental import pallas as pl
from jax.experimental.pallas import tpu as pltpu
from jax.sharding import PartitionSpec as P

SINGLE = jnp.float32
LOW = jnp.bfloat16
MESH = pl.DeviceIdType.MESH
RING = 4
Z_HIGH = 4
LANES = 128
VMEM_BYTES = 58 * 1024 * 1024
PARTS = 4
CHUNK = 16


def remote(src, dst, send, recv, device):
    copy = pltpu.make_async_remote_copy(
        src_ref=src, dst_ref=dst, send_sem=send, recv_sem=recv, device_id=device, device_id_type=MESH
    )
    copy.start()
    return copy


def await_bytes(ref, sem):
    pltpu.make_async_copy(ref, ref, sem).wait()


def gelu_and_slope(v):
    c = 0.7978845608028654
    square = v * v
    t = jnp.tanh(c * v * (1.0 + 0.044715 * square))
    half = 0.5 * (1.0 + t)
    slope = half + 0.5 * v * (1.0 - t * t) * (c * (1.0 + 3.0 * 0.044715 * square))
    return v * half, slope


def turn(lhs, rhs):
    return lax.dot_general(lhs, rhs, (((1,), (1,)), ((), ())), preferred_element_type=SINGLE)


def outer(lhs, rhs):
    return lax.dot_general(lhs, rhs, (((0,), (0,)), ((), ())), preferred_element_type=SINGLE)


def dot(lhs, rhs):
    return jnp.dot(lhs, rhs, preferred_element_type=SINGLE)


def layer_kernel(
    experts,
    images,
    tokens_hbm,
    cotangent_hbm,
    router_columns,
    w_in_hbm,
    w_out_hbm,
    mixed_hbm,
    tokens_grad_hbm,
    w_in_grad_hbm,
    w_out_grad_hbm,
    router_grad,
    raw,
    held,
    w_in,
    w_out,
    mate_in,
    mate_out,
    give_in,
    give_out,
    took_in,
    took_out,
    router_own,
    router_got,
    router,
    dispatch,
    combine,
    dispatch_low,
    combine_low,
    message,
    got,
    rows,
    part,
    act,
    slope,
    pre_grad,
    far,
    near,
    cross,
    aside,
    over,
    ready,
    back,
    combine_term,
    w_in_grad,
    w_out_grad,
    router_message,
    router_first,
    router_mine,
    router_second,
    local,
    a2a_send,
    a2a_recv,
    swap_send,
    swap_recv,
    ag_send,
    ag_recv,
    ag_far,
    rs_send,
    far_recv,
    near_recv,
    cross_recv,
    aside_recv,
    over_recv,
):
    dp, ex = lax.axis_index("dp"), lax.axis_index("expert")
    shards = 2 * RING
    x, z = lax.rem(dp, RING), dp // RING
    odd = lax.rem(x, 2)
    partner = ((1 - z) * RING + x, ex)
    right = (z * RING + lax.rem(x + 1, RING), ex)
    left = (z * RING + lax.rem(x + 3, RING), ex)
    across = (z * RING + lax.rem(x + 1 + 2 * odd, RING), ex)
    beside = (z * RING + lax.rem(x + 3 + 2 * odd, RING), ex)
    n_rows = experts * images
    half = rows.shape[-1] // 2
    slots = 2 * experts
    pairs = images * slots
    n_tokens, n_padded = tokens_hbm.shape[0] * images, held.shape[1]
    chunks = rows.shape[-1] // LANES
    inner = experts // Z_HIGH
    lane = lax.rem(ex, inner)
    z_at = (ex // inner) * 2 + z
    way = 1 - 2 * z

    loads = [
        pltpu.make_async_copy(src, dst, local.at[k])
        for k, (src, dst) in enumerate(
            (
                (tokens_hbm, raw.at[0]),
                (cotangent_hbm, raw.at[1]),
                (w_in_hbm, w_in),
                (w_out_hbm, w_out),
            )
        )
    ]
    for load in loads:
        load.start()
    owned = router_columns.shape[0]
    value = router_columns[...].astype(SINGLE)
    lines = [value[s : s + 1, c * LANES : (c + 1) * LANES] for s in range(owned) for c in range(chunks)]
    lines.append(jnp.zeros((CHUNK - owned * chunks, LANES), SINGLE))
    router_own[...] = jnp.concatenate(lines, axis=0).astype(LOW)

    barrier = pltpu.get_barrier_semaphore()

    def each_lane(step, what):
        def one(i, carry):
            what(lax.rem(lane + i, inner))
            return carry

        lax.fori_loop(0 if step else 1, inner, one, 0, unroll=True)

    def at_z(offset):
        z_to = lax.rem(z_at + offset + 4 * Z_HIGH, 2 * Z_HIGH)
        return lax.rem(z_to, 2) * RING + x, (z_to // 2) * inner

    def greet_experts(step, offset):
        dp_to, first = at_z(offset)

        def one(there):
            to = (dp_to, first + there)
            pl.semaphore_signal(barrier, inc=1, device_id=to, device_id_type=MESH)

        each_lane(step, one)

    def greet_shards(k, carry):
        to = (lax.rem(dp + k, shards), ex)
        pl.semaphore_signal(barrier, inc=1, device_id=to, device_id_type=MESH)
        return carry

    greeted = (Z_HIGH + 1) * inner
    for step, offset in enumerate((0, -way, -2 * way, -3 * way, 2 * way)):
        greet_experts(step, offset)
    lax.fori_loop(1, shards, greet_shards, 0, unroll=True)

    def hold(k):
        loads[k].wait()
        held[k, :n_tokens] = raw[k].reshape(n_tokens, held.shape[2])
        if n_padded > n_tokens:
            held[k, n_tokens:] = jnp.zeros((n_padded - n_tokens, held.shape[2]), LOW)

    hold(0)
    pl.semaphore_wait(barrier, greeted - 1 + shards - 1)

    swap_with = (partner, across)
    some = w_out.shape[1] // 2
    early, late = pl.ds(0, some), pl.ds(some, some)

    def swap(e, k, src, dst):
        sent.append(remote(src, dst, swap_send.at[e, k], swap_recv.at[e, k], swap_with[e]))

    sent = []

    def deliver(src, dst, k):
        for step in range(Z_HIGH):
            dp_to, first = at_z(step * way * (1 - 2 * (step % 2)))

            def one(there, step=step, dp_to=dp_to, first=first):
                pltpu.make_async_remote_copy(
                    src_ref=src.at[first + there],
                    dst_ref=dst.at[step * inner + lane],
                    send_sem=a2a_send.at[k],
                    recv_sem=a2a_recv.at[k],
                    device_id=(dp_to, first + there),
                    device_id_type=MESH,
                ).start()

            each_lane(step, one)
        dst[lane] = src[ex]

    def collect(src_of, dst, k):
        for step in range(Z_HIGH):
            dp_to, first = at_z(-step * way)

            def one(there, step=step, dp_to=dp_to, first=first):
                pltpu.make_async_remote_copy(
                    src_ref=src_of(step * inner + there),
                    dst_ref=dst.at[ex],
                    send_sem=a2a_send.at[k],
                    recv_sem=a2a_recv.at[k],
                    device_id=(dp_to, first + there),
                    device_id_type=MESH,
                ).start()

            each_lane(step, one)

    def received(ref, k):
        await_bytes(ref.at[pl.ds(0, experts - 1)], a2a_recv.at[k])

    def iota(shape, axis):
        return lax.broadcasted_iota(jnp.int32, shape, axis)

    def bits(n):
        return n.bit_length() - 1

    def by_expert(row):
        slot = (row >= n_rows).astype(jnp.int32)
        row = row - slot * n_rows
        image = lax.bitwise_and(row, images - 1)
        return lax.shift_right_logical(row, bits(images)) * 4 * images + slot * images + image

    def by_image(row):
        slot = lax.bitwise_and(row, slots - 1)
        image = lax.shift_right_logical(row, bits(slots))
        odd = lax.bitwise_and(slot, 1)
        return lax.shift_right_logical(slot, 1) * 4 * images + odd * images + image

    def by_slot(row):
        odd = lax.bitwise_and(row, 1)
        return lax.shift_right_logical(row, 1) * CHUNK + odd * chunks

    def distance(shape, axis, order):
        return iota(shape, axis) - order(iota(shape, 1 - axis))

    def mark(distances, at):
        return (distances == at).astype(SINGLE).astype(LOW)

    def pack(value, order):
        n = value.shape[0]
        away = distance((experts * 4 * images, n), 0, order)
        block = sum(
            dot(mark(away, h * 2 * images), value[:, h * half : (h + 1) * half]) for h in range(2)
        )
        return block.astype(LOW).reshape(experts, 4 * images, half)

    def unpack(value, order, n):
        flat = value.reshape(experts * 4 * images, half)
        away = distance((n, experts * 4 * images), 1, order)
        return [dot(mark(away, h * 2 * images), flat).astype(LOW) for h in range(2)]

    collect(lambda block: router_own, router_got, 4)
    for load in loads[2:]:
        load.wait()
    swap(1, 0, w_in.at[1], mate_in.at[1])
    swap(0, 0, w_in.at[0], mate_in.at[0])
    swap(1, 1, w_out.at[1], mate_out.at[1])
    router_got[ex] = router_own[...]
    received(router_got, 4)
    flat = router_got[...].reshape(experts * CHUNK, LANES)
    away = distance((slots, experts * CHUNK), 1, by_slot)
    for c in range(chunks):
        router[:, c * LANES : (c + 1) * LANES] = dot(mark(away, c), flat).astype(LOW)

    column = iota((slots, n_padded), 1)
    image_of = jnp.where(column < n_tokens, lax.bitwise_and(column, images - 1), -1)

    def per_image(reduce, value, fill):
        spread = jnp.zeros_like(value)
        for i in range(images):
            mine = image_of == i
            total = reduce(jnp.where(mine, value, fill), axis=1, keepdims=True)
            spread = jnp.where(mine, total, spread)
        return spread

    def apart(value, low):
        for i in range(images):
            low[i * slots : (i + 1) * slots] = jnp.where(image_of == i, value, 0.0).astype(LOW)

    def together(value):
        total = jnp.zeros((slots, n_padded), SINGLE)
        for i in range(images):
            total = jnp.where(image_of == i, value[i * slots : (i + 1) * slots], total)
        return total

    logits = turn(router[...], held[0])
    weight = jnp.exp(logits - per_image(jnp.max, logits, -jnp.inf))
    weight = jnp.where(image_of >= 0, weight, 0.0)
    weight = weight / jnp.where(image_of >= 0, per_image(jnp.sum, weight, 0.0), 1.0)
    dispatch[...] = weight
    apart(weight, dispatch_low)
    message[0] = pack(dot(dispatch_low[...], held[0]).astype(LOW), by_image)
    deliver(message.at[0], got.at[0], 0)
    swap(0, 1, w_out.at[0, early], mate_out.at[0, early])
    hold(1)
    weight = jnp.exp(logits - jnp.max(logits, axis=0, keepdims=True))
    weight = weight / jnp.sum(weight, axis=0, keepdims=True)
    combine[...] = weight
    apart(weight, combine_low)
    message[1] = pack(dot(combine_low[...], held[1]).astype(LOW), by_image)

    def own_rows(a):
        received(got.at[a], a)
        for h, block in enumerate(unpack(got[a], by_expert, 2 * n_rows)):
            for e in range(2):
                rows[a, e, 0, :, h * half : (h + 1) * half] = block[e * n_rows : (e + 1) * n_rows]

    bands = (pl.ds(0, n_rows // 2), pl.ds(n_rows // 2, n_rows // 2))
    onward = (right, left)

    def send_block(a, e, src, dst, to, slot):
        sent.append(
            remote(rows.at[a, e, src], rows.at[a, e, dst], ag_send.at[a, slot], ag_recv.at[a, e, dst], to)
        )

    def arrived(a, e, j):
        await_bytes(rows.at[a, e, j], ag_recv.at[a, e, j])

    def gather_own(a):
        send_block(a, 1, 0, 1, partner, 0)
        send_block(a, 0, 0, 3, right, 1)
        send_block(a, 0, 0, 1, left, 2)
        send_block(a, 1, 0, 2, beside, 3)

    def gather_mate(a):
        arrived(a, 1, 1)
        send_block(a, 1, 1, 3, beside, 4)

    def gather_far(a):
        for side, j in enumerate((3, 1)):
            arrived(a, 0, j)
            sent.append(
                remote(
                    rows.at[a, 0, j, bands[side]],
                    rows.at[a, 0, 2, bands[side]],
                    ag_send.at[a, 5 + side],
                    ag_far.at[a, side],
                    onward[side],
                )
            )

    def far_rest(a):
        for side in range(2):
            await_bytes(rows.at[a, 0, 2, bands[side]], ag_far.at[a, side])

    def hidden(e):
        return ((w_in.at[e], w_out.at[e]), (mate_in.at[e], mate_out.at[e]))

    def forward(e, j):
        total = 0.0
        for h, (first, second) in enumerate(hidden(e)):
            value, grade = gelu_and_slope(dot(rows[0, e, j], first[...]))
            value = value.astype(LOW)
            act[e, h, j] = value
            slope[e, h, j] = grade
            total = total + dot(value, second[...])
        part[0, e, j] = total.astype(LOW)

    def backward(e, j):
        total = 0.0
        for h, (first, second) in enumerate(hidden(e)):
            grad = turn(rows[1, e, j], second[...])
            grad = (grad * slope[e, h, j]).astype(LOW)
            pre_grad[e, h, j] = grad
            total = total + turn(grad, first[...])
        part[1, e, j] = total.astype(LOW)

    def several(step, e, start, stop):
        def one(j, carry):
            step(e, j)
            return carry

        lax.fori_loop(start, stop, one, 0)

    def send_part(src, dst, send, recv, to):
        sent.append(remote(src, dst, send, recv, to))

    def reduce_far(a):
        for side in range(2):
            send_part(
                part.at[a, 0, 2, bands[side]],
                far.at[a, side],
                rs_send.at[a, side],
                far_recv.at[a, side],
                onward[side],
            )

    def send_near(a, side, band):
        send_part(
            part.at[a, 0, (1, 3)[side], bands[band]],
            near.at[a, side, bands[band]],
            rs_send.at[a, 2 + 2 * side + band],
            near_recv.at[a, side, band],
            onward[side],
        )

    def near_free(a):
        for side in range(2):
            send_near(a, side, 1 - side)

    def near_summed(a):
        for side in range(2):
            j = (1, 3)[side]
            await_bytes(far.at[a, side], far_recv.at[a, side])
            total = part[a, 0, j, bands[side]].astype(SINGLE) + far[a, side].astype(SINGLE)
            part[a, 0, j, bands[side]] = total.astype(LOW)
            send_near(a, side, side)

    def reduce_cross(a):
        send_part(part.at[a, 1, 3], cross.at[a], rs_send.at[a, 6], cross_recv.at[a], partner)
        send_part(part.at[a, 1, 1], over.at[a], rs_send.at[a, 7], over_recv.at[a], partner)

    def reduce_beside(a):
        await_bytes(cross.at[a], cross_recv.at[a])
        total = part[a, 1, 2].astype(SINGLE) + cross[a].astype(SINGLE)
        part[a, 1, 2] = total.astype(LOW)
        send_part(part.at[a, 1, 2], aside.at[a], rs_send.at[a, 8], aside_recv.at[a], beside)

    def give_back(a):
        first = part[a, 0, 0].astype(SINGLE)
        for side in range(2):
            for band in range(2):
                await_bytes(near.at[a, side, bands[band]], near_recv.at[a, side, band])
            first = first + near[a, side].astype(SINGLE)
        await_bytes(aside.at[a], aside_recv.at[a])
        await_bytes(over.at[a], over_recv.at[a])
        second = part[a, 1, 0].astype(SINGLE) + aside[a].astype(SINGLE) + over[a].astype(SINGLE)
        total = jnp.concatenate([first.astype(LOW), second.astype(LOW)], axis=0)
        ready[a] = pack(total, by_expert)
        collect(lambda block: ready.at[a, block], back.at[a], 2 + a)
        back[a, ex] = ready[a, lane]

    def given(a):
        received(back.at[a], 2 + a)
        return jnp.concatenate(unpack(back[a], by_image, pairs), axis=1)

    stores = []

    def store(src, dst, k):
        copy = pltpu.make_async_copy(src, dst, local.at[k])
        copy.start()
        stores.append(copy)

    def flat(value):
        return value.reshape(value.shape[0] * value.shape[1], value.shape[2])

    def weights_out(e):
        give_out[e] = outer(flat(act[e, 1]), flat(rows[1, e])).astype(LOW)
        swap(e, 2, give_out.at[e], took_out.at[e])

    third = w_in.shape[1] // 3
    thirds = [pl.ds(k * third, third) for k in range(3)]

    def weights_in(e):
        give_in[e] = outer(flat(rows[0, e]), flat(pre_grad[e, 1])).astype(LOW)

    def weights_in_given(e, k):
        swap(e, 4 + k, give_in.at[e, thirds[k]], took_in.at[e, thirds[k]])

    def weights_own(e):
        w_out_grad[e] = outer(flat(act[e, 0]), flat(rows[1, e]))
        w_in_grad[e] = outer(flat(rows[0, e]), flat(pre_grad[e, 0]))

    def weights_out_taken(e):
        await_bytes(took_out.at[e], swap_recv.at[e, 2])
        w_out_grad[e] = w_out_grad[e] + took_out[e].astype(SINGLE)
        store(w_out_grad.at[e], w_out_grad_hbm.at[e], 4 + e)

    def weights_in_taken(e):
        for k in range(3):
            await_bytes(took_in.at[e, thirds[k]], swap_recv.at[e, 4 + k])
        w_in_grad[e] = w_in_grad[e] + took_in[e].astype(SINGLE)
        store(w_in_grad.at[e], w_in_grad_hbm.at[e], 6 + e)

    def weights_here(e):
        await_bytes(mate_in.at[e], swap_recv.at[e, 0])
        if e == 0:
            await_bytes(mate_out.at[e, early], swap_recv.at[e, 1])
            await_bytes(mate_out.at[e, late], swap_recv.at[e, 3])
        else:
            await_bytes(mate_out.at[e], swap_recv.at[e, 1])

    own_rows(0)
    gather_own(0)
    deliver(message.at[1], got.at[1], 1)
    swap(0, 3, w_out.at[0, late], mate_out.at[0, late])
    gather_mate(0)
    weights_here(1)
    forward(1, 0)
    gather_far(0)
    forward(1, 1)
    own_rows(1)
    gather_own(1)
    for j in (2, 3):
        arrived(0, 1, j)
    several(forward, 1, 2, 4)
    gather_mate(1)
    gather_far(1)
    reduce_cross(0)
    weights_here(0)
    far_rest(0)
    several(forward, 0, 0, 4)
    reduce_far(0)
    near_free(0)
    reduce_beside(0)
    several(backward, 1, 0, 2)
    for j in (2, 3):
        arrived(1, 1, j)
    several(backward, 1, 2, 4)
    reduce_cross(1)
    near_summed(0)
    far_rest(1)
    several(backward, 0, 0, 4)
    reduce_far(1)
    near_free(1)
    weights_out(0)
    near_summed(1)
    give_back(0)
    reduce_beside(1)
    weights_out(1)
    give_back(1)
    weights_in(0)
    weights_in_given(0, 0)
    weights_in(1)
    for k in range(3):
        weights_in_given(1, k)
    weights_own(0)
    weights_own(1)
    weights_out_taken(0)

    slot_out = given(0)
    value = outer(combine_low[...], slot_out)[:n_tokens].astype(LOW)
    raw[0] = value.reshape(raw.shape[1:])
    store(raw.at[0], mixed_hbm, 8)
    grad = together(turn(slot_out, held[1]))
    weight = combine[...]
    combine_term[...] = weight * (grad - jnp.sum(weight * grad, axis=0, keepdims=True))

    input_slots = given(1)
    grad = together(turn(input_slots, held[0]))
    weight = dispatch[...]
    grad = weight * (grad - per_image(jnp.sum, weight * grad, 0.0)) + combine_term[...]
    grad = jnp.where(image_of >= 0, grad, 0.0).astype(LOW)
    total = dot(grad, held[0]).astype(LOW)
    away = distance((experts * CHUNK, slots), 0, by_slot)
    block = sum(
        dot(mark(away, c), total[:, c * LANES : (c + 1) * LANES]) for c in range(chunks)
    )
    router_message[...] = block.astype(LOW).reshape(experts, CHUNK, LANES)
    deliver(router_message, router_first, 5)
    for k in (1, 2):
        weights_in_given(0, k)
    value = outer(dispatch_low[...], input_slots) + outer(grad, router[...])
    raw[1] = value[:n_tokens].astype(LOW).reshape(raw.shape[1:])
    store(raw.at[1], tokens_grad_hbm, 9)

    received(router_first, 5)
    router_mine[...] = jnp.sum(router_first[...].astype(SINGLE), axis=0)

    def share(k, carry):
        pltpu.make_async_remote_copy(
            src_ref=router_mine,
            dst_ref=router_second.at[dp],
            send_sem=a2a_send.at[6],
            recv_sem=a2a_recv.at[6],
            device_id=(lax.rem(dp + k, shards), ex),
            device_id_type=MESH,
        ).start()
        return carry

    lax.fori_loop(1, shards, share, 0, unroll=True)
    router_second[dp] = router_mine[...]
    weights_out_taken(1)
    weights_in_taken(1)
    await_bytes(router_second.at[pl.ds(0, shards - 1)], a2a_recv.at[6])
    value = jnp.sum(router_second[...], axis=0)
    for s in range(owned):
        for c in range(chunks):
            at = s * chunks + c
            router_grad[s : s + 1, c * LANES : (c + 1) * LANES] = value[at : at + 1]

    weights_in_taken(0)
    for k in range(4):
        await_bytes(got.at[0, pl.ds(0, experts - 1)], a2a_send.at[k])
    for k in range(4, 6):
        await_bytes(router_got.at[pl.ds(0, experts - 1)], a2a_send.at[k])
    await_bytes(router_second.at[pl.ds(0, shards - 1)], a2a_send.at[6])
    for copy in sent:
        copy.wait_send()
    for copy in stores:
        copy.wait()


def finish_kernel(*refs):
    count = (len(refs) - 2) // 3
    sources, results, staged = (refs[k * count : (k + 1) * count] for k in range(3))
    into, out = refs[-2:]
    pieces = []
    for src, dst, held in zip(sources, results, staged):
        parts = 1 if len(src.shape) < 3 else PARTS if src.shape[0] % PARTS == 0 else src.shape[0]
        size = src.shape[0] // parts
        for at in range(parts):
            rows, k = pl.ds(at * size, size), len(pieces)
            pieces.append(
                (
                    pltpu.make_async_copy(src.at[rows], held.at[rows], into.at[k]),
                    pltpu.make_async_copy(held.at[rows], dst.at[rows], out.at[k]),
                )
            )
    for read, _ in pieces:
        read.start()
    for read, write in pieces:
        read.wait()
        write.start()
    for _, write in pieces:
        write.wait()


def finish(*values):
    anywhere = pl.BlockSpec(memory_space=pl.ANY)
    return pl.pallas_call(
        finish_kernel,
        out_shape=[jax.ShapeDtypeStruct(value.shape, value.dtype) for value in values],
        in_specs=[anywhere] * len(values),
        out_specs=[anywhere] * len(values),
        scratch_shapes=[pltpu.VMEM(value.shape, value.dtype) for value in values]
        + [pltpu.SemaphoreType.DMA((PARTS * len(values),))] * 2,
        compiler_params=pltpu.CompilerParams(vmem_limit_bytes=VMEM_BYTES),
        name="finish",
    )(*values)


def body(experts, tokens, router, w_in, w_out, cotangent):
    images, n, d = tokens.shape
    hidden = w_in.shape[2]
    owned = router.shape[1]
    slots = experts * owned
    n_tokens = images * n
    n_padded = -(-n_tokens // LANES) * LANES
    n_rows = experts * images
    half = d // 2

    def swap(value):
        return value.transpose(1, 0, 2)

    def low(*shape):
        return pltpu.VMEM(shape, LOW)

    def single(*shape):
        return pltpu.VMEM(shape, SINGLE)

    anywhere = pl.BlockSpec(memory_space=pl.ANY)
    in_hbm = pl.BlockSpec(memory_space=pltpu.HBM)
    vmem = pl.BlockSpec(memory_space=pltpu.VMEM)
    dma = pltpu.SemaphoreType.DMA
    mixed, tokens_grad, w_in_grad, w_out_grad, router_grad = pl.pallas_call(
        functools.partial(layer_kernel, experts, images),
        out_shape=[
            jax.ShapeDtypeStruct((n, images, d), LOW),
            jax.ShapeDtypeStruct((n, images, d), LOW),
            jax.ShapeDtypeStruct(w_in.shape, SINGLE),
            jax.ShapeDtypeStruct(w_out.shape, SINGLE),
            jax.ShapeDtypeStruct((owned, d), SINGLE),
        ],
        in_specs=[in_hbm, in_hbm, vmem, in_hbm, in_hbm],
        out_specs=[anywhere] * 4 + [vmem],
        scratch_shapes=[
            low(2, n, images, d),
            low(2, n_padded, d),
            low(*w_in.shape),
            low(*w_out.shape),
            low(*w_in.shape),
            low(*w_out.shape),
            low(*w_in.shape),
            low(*w_out.shape),
            low(*w_in.shape),
            low(*w_out.shape),
            low(CHUNK, LANES),
            low(experts, CHUNK, LANES),
            low(slots, d),
            single(slots, n_padded),
            single(slots, n_padded),
            low(images * slots, n_padded),
            low(images * slots, n_padded),
            low(2, experts, 4 * images, half),
            low(2, experts, 4 * images, half),
            low(2, 2, RING, n_rows, d),
            low(2, 2, RING, n_rows, d),
            low(2, 2, RING, n_rows, hidden),
            single(2, 2, RING, n_rows, hidden),
            low(2, 2, RING, n_rows, hidden),
            low(2, 2, n_rows // 2, d),
            low(2, 2, n_rows, d),
            low(2, n_rows, d),
            low(2, n_rows, d),
            low(2, n_rows, d),
            low(2, experts, 4 * images, half),
            low(2, experts, 4 * images, half),
            single(slots, n_padded),
            single(*w_in.shape),
            single(*w_out.shape),
            low(experts, CHUNK, LANES),
            low(experts, CHUNK, LANES),
            single(CHUNK, LANES),
            single(2 * RING, CHUNK, LANES),
            dma((10,)),
            dma((7,)),
            dma((7,)),
            dma((2, 7)),
            dma((2, 7)),
            dma((2, 7)),
            dma((2, 2, RING)),
            dma((2, 2)),
            dma((2, 9)),
            dma((2, 2)),
            dma((2, 2, 2)),
            dma((2,)),
            dma((2,)),
            dma((2,)),
        ],
        compiler_params=pltpu.CompilerParams(
            collective_id=0, has_side_effects=True, vmem_limit_bytes=VMEM_BYTES
        ),
        name="layer",
    )(swap(tokens), swap(cotangent), router.T, w_in, w_out)
    mixed, tokens_grad, w_in_grad, w_out_grad, router_grad = finish(
        mixed, tokens_grad, w_in_grad, w_out_grad, router_grad
    )
    return (swap(mixed), swap(tokens_grad), w_in_grad, w_out_grad, router_grad.T)


def solution(mesh):
    placed = (
        P(("dp", "expert"), None, None),
        P(None, "expert"),
        P("expert", None, "dp"),
        P("expert", "dp", None),
        P(("dp", "expert"), None, None),
    )
    return jax.shard_map(
        functools.partial(body, mesh.shape["expert"]),
        mesh=mesh,
        in_specs=placed,
        out_specs=(
            P(("dp", "expert"), None, None),
            P(("dp", "expert"), None, None),
            P("expert", None, "dp"),
            P("expert", "dp", None),
            P(None, "expert"),
        ),
        check_vma=False,
    )
```
